128 devices in a mesh: section: 2 (over core), head: 4 (over y), seq: 16 (over x, z).
Axes of the slice: x: 4, y: 4, z: 4, core: 2. Of those that a mesh axis runs over, the one named last changes fastest.
Arguments:
- x_in: bfloat16 [2, 4096, 1536], P(None, 'seq'), may hold values from -6 to 6
- norm_gain: float32 [2, 1536], P('section'), may hold values from 0.5 to 1.5
- w_zx: bfloat16 [2, 1536, 2, 3072], P('section', None, None, 'head'), may hold values from -0.15625 to 0.15625
- w_bc: bfloat16 [2, 1536, 256], P('section'), may hold values from -0.15625 to 0.15625
- w_dt: bfloat16 [2, 1536, 48], P('section', None, 'head'), may hold values from -0.15625 to 0.15625
- dt_bias: float32 [2, 48], P('section', 'head'), may hold values from -8 to -3
- a_log: float32 [2, 48], P('section', 'head'), may hold values from 0 to 1.5
- d_skip: float32 [2, 48], P('section', 'head'), may hold values from 0.5 to 1.5
- conv_x: bfloat16 [2, 4, 3072], P('section', None, 'head'), may hold values from -3 to 3
- conv_bc: bfloat16 [2, 4, 256], P('section'), may hold values from -3 to 3
- gate_gain: float32 [2, 3072], P('section', 'head'), may hold values from 0.5 to 1.5
- w_out: bfloat16 [2, 3072, 1536], P('section', 'head'), may hold values from -0.109375 to 0.109375
- cotangent: bfloat16 [2, 4096, 1536], P(None, 'seq'), may hold values from -6 to 6
Outputs:
- section_out: bfloat16 [2, 2, 4096, 1536], P('section', None, 'seq')
- grads_in: bfloat16 [2, 2, 4096, 1536], P('section', None, 'seq')
- g_norm_gain: float32 [2, 1536], P('section')
- g_w_zx: float32 [2, 1536, 2, 3072], P('section', None, None, 'head')
- g_w_bc: float32 [2, 1536, 256], P('section')
- g_w_dt: float32 [2, 1536, 48], P('section', None, 'head')
- g_dt_bias: float32 [2, 48], P('section', 'head')
- g_a_log: float32 [2, 48], P('section', 'head')
- g_d_skip: float32 [2, 48], P('section', 'head')
- g_conv_x: float32 [2, 4, 3072], P('section', None, 'head')
- g_conv_bc: float32 [2, 4, 256], P('section')
- g_gate_gain: float32 [2, 3072], P('section', 'head')
- g_w_out: float32 [2, 3072, 1536], P('section', 'head')
The draws below stay inside these ranges and needn't reach their ends.
All inputs are finite; a program needn't handle non-finite values.
Results may differ from the reference program's by a relative error of at most 0.025.
Values may be sent and summed in bfloat16 or wider, within the bound.
A program may use at most 192 MiB of HBM per device.

```python
import jax
import jax.numpy as jnp
from jax import lax

D = 1536
HEADS = 48
HEAD_DIM = 64
STATE = 128
KERNEL = 4
INNER = 3072
MICRO = 2
SEQ_LEN = 4096
BLOCK = 256
SECTIONS = 2


def steps_of(stream_key, shape, shards, low, largest):
    gain = 1.0
    for axis_at, blocks in shards:
        draws = jax.random.uniform(jax.random.fold_in(jax.random.fold_in(stream_key, 6), axis_at), (blocks,), jnp.float32, low / len(shards), largest / len(shards))
        gain = gain * jnp.repeat(jnp.exp(draws), shape[axis_at] // blocks).reshape((-1,) + (1,) * (len(shape) - 1 - axis_at))
    return gain


def noise(own_key, dims, scale, reach, split=(), kind=jnp.bfloat16):
    drawn = scale * jax.random.normal(own_key, dims, jnp.float32)
    if split:
        drawn = drawn * steps_of(own_key, dims, split, -0.22, 0.18)
    return jnp.clip(drawn, -reach, reach).astype(kind)


def setup_inputs(seed: int = 0) -> dict:
    arg_keys = jax.random.split(jax.random.key(seed), 14)
    return {
        "x_in": noise(arg_keys[0], (MICRO, SEQ_LEN, D), 1.0, 6.0, ((1, 16),)),
        "norm_gain": jnp.clip(1.0 + 0.1 * jax.random.normal(arg_keys[1], (SECTIONS, D), jnp.float32), 0.5, 1.5),
        "w_zx": noise(arg_keys[2], (SECTIONS, D, 2, INNER), D ** -0.5, 0.15625, ((0, 2), (3, 4))),
        "w_bc": noise(arg_keys[3], (SECTIONS, D, 2 * STATE), D ** -0.5, 0.15625, ((0, 2),)),
        "w_dt": noise(arg_keys[4], (SECTIONS, D, HEADS), D ** -0.5, 0.15625, ((0, 2), (2, 4))),
        "dt_bias": jnp.clip(-8.0 + 5.0 * jax.random.uniform(arg_keys[5], (SECTIONS, HEADS), jnp.float32) ** steps_of(arg_keys[5], (SECTIONS, HEADS), ((0, 2), (1, 4)), -0.2, 0.2), -8.0, -3.0),
        "a_log": jnp.clip(1.5 * jax.random.uniform(arg_keys[6], (SECTIONS, HEADS), jnp.float32) ** steps_of(arg_keys[6], (SECTIONS, HEADS), ((0, 2), (1, 4)), -0.2, 0.2), 0.0, 1.5),
        "d_skip": jnp.clip(0.5 + 1.0 * jax.random.uniform(arg_keys[7], (SECTIONS, HEADS), jnp.float32) ** steps_of(arg_keys[7], (SECTIONS, HEADS), ((0, 2), (1, 4)), -0.2, 0.2), 0.5, 1.5),
        "conv_x": noise(arg_keys[8], (SECTIONS, KERNEL, INNER), KERNEL ** -0.5, 3.0, ((0, 2), (2, 4))),
        "conv_bc": noise(arg_keys[9], (SECTIONS, KERNEL, 2 * STATE), KERNEL ** -0.5, 3.0, ((0, 2),)),
        "gate_gain": jnp.clip(1.0 + 0.1 * jax.random.normal(arg_keys[10], (SECTIONS, INNER), jnp.float32), 0.5, 1.5),
        "w_out": noise(arg_keys[11], (SECTIONS, INNER, D), INNER ** -0.5, 0.109375, ((0, 2), (1, 4))),
        "cotangent": noise(arg_keys[12], (MICRO, SEQ_LEN, D), 1.0, 6.0, ((1, 16),)),
    }


EPS = 1e-05
HIGH = lax.Precision.HIGHEST

@jax.custom_vjp
def low(v):
    return lax.optimization_barrier(v.astype(jnp.bfloat16)).astype(jnp.float32)

@jax.custom_vjp
def low_back(v):
    return v

def low_keep(v):
    return (low(v), None)

def low_pass(kept, grad):
    return (grad,)

def back_keep(v):
    return (v, None)

def back_low(kept, grad):
    return (low(grad),)
low.defvjp(low_keep, low_pass)
low_back.defvjp(back_keep, back_low)

def silu(values):
    return values * jax.nn.sigmoid(values)

def ssd_block(x_heads, b_rows, c_rows, step_sizes, a_rates, state_in):
    length = x_heads.shape[0]
    log_decay = jnp.cumsum(step_sizes * a_rates[None, :], axis=0)
    places = jnp.arange(length)
    causal = places[:, None] >= places[None, :]
    spans = jnp.where(causal[:, :, None], log_decay[:, None, :] - log_decay[None, :, :], -1e+30)
    scores = jnp.dot(c_rows, b_rows.T, precision=HIGH)
    mixing = scores[:, :, None] * jnp.exp(spans) * step_sizes[None, :, :]
    y_inner = jnp.einsum('tsh,shp->thp', mixing, x_heads, precision=HIGH)
    y_carry = jnp.exp(log_decay)[:, :, None] * jnp.einsum('tn,hpn->thp', c_rows, state_in, precision=HIGH)
    weights_tail = jnp.exp(log_decay[-1:, :] - log_decay) * step_sizes
    state_out = jnp.exp(log_decay[-1])[:, None, None] * state_in + jnp.einsum('sh,sn,shp->hpn', weights_tail, b_rows, x_heads, precision=HIGH)
    return (y_inner + y_carry, state_out)

def causal_conv(pre_rows, taps):
    length = pre_rows.shape[0]
    padded = jnp.concatenate([jnp.zeros((KERNEL - 1, pre_rows.shape[1]), jnp.float32), pre_rows], axis=0)
    total = taps[0] * padded[0:length]
    for offset in range(1, KERNEL):
        total = total + taps[offset] * padded[offset:offset + length]
    return silu(total)

def mamba_layer(x_rows, section_set):
    norm_gain, w_zx, w_bc, w_dt, dt_bias, a_log, d_skip, conv_x, conv_bc, gate_gain, w_out = section_set
    length = x_rows.shape[0]
    norm_scale = lax.rsqrt(lax.optimization_barrier(jnp.mean(x_rows * x_rows, axis=-1, keepdims=True)) + EPS)
    normed = low(x_rows * norm_scale * norm_gain)
    zx_rows = low_back(jnp.einsum('td,dki->tki', normed, w_zx, precision=HIGH))
    z_part = zx_rows[:, 0, :]
    x_pre = zx_rows[:, 1, :]
    bc_pre = jnp.dot(normed, w_bc, precision=HIGH)
    dt_pre = jnp.dot(normed, w_dt, precision=HIGH)
    x_act = causal_conv(x_pre, conv_x)
    bc_act = causal_conv(bc_pre, conv_bc)
    step_sizes = jax.nn.softplus(dt_pre + dt_bias)
    a_rates = -jnp.exp(a_log)
    x_heads = x_act.reshape(length, HEADS, HEAD_DIM)
    b_rows = bc_act[:, :STATE]
    c_rows = bc_act[:, STATE:]
    blocks = length // BLOCK

    def block_step(state_now, pieces):
        x_piece, b_piece, c_piece, dt_piece = pieces
        y_piece, state_next = jax.checkpoint(ssd_block)(x_piece, b_piece, c_piece, dt_piece, a_rates, state_now)
        return (state_next, y_piece)
    start_state = jnp.zeros((HEADS, HEAD_DIM, STATE), jnp.float32)
    pieces = (x_heads.reshape(blocks, BLOCK, HEADS, HEAD_DIM), b_rows.reshape(blocks, BLOCK, STATE), c_rows.reshape(blocks, BLOCK, STATE), step_sizes.reshape(blocks, BLOCK, HEADS))
    unused_state, y_blocks = lax.scan(block_step, start_state, pieces)
    y_heads = y_blocks.reshape(length, HEADS, HEAD_DIM) + d_skip[None, :, None] * x_heads
    gated = y_heads.reshape(length, INNER) * silu(z_part)
    gate_scale = lax.rsqrt(lax.optimization_barrier(jnp.mean(gated * gated, axis=-1, keepdims=True)) + EPS)
    mixed_in = low(gated * gate_scale * gate_gain)
    return x_rows + jnp.dot(mixed_in, w_out, precision=HIGH)

def reference(x_in, norm_gain, w_zx, w_bc, w_dt, dt_bias, a_log, d_skip, conv_x, conv_bc, gate_gain, w_out, cotangent):
    weights = tuple((tensor.astype(jnp.float32) for tensor in (norm_gain, w_zx, w_bc, w_dt, dt_bias, a_log, d_skip, conv_x, conv_bc, gate_gain, w_out)))
    inputs = x_in.astype(jnp.float32)
    probe_zero = jnp.zeros_like(inputs)

    def forward(inputs, probe_zero, weights):
        first_set = tuple((tensor[0] for tensor in weights))
        second_set = tuple((tensor[1] for tensor in weights))
        middle = lax.map(lambda seq_rows: low(mamba_layer(seq_rows, first_set)), inputs)
        middle = low_back(middle + probe_zero)
        final_out = lax.map(lambda seq_rows: mamba_layer(seq_rows, second_set), middle)
        return (middle, final_out)
    (middle, final_out), pull_back = jax.vjp(forward, inputs, probe_zero, weights)
    grad_first, grad_mid, grad_sets = pull_back((jnp.zeros_like(middle), cotangent.astype(jnp.float32)))
    section_out = jnp.stack([middle, final_out]).astype(jnp.bfloat16)
    grads_in = jnp.stack([grad_first, grad_mid]).astype(jnp.bfloat16)
    return (section_out, grads_in, grad_sets[0], grad_sets[1], grad_sets[2], grad_sets[3], grad_sets[4], grad_sets[5], grad_sets[6], grad_sets[7], grad_sets[8], grad_sets[9], grad_sets[10])
```

```python
import functools

import jax
import jax.numpy as jnp
from jax import lax
from jax.experimental import pallas as pl
from jax.experimental.pallas import tpu as pltpu
from jax.sharding import PartitionSpec as P

MESH = pl.DeviceIdType.MESH
F32 = jnp.float32
BF = jnp.bfloat16
EPS = 1e-05
INNER = 3072
ROWS = 256
WIDTH = 1536
INNER_DEV = 768
HEADS_DEV = 12
HEAD_DIM = 64
STATE = 128
RIM = 16
VMEM_CAP = 60 << 20
FIRST = (((0,), (0,)), ((), ()))
LAST = (((1,), (1,)), ((), ()))


def dot(a, b):
    return jnp.dot(a, b, preferred_element_type=F32)


def dot_first(a, b):
    return lax.dot_general(a, b, FIRST, preferred_element_type=F32)


def dot_last(a, b):
    return lax.dot_general(a, b, LAST, preferred_element_type=F32)


def two_part(a):
    high = a.astype(BF)
    return high, (a - high.astype(F32)).astype(BF)


def silu(a):
    return a * jax.nn.sigmoid(a)


def silu_slope(a):
    sigma = jax.nn.sigmoid(a)
    return sigma * (1.0 + a * (1.0 - sigma))


def spread(a):
    rows = a.shape[0]
    low_half = lax.broadcasted_iota(jnp.int32, (rows, 128), 1) < HEAD_DIM
    return jnp.concatenate(
        [
            jnp.where(low_half, a[:, 2 * j : 2 * j + 1], a[:, 2 * j + 1 : 2 * j + 2])
            for j in range(HEADS_DEV // 2)
        ],
        axis=1,
    )


def triangle(keep_after):
    t = lax.broadcasted_iota(jnp.int32, (ROWS, ROWS), 0)
    s = lax.broadcasted_iota(jnp.int32, (ROWS, ROWS), 1)
    return jnp.where((s >= t) if keep_after else (t >= s), 1.0, 0.0).astype(BF)


def running(a, keep_after):
    weights = triangle(keep_after)
    high, low = two_part(a)
    return dot(weights, high) + dot(weights, low)


S_NORM, S_GATE, S_CONV, S_BIAS, S_RATE, S_SKIP = 0, 1, 2, 6, 7, 9
STEP = 32
BLOCKS = ROWS // STEP


def softplus(a):
    return jnp.maximum(a, 0.0) + jnp.log1p(jnp.exp(-jnp.abs(a)))


def rows_at(i, more=0):
    return pl.ds(pl.multiple_of(i * STEP, STEP), STEP + more)


def tile_at(i, width=256, base=0):
    return pl.ds(pl.multiple_of(base + i * width, width), width)


def conv_rows(pre, taps):
    total = taps[0:1] * pre[RIM - 3 : RIM - 3 + STEP]
    for k in range(1, 4):
        total = total + taps[k : k + 1] * pre[RIM - 3 + k : RIM - 3 + k + STEP]
    return total


def shifted(place, distance, count):
    return lax.rem(place + distance + count, count)


def meet(targets):
    barrier = pltpu.get_barrier_semaphore()
    for target in targets:
        pl.semaphore_signal(barrier, inc=1, device_id=target, device_id_type=MESH)
    pl.semaphore_wait(barrier, len(targets))


def send(src, dst, send_sem, recv_sem, target):
    copy = pltpu.make_async_remote_copy(
        src_ref=src,
        dst_ref=dst,
        send_sem=send_sem,
        recv_sem=recv_sem,
        device_id=target,
        device_id_type=MESH,
    )
    copy.start()
    return copy


def comm_params(number):
    return pltpu.CompilerParams(
        collective_id=number, has_side_effects=True, vmem_limit_bytes=VMEM_CAP
    )


ANY = pl.BlockSpec(memory_space=pl.ANY)
VM = pl.BlockSpec(memory_space=pltpu.VMEM)


def quarter(place):
    return pl.ds(pl.multiple_of(place * 384, 384), 384)


KEPT = (
    ("normed", (ROWS + RIM, WIDTH), BF),
    ("z", (ROWS, INNER_DEV), F32),
    ("x_pre", (ROWS + RIM, INNER_DEV), F32),
    ("bc_pre", (ROWS + RIM, 256), F32),
    ("dt_pre", (ROWS, 128), F32),
    ("la", (ROWS, 128), F32),
    ("la_t", (128, ROWS), F32),
    ("xd", (ROWS, INNER_DEV), BF),
    ("bc_act", (ROWS, 256), BF),
    ("x_act", (ROWS, INNER_DEV), F32),
    ("y", (ROWS, INNER_DEV), F32),
    ("decay", (8, INNER_DEV), F32),
    ("state", (STATE, INNER_DEV), BF),
    ("scale", (ROWS, 128), F32),
    ("out", (ROWS, WIDTH), BF),
    ("following", (ROWS, WIDTH), BF),
)


def chain_load(own, decay, out_buf):
    for j in range(16):
        rows = own[8 * j : 8 * j + 8]
        out_buf[j, :, 0:384] = jnp.concatenate([rows[:, :384], rows[:, 384:]], axis=0).astype(BF)
    six = jnp.concatenate([decay[0:1, 128 * k : 128 * k + 128] for k in range(6)] * 3, axis=0)
    six = six[0:16].astype(BF)
    for j in range(16):
        out_buf[j, :, 384:512] = six


def chain_scan(forward, in_buf, back_buf):
    state = jnp.zeros((16, 384), F32)
    for step in range(16):
        i = step if forward else 15 - step
        back_buf[i] = state.astype(BF)
        part = in_buf[i].astype(F32)
        decay = jnp.concatenate(
            [
                jnp.concatenate(
                    [
                        jnp.broadcast_to(part[3 * half + k : 3 * half + k + 1, 384:512], (8, 128))
                        for k in range(3)
                    ],
                    axis=1,
                )
                for half in range(2)
            ],
            axis=0,
        )
        state = decay * state + part[:, 0:384]


def chain_unload(got_buf, state_ref):
    for j in range(8):
        first, second = got_buf[2 * j].astype(F32), got_buf[2 * j + 1].astype(F32)
        for half in range(2):
            rows = jnp.concatenate(
                [first[8 * half : 8 * half + 8], second[8 * half : 8 * half + 8]], axis=0
            )
            state_ref[16 * j : 16 * j + 16, 384 * half : 384 * half + 384] = rows.astype(BF)


def spread_send(src, dst, me, send_sem, recv_sem):
    copies = []
    for d in range(1, 16):
        to = shifted(me, d, 16)
        copies.append(send(src.at[to], dst.at[me], send_sem.at[d], recv_sem.at[d], {"seq": to}))
    dst[me] = src[me]
    return copies


def finish(copies):
    for copy in copies:
        copy.wait()


def norm_rows(v, gain):
    v = v.astype(F32)
    scale = lax.rsqrt(jnp.mean(v * v, axis=-1, keepdims=True) + EPS)
    return (v * scale * gain).astype(BF)


def forward_kernel(*refs):
    x_ref, zx_m, bd_m, out_m, small_m = refs[:5]
    kept = [{name: refs[5 + 16 * s + i] for i, (name, _, _) in enumerate(KEPT)} for s in range(2)]
    zx_t, bd_t, out_t, small_w = refs[37:41]
    v_buf, rim_buf, zx_w, bd_w, out_w = refs[41:46]
    bd_out, tail_x, scores, dt_buf, tail, low, sq, part = refs[46:54]
    chain_out, chain_in, chain_back, chain_got = refs[54:58]
    sum_in, square_out, square_in, sum_own, next_own = refs[58:63]
    w_send, w_recv, w_own, rim_send, rim_recv = refs[63:68]
    c_sems, s_sems, t_sem, v_sem = refs[68:72], refs[72:76], refs[76], refs[77]

    core, me, place = lax.axis_index("section"), lax.axis_index("seq"), lax.axis_index("head")
    other = {"section": 1 - core}
    later = shifted(me, 1, 16)
    barrier = pltpu.get_barrier_semaphore()
    targets = [other]
    targets += [{"seq": shifted(me, d, 16)} for d in range(1, 16)]
    heads = [{"head": shifted(place, d, 4)} for d in range(1, 4)]
    targets += heads
    targets += [{"head": shifted(place, d, 4), "seq": shifted(me, -1, 16)} for d in range(1, 4)]
    for target in targets:
        pl.semaphore_signal(barrier, inc=1, device_id=target, device_id_type=MESH)

    moves = [
        (bd_m, bd_w.at[core]),
        (zx_m.at[:, INNER_DEV:], zx_w.at[core, :, INNER_DEV:]),
        (zx_m.at[:, :INNER_DEV], zx_w.at[core, :, :INNER_DEV]),
        (out_m, out_w.at[core]),
    ]
    own_moves = [pltpu.make_async_copy(src, dst, w_own.at[i]) for i, (src, dst) in enumerate(moves)]
    for move in own_moves:
        move.start()
    load_v = pltpu.make_async_copy(x_ref.at[core], v_buf, v_sem)
    load_v.start()
    pl.semaphore_wait(barrier, len(targets))
    rim_copy = send(x_ref.at[core, ROWS - RIM :], rim_buf.at[0], rim_send.at[0], rim_recv.at[0], {"seq": later})
    across = [send(small_m, small_w.at[core], w_send.at[4], w_recv.at[4], other)]
    for i, (src, dst) in enumerate(moves):
        across.append(send(src, dst, w_send.at[i], w_recv.at[i], other))
    small_w[core] = small_m[...]

    def arrive(section, i):
        @pl.when(core == section)
        def _():
            own_moves[i].wait()

        @pl.when(core != section)
        def _():
            across[i + 1].wait_recv()

    load_v.wait()
    rim_copy.wait()

    @pl.when(me == 0)
    def _():
        rim_buf[0] = jnp.zeros((RIM, WIDTH), BF)

    across[0].wait_recv()
    entering = v_buf
    for s in range(2):
        k = kept[s]
        small = small_w.at[s]
        normed, z_ref, x_pre, bc_pre, la_ref, la_t_ref = (
            k["normed"], k["z"], k["x_pre"], k["bc_pre"], k["la"], k["la_t"]
        )
        xd_ref, bc_act, x_act, y_ref = k["xd"], k["bc_act"], k["x_act"], k["y"]
        gain = small[S_NORM : S_NORM + 1]
        if s:
            finish(rim_in)

            @pl.when(me == 0)
            def _():
                rim_buf[1] = jnp.zeros((RIM, WIDTH), BF)

        normed[0:RIM] = norm_rows(rim_buf[s], gain)

        @pl.loop(0, ROWS // 16)
        def _(i):
            at = pl.ds(pl.multiple_of(i * 16, 16), 16)
            normed[pl.ds(pl.multiple_of(i * 16 + RIM, 16), 16)] = norm_rows(entering[at], gain)

        arrive(s, 0)
        bd_out[...] = dot(normed[...], bd_w[s])
        bc_pre[...] = bd_out[:, : 2 * STATE]
        dt_raw = bd_out[RIM:, 2 * STATE :]
        k["dt_pre"][...] = dt_raw
        arrive(s, 1)

        @pl.loop(0, 3)
        def _(j):
            x_pre[:, tile_at(j)] = dot(normed[...], zx_w[s, :, tile_at(j, 256, INNER_DEV)])

        dt = softplus(dt_raw + small[S_BIAS : S_BIAS + 1, :128])
        dt_buf[...] = dt
        la = running(dt * small[S_RATE : S_RATE + 1, :128], False)
        la_ref[...] = la
        la_t_ref[...] = la.T
        tail[...] = jnp.exp(la[ROWS - 1 : ROWS] - la)
        decay = jnp.broadcast_to(spread(jnp.exp(la[ROWS - 8 : ROWS]))[7:8], (8, INNER_DEV))
        k["decay"][...] = decay

        @pl.loop(0, BLOCKS)
        def _(i):
            taps = small[S_CONV : S_CONV + 4]
            act = silu(conv_rows(x_pre[rows_at(i, RIM)], taps[:, :INNER_DEV]))
            x_act[rows_at(i)] = act
            xd = (act * spread(dt_buf[rows_at(i)])).astype(BF)
            xd_ref[rows_at(i)] = xd
            tail_x[rows_at(i)] = (xd.astype(F32) * spread(tail[rows_at(i)])).astype(BF)
            bc = conv_rows(bc_pre[rows_at(i, RIM)], taps[:, INNER_DEV : INNER_DEV + 256])
            bc_act[rows_at(i)] = silu(bc).astype(BF)

        b_rows, c_rows = bc_act[:, :STATE], bc_act[:, STATE:]
        chain_load(dot_first(b_rows, tail_x[...]), decay, chain_out.at[s])
        copies = spread_send(chain_out.at[s], chain_in.at[s], me, c_sems[0].at[s], c_sems[1].at[s])
        arrive(s, 2)

        @pl.loop(0, 3)
        def _(j):
            z_ref[:, tile_at(j)] = dot(normed[RIM:], zx_w[s, :, tile_at(j)])

        scores[...] = dot_last(c_rows, b_rows)

        def heads_of(half):
            span = (half + 1) * 128
            rows = slice(half * 128, span)
            t = lax.broadcasted_iota(jnp.int32, (128, span), 0) + half * 128
            causal = t >= lax.broadcasted_iota(jnp.int32, (128, span), 1)
            for pair in range(HEADS_DEV // 2):
                parts = []
                for h in (2 * pair, 2 * pair + 1):
                    gap = la_ref[rows, h : h + 1] - la_t_ref[h : h + 1, :span]
                    mixing = scores[rows, :span] * jnp.exp(jnp.where(causal, gap, -1e30))
                    cols = slice(h * HEAD_DIM, (h + 1) * HEAD_DIM)
                    parts.append(dot(mixing.astype(BF), xd_ref[:span, cols]))
                y_ref[rows, pair * 128 : pair * 128 + 128] = jnp.concatenate(parts, axis=1)

        heads_of(0)
        finish(copies)
        chain_scan(True, chain_in.at[s], chain_back.at[s])
        copies = spread_send(chain_back.at[s], chain_got.at[s], me, c_sems[2].at[s], c_sems[3].at[s])
        heads_of(1)
        finish(copies)
        chain_unload(chain_got.at[s], k["state"])

        @pl.loop(0, BLOCKS)
        def _(i):
            at = rows_at(i)
            y = y_ref[at] + spread(jnp.exp(la_ref[at])) * dot(bc_act[at, STATE:], k["state"][...])
            y_ref[at] = y
            ssd = y + small[S_SKIP : S_SKIP + 1, :INNER_DEV] * x_act[at]
            gated = ssd * silu(z_ref[at])
            sq[at] = jnp.broadcast_to(jnp.sum(gated * gated, axis=-1, keepdims=True), (STEP, 128))
            low[at] = (gated * small[S_GATE : S_GATE + 1, :INNER_DEV]).astype(BF)

        square_out[s] = sq[...].T[0:8]
        arrive(s, 3)
        if s:
            for move in store_theirs(core, (bd_w, zx_w, out_w), (bd_t, zx_t, out_t), t_sem):
                move.start()

        @pl.loop(0, 6)
        def _(j):
            part[s, :, tile_at(j)] = dot(low[...], out_w[s, :, tile_at(j)]).astype(BF)

        copies = []
        for d in range(1, 4):
            src = part.at[s, :, quarter(shifted(place, d, 4))]
            copies.append(send(src, sum_in.at[s, d], s_sems[0].at[s, d], s_sems[1].at[s, d], heads[d - 1]))
        for d in range(1, 4):
            copies.append(
                send(square_out.at[s], square_in.at[s, d], s_sems[0].at[s, d + 4], s_sems[1].at[s, d + 4], heads[d - 1])
            )
        finish(copies)
        square = square_out[s]
        for d in range(1, 4):
            square = square + square_in[s, d]
        column = lax.rsqrt(square * (1.0 / INNER) + EPS).T[:, 0:1]
        k["scale"][...] = jnp.broadcast_to(column, (ROWS, 128))

        @pl.loop(0, BLOCKS)
        def _(i):
            at = rows_at(i)
            total = part[s, at, quarter(place)].astype(F32)
            for d in range(1, 4):
                total = total + sum_in[s, d, at].astype(F32)
            total = (total * k["scale"][at][:, 0:1]).astype(BF)
            sum_own[s, at] = total
            k["out"][at, quarter(place)] = total

        copies = []
        for d in range(1, 4):
            copies.append(
                send(sum_own.at[s], k["out"].at[:, quarter(place)], s_sems[2].at[s, d], s_sems[3].at[s, d], heads[d - 1])
            )
        if s == 0:
            edge = slice(ROWS - RIM, ROWS)
            next_own[...] = (
                v_buf[edge, quarter(place)].astype(F32) + sum_own[0, edge].astype(F32)
            ).astype(BF)
            rim_in = []
            for d in range(4):
                dst = rim_buf.at[1, :, quarter(place)]
                target = {"head": shifted(place, d, 4), "seq": later}
                rim_in.append(send(next_own, dst, rim_send.at[1 + d], rim_recv.at[1 + d], target))
        finish(copies)

        @pl.loop(0, BLOCKS)
        def _(i):
            at = rows_at(i)
            k["following"][at] = (entering[at].astype(F32) + k["out"][at].astype(F32)).astype(BF)

        entering = k["following"]

    for copy in across:
        copy.wait_send()
    for move in store_theirs(core, (bd_w, zx_w, out_w), (bd_t, zx_t, out_t), t_sem):
        move.wait()


def store_theirs(core, held, dst, sem):
    return [
        pltpu.make_async_copy(held[i].at[1 - core], dst[i], sem.at[i]) for i in range(3)
    ]


def forward(x_in, zx_m, bd_m, out_m, small_m, number):
    dma = pltpu.SemaphoreType.DMA
    sds = jax.ShapeDtypeStruct
    vm = pltpu.VMEM
    got = pl.pallas_call(
        forward_kernel,
        out_shape=[sds(shape, kind) for _, shape, kind in KEPT * 2]
        + [sds(zx_m.shape, BF), sds(bd_m.shape, BF), sds(out_m.shape, BF), sds((2, 16, WIDTH), F32)],
        in_specs=[ANY] * 4 + [VM],
        out_specs=[VM] * 32 + [ANY] * 3 + [VM],
        scratch_shapes=[
            vm((ROWS, WIDTH), BF),
            vm((2, RIM, WIDTH), BF),
            vm((2, WIDTH, WIDTH), BF),
            vm((2, WIDTH, 384), BF),
            vm((2, INNER_DEV, WIDTH), BF),
            vm((ROWS + RIM, 384), F32),
            vm((ROWS, INNER_DEV), BF),
            vm((ROWS, ROWS), F32),
            vm((ROWS, 128), F32),
            vm((ROWS, 128), F32),
            vm((ROWS, INNER_DEV), BF),
            vm((ROWS, 128), F32),
            vm((2, ROWS, WIDTH), BF),
            vm((2, 16, 16, 512), BF),
            vm((2, 16, 16, 512), BF),
            vm((2, 16, 16, 384), BF),
            vm((2, 16, 16, 384), BF),
            vm((2, 4, ROWS, 384), BF),
            vm((2, 8, ROWS), F32),
            vm((2, 4, 8, ROWS), F32),
            vm((2, ROWS, 384), BF),
            vm((RIM, 384), BF),
            dma((5,)),
            dma((5,)),
            dma((4,)),
            dma((5,)),
            dma((5,)),
            dma((2, 16)),
            dma((2, 16)),
            dma((2, 16)),
            dma((2, 16)),
            dma((2, 8)),
            dma((2, 8)),
            dma((2, 4)),
            dma((2, 4)),
            dma((3,)),
            dma,
        ],
        compiler_params=comm_params(number),
        name="forward_layers",
    )(x_in, zx_m, bd_m, out_m, small_m)
    kept = [{name: got[16 * s + i] for i, (name, _, _) in enumerate(KEPT)} for s in range(2)]
    return kept, got[32:36]


ZX, OUT = 96, 48
WIDE = ZX + OUT
SUB = WIDE + 32
SLOT = ("z", "x_pre", "bc_pre", "dt_pre", "la", "la_t", "xd", "bc_act", "x_act", "y", "decay", "state", "scale", "out")
SHAPES = {name: (shape, kind) for name, shape, kind in KEPT}


def add_rows(total, more):
    return total.astype(F32) + more.astype(F32)


def backward_kernel(*refs):
    cot_ref, x_ref, last_ref = refs[:3]
    held = (refs[3:6], refs[6:9])
    small_all = refs[9]
    saved = [{name: refs[10 + 16 * s + i] for i, (name, _, _) in enumerate(KEPT)} for s in range(2)]
    grads_ref, section_ref, leaving_ref = refs[42:45]
    rest = list(refs[45:])

    def take(count):
        got = rest[:count]
        del rest[:count]
        return got

    k = dict(zip(SLOT, take(len(SLOT))))
    normed_all, v_all, d_v, g_o_buf = take(4)
    zx_w, bd_w, out_w = take(3)
    own, spare, theirs, first, mid, second, ring = take(7)
    d_y_ref, d_z_ref, d_xd, d_y_low, wide_x, wide_y = take(6)
    scores_t, d_scores_t, d_bc, terms, direct, tail_ref, dt_ref = take(7)
    ext, d_zx, d_bd, part, sum_in, d_normed_ref, sum_own = take(7)
    chain_out, chain_in, chain_back, chain_got, state_grad = take(5)
    rim_buf, taps_ref, taps_in, taps_all, norm_ref, sums_ref, small_rows, head_in = take(8)
    k_sem, n_sem, w_sem, move_sem = take(4)
    c_sems, s_sems, rim_sems, swap_sems = take(4), take(4), take(2), take(2)
    cross_sems, one_sems, two_sems, head_sems, back_sems, last_sems = (
        take(2), take(2), take(2), take(2), take(2), take(2)
    )
    theirs_free, first_free = take(2)

    core, me, place = lax.axis_index("section"), lax.axis_index("seq"), lax.axis_index("head")
    x, z = lax.div(me, 4), lax.rem(me, 4)
    a = x + core * (z - x)
    b = z + core * (x - z)

    def at_place(i, j):
        return i * (4 - 3 * core) + j * (1 + 3 * core)

    other = {"section": 1 - core}
    heads = [{"head": shifted(place, d, 4)} for d in range(1, 4)]
    near = [{"seq": at_place(a, shifted(b, d, 4))} for d in range(1, 4)]
    far = [{"seq": at_place(shifted(a, d, 4), b)} for d in range(1, 4)]
    targets = [other] + [{"seq": shifted(me, d, 16)} for d in range(1, 16)] + heads
    targets += [{"section": 1 - core, "seq": at_place(shifted(a, d, 4), b)} for d in range(1, 4)]
    barrier = pltpu.get_barrier_semaphore()
    for target in targets:
        pl.semaphore_signal(barrier, inc=1, device_id=target, device_id_type=MESH)

    def load_kept(s):
        return [
            pltpu.make_async_copy(saved[s][name], k[name], k_sem.at[i]) for i, name in enumerate(SLOT)
        ]

    def load_rows(s):
        source = x_ref.at[core] if s == 0 else saved[0]["following"]
        return [
            pltpu.make_async_copy(saved[s]["normed"], normed_all.at[s], n_sem.at[s, 0]),
            pltpu.make_async_copy(source, v_all.at[s], n_sem.at[s, 1]),
        ]

    weight_slots = (zx_w, bd_w, out_w)

    def load_weight(s, i):
        @pl.when(core == s)
        def _():
            pltpu.make_async_copy(held[0][i], weight_slots[i], w_sem.at[i]).start()

        @pl.when(core != s)
        def _():
            pltpu.make_async_copy(held[1][i], weight_slots[i], w_sem.at[i]).start()

    def wait_weight(i):
        pltpu.make_async_copy(held[0][i], weight_slots[i], w_sem.at[i]).wait()

    load_g_o = pltpu.make_async_copy(cot_ref.at[core], g_o_buf, n_sem.at[0, 2])
    load_g_o.start()
    load_weight(1, 2)
    for move in load_kept(1):
        move.start()
    load_weight(1, 0)
    load_weight(1, 1)
    for s in (1, 0):
        for move in load_rows(s):
            move.start()

    @pl.loop(0, 4)
    def _(i):
        @pl.loop(0, 4)
        def _(j):
            blank = jnp.zeros((16, INNER_DEV), BF)
            own[0, i, j, WIDE + 16 :] = blank
            own[1, i, j, WIDE + 16 :] = blank
            spare[i, j, WIDE + 16 :] = blank

    small_rows[...] = jnp.zeros_like(small_rows)
    pl.semaphore_wait(barrier, len(targets))

    def swapped(i, src, dst):
        return pltpu.make_async_remote_copy(
            src_ref=src,
            dst_ref=dst.at[core],
            send_sem=swap_sems[0].at[i],
            recv_sem=swap_sems[1].at[i],
            device_id=other,
            device_id_type=MESH,
        )

    @pl.when(core == 0)
    def _():
        swapped(0, last_ref, section_ref).start()

    @pl.when(core == 1)
    def _():
        swapped(0, saved[0]["following"], section_ref).start()

    spans = ((ZX, WIDE), (0, ZX), (WIDE, SUB))

    def cross(s, piece):
        lo, hi = spans[piece]
        return pltpu.make_async_remote_copy(
            src_ref=spare.at[:, :, lo:hi],
            dst_ref=theirs.at[:, :, lo:hi],
            send_sem=cross_sems[0].at[s, piece],
            recv_sem=cross_sems[1].at[s, piece],
            device_id=other,
            device_id_type=MESH,
        )

    def reduction(s, group):
        lo, hi = ((0, WIDE), (WIDE, SUB))[group]
        for piece in ((0, 1), (2,))[group]:
            cross(s, piece).wait_recv()

        @pl.loop(0, 4)
        def _(i):
            @pl.loop(0, 4)
            def _(j):
                own[s, i, j, lo:hi] = add_rows(own[s, i, j, lo:hi], theirs[i, j, lo:hi]).astype(BF)

        if s == 0 and group == 0:
            pl.semaphore_wait(first_free, 3)
        copies = []
        for d in range(1, 4):
            src = own.at[s, :, shifted(b, d, 4), lo:hi]
            dst = first.at[d - 1, :, lo:hi]
            copies.append(
                send(src, dst, one_sems[0].at[s, group, d], one_sems[1].at[s, group, d], near[d - 1])
            )
        yield
        finish(copies)

        @pl.loop(0, 4)
        def _(i):
            total = own[s, i, b, lo:hi].astype(F32)
            for d in range(3):
                total = total + first[d, i, lo:hi].astype(F32)
            mid[i, lo:hi] = total.astype(BF)

        copies = []
        for d in range(1, 4):
            src = mid.at[shifted(a, d, 4), lo:hi]
            dst = second.at[s, d - 1, lo:hi]
            copies.append(
                send(src, dst, two_sems[0].at[s, group, d], two_sems[1].at[s, group, d], far[d - 1])
            )
        yield
        finish(copies)
        total = mid[a, lo:hi].astype(F32)
        for d in range(3):
            total = total + second[s, d, lo:hi].astype(F32)
        ring[s, a, lo:hi] = total.astype(BF)
        if group:
            copies = []
            for d in range(1, 4):
                src = ring.at[s, a, WIDE : WIDE + 16]
                copies.append(
                    send(src, head_in.at[s, d - 1], head_sems[0].at[s, d], head_sems[1].at[s, d], heads[d - 1])
                )
            yield
            finish(copies)
            total = ring[s, a, WIDE : WIDE + 16].astype(F32)
            for d in range(3):
                total = total + head_in[s, d].astype(F32)
            ring[s, a, WIDE : WIDE + 16] = total.astype(BF)
        copies = []
        for d in range(1, 4):
            block = ring.at[s, a, lo:hi]
            copies.append(
                send(block, block, back_sems[0].at[s, group, d], back_sems[1].at[s, group, d], far[d - 1])
            )
        yield
        finish(copies)
        src = ring.at[s, :, lo:hi]

        def last(d, half, spot):
            return pltpu.make_async_remote_copy(
                src_ref=src,
                dst_ref=grads_ref.at[half, :, spot, lo:hi],
                send_sem=last_sems[0].at[s, group, d],
                recv_sem=last_sems[1].at[s, group, half, d],
                device_id={"section": s, "seq": at_place(a, shifted(b, d, 4))},
                device_id_type=MESH,
            )

        stay = pltpu.make_async_copy(src, grads_ref.at[core, :, b, lo:hi], last_sems[0].at[s, group, 0])
        for d in range(1, 4):
            last(d, core, b).start()

        @pl.when(core == s)
        def _():
            stay.start()

        @pl.when(core != s)
        def _():
            last(0, core, b).start()

        yield
        for d in range(1, 4):
            last(d, core, b).wait_send()

        @pl.when(core == s)
        def _():
            stay.wait()
            for d in range(1, 4):
                last(d, s, b).wait_recv()
            for d in range(4):
                last(d, 1 - s, b).wait_recv()

        @pl.when(core != s)
        def _():
            last(0, core, b).wait_send()

        yield

    member_rows = lax.broadcasted_iota(jnp.int32, (INNER_DEV, 128), 0)
    member_lanes = lax.broadcasted_iota(jnp.int32, (INNER_DEV, 128), 1) * HEAD_DIM
    inside = (member_rows >= member_lanes) & (member_rows < member_lanes + HEAD_DIM)
    member = jnp.where(inside, 1.0, 0.0).astype(BF)

    def sums_of(value):
        high, low = two_part(value)
        return dot(high, member) + dot(low, member)

    half_cols = [pl.ds(pl.multiple_of(h * INNER_DEV, INNER_DEV), INNER_DEV) for h in (core, 1 - core)]
    wide, loose = None, None
    load_g_o.wait()
    for s in (1, 0):
        small = small_all.at[s]
        normed, v_ref = normed_all.at[s], v_all.at[s]
        g_o_ref = g_o_buf if s else d_v.at[1]
        y_ref, z_ref, la_ref, la_t_ref = k["y"], k["z"], k["la"], k["la_t"]
        xd_ref, bc_act, x_act = k["xd"], k["bc_act"], k["x_act"]
        x_pre, bc_pre = k["x_pre"], k["bc_pre"]
        stages = (own.at[s], spare)

        sums_ref[...] = jnp.zeros_like(sums_ref)
        wait_weight(2)

        @pl.loop(0, 3)
        def _(j):
            d_xd[:, tile_at(j)] = dot_last(g_o_ref[...], out_w[tile_at(j), :])

        if s:
            load_weight(0, 2)
        finish(load_kept(s))
        if s:
            finish(load_rows(1))

        @pl.loop(0, BLOCKS)
        def _(i):
            at = rows_at(i)
            gain = small[S_GATE : S_GATE + 1, :INNER_DEV]
            scale = k["scale"][at][:, 0:1]
            act, gate, dm = x_act[at], z_ref[at], d_xd[at]
            ssd = y_ref[at] + small[S_SKIP : S_SKIP + 1, :INNER_DEV] * act
            sigma = jax.nn.sigmoid(gate)
            gate_silu = gate * sigma
            gated = ssd * gate_silu
            scaled = gated * scale
            mean = jnp.sum(g_o_ref[at].astype(F32) * k["out"][at].astype(F32), axis=-1, keepdims=True)
            mean = mean * scale * scale * (1.0 / INNER)
            wide_x[at] = (scaled * gain).astype(BF)
            d_gated = scale * gain * dm - gated * mean
            d_y = d_gated * gate_silu
            d_y_ref[at] = d_y
            d_y_low[at] = d_y.astype(BF)
            d_z_ref[at] = (d_gated * ssd * sigma * (1.0 + gate * (1.0 - sigma))).astype(BF)
            wide_y[at] = (spread(jnp.exp(la_ref[at])) * d_y).astype(BF)
            sums_ref[0:1] += jnp.sum(scaled * dm, axis=0, keepdims=True)
            sums_ref[1:2] += jnp.sum(d_y * act, axis=0, keepdims=True)

        b_rows, c_rows = bc_act[:, :STATE], bc_act[:, STATE:]
        chain_load(dot_first(c_rows, wide_y[...]), k["decay"], chain_out)
        copies = spread_send(chain_out, chain_in, me, c_sems[0].at[s], c_sems[1].at[s])

        if s == 0:
            for piece in range(3):
                cross(1, piece).wait_send()
        for stage, cols in zip(stages, half_cols):
            for j in range(2):
                got = dot_first(wide_x[:, 384 * j : 384 * j + 384], g_o_ref[:, cols]).astype(BF)
                for i in range(8):
                    sub = 8 * j + i
                    stage[sub // 4, sub % 4, ZX:WIDE] = got[OUT * i : OUT * i + OUT]
        if s == 0:
            next(loose)
            pl.semaphore_signal(theirs_free, inc=1, device_id=other, device_id_type=MESH)
            pl.semaphore_wait(theirs_free, 1)
        cross(s, 0).start()

        la = la_ref[...]
        tail_ref[...] = jnp.exp(la[ROWS - 1 : ROWS] - la)
        dt_in = k["dt_pre"][...] + small[S_BIAS : S_BIAS + 1, :128]
        dt_ref[...] = softplus(dt_in)
        scores_t[...] = dot_last(b_rows, c_rows)

        def heads_of(half):
            base = half * 128
            rows = slice(base, base + 128)
            t = lax.broadcasted_iota(jnp.int32, (128, ROWS - base), 1)
            later = t >= lax.broadcasted_iota(jnp.int32, (128, ROWS - base), 0)
            total = jnp.zeros((128, ROWS - base), F32)
            for pair in range(HEADS_DEV // 2):
                parts = []
                for h in (2 * pair, 2 * pair + 1):
                    cols = slice(h * HEAD_DIM, (h + 1) * HEAD_DIM)
                    gap = la_t_ref[h : h + 1, base:] - la_ref[rows, h : h + 1]
                    decay = jnp.exp(jnp.where(later, gap, -1e30))
                    total = total + decay * dot_last(xd_ref[rows, cols], d_y_low[base:, cols])
                    mixing = (scores_t[rows, base:] * decay).astype(BF)
                    parts.append(dot(mixing, d_y_low[base:, cols]))
                d_xd[rows, pair * 128 : pair * 128 + 128] = jnp.concatenate(parts, axis=1)
            if half:
                d_scores_t[rows, 0:128] = jnp.zeros((128, 128), BF)
            d_scores_t[rows, base:] = total.astype(BF)

        heads_of(0)
        finish(copies)
        chain_scan(False, chain_in, chain_back)
        copies = spread_send(chain_back, chain_got, me, c_sems[2].at[s], c_sems[3].at[s])
        heads_of(1)
        if s == 0:
            next(wide)
            next(loose)
            for target in near:
                pl.semaphore_signal(first_free, inc=1, device_id=target, device_id_type=MESH)
        finish(copies)
        chain_unload(chain_got, state_grad)
        norm_ref[...] = jnp.zeros_like(norm_ref)
        taps_ref[...] = jnp.zeros_like(taps_ref)

        @pl.loop(0, BLOCKS)
        def _(i):
            at = rows_at(i)
            tail = spread(tail_ref[at])
            xd = xd_ref[at].astype(F32)
            wide_x[at] = (tail * xd).astype(BF)
            state_part = tail * dot(bc_act[at, :STATE], state_grad[...])
            got = d_xd[at] + state_part
            d_xd[at] = got
            norm_ref[1:2, :INNER_DEV] += jnp.sum(xd * state_part, axis=0, keepdims=True)
            terms[at] = sums_of(d_y_low[at].astype(F32) * y_ref[at] - xd * got)
            direct[at] = sums_of(x_act[at] * got)

        d_bc[:, :STATE] = dot(d_scores_t[...], c_rows) + dot_last(wide_x[...], state_grad[...])
        d_bc[:, STATE:] = dot_first(d_scores_t[...], b_rows) + dot_last(wide_y[...], k["state"][...])
        end_wide = spread(jnp.exp(la[ROWS - 8 : ROWS]))[7:8]
        both = state_grad[...].astype(F32) * k["state"][...].astype(F32)
        tail_sum = norm_ref[1:2, :INNER_DEV] + end_wide * jnp.sum(both, axis=0, keepdims=True)
        tail_sum = sums_of(jnp.broadcast_to(tail_sum, (16, INNER_DEV)))[0:1]
        d_log = running(terms[...], True) + tail_sum
        rate = small[S_RATE : S_RATE + 1, :128]
        d_dt = direct[...] + rate * d_log
        d_dt_pre = d_dt * jax.nn.sigmoid(dt_in)
        d_bd[:, 256:] = d_dt_pre.astype(BF)
        sums_ref[2:3, :128] = jnp.sum(dt_ref[...] * d_log, axis=0, keepdims=True) * rate
        sums_ref[3:4, :128] = jnp.sum(d_dt_pre, axis=0, keepdims=True)

        @pl.loop(0, BLOCKS)
        def _(i):
            at = rows_at(i)
            taps = small[S_CONV : S_CONV + 4]
            pre = x_pre[rows_at(i, RIM)]
            d_x = spread(dt_ref[at]) * d_xd[at] + small[S_SKIP : S_SKIP + 1, :INNER_DEV] * d_y_ref[at]
            d_xc = d_x * silu_slope(conv_rows(pre, taps[:, :INNER_DEV]))
            ext[at, :INNER_DEV] = d_xc
            for t in range(4):
                moved = pre[RIM - 3 + t : RIM - 3 + t + STEP]
                taps_ref[t : t + 1, :INNER_DEV] += jnp.sum(moved * d_xc, axis=0, keepdims=True)
            pre = bc_pre[rows_at(i, RIM)]
            d_bcc = d_bc[at] * silu_slope(conv_rows(pre, taps[:, INNER_DEV : INNER_DEV + 256]))
            ext[at, INNER_DEV:] = d_bcc
            for t in range(4):
                moved = pre[RIM - 3 + t : RIM - 3 + t + STEP]
                taps_ref[t : t + 1, INNER_DEV:] += jnp.sum(moved * d_bcc, axis=0, keepdims=True)

        rim = send(
            ext.at[0:8], rim_buf, rim_sems[0].at[s], rim_sems[1].at[s], {"seq": shifted(me, -1, 16)}
        )
        if s:
            for move in load_kept(0):
                move.start()
        taps_all[...] = taps_ref[:, INNER_DEV:]

        for stage, h in zip(stages, (core, 1 - core)):

            @pl.when(h == 0)
            def _():
                @pl.loop(0, 4)
                def _(j):
                    got = dot_first(normed[RIM:, tile_at(j, 384)], d_z_ref[...]).astype(BF)
                    for i in range(4):
                        stage[j, i, 0:ZX] = got[ZX * i : ZX * i + ZX]

        rim.wait()

        @pl.when(me == 15)
        def _():
            rim_buf[...] = jnp.zeros_like(rim_buf)

        ext[ROWS : ROWS + 8] = rim_buf[...]

        @pl.loop(0, BLOCKS)
        def _(i):
            at = rows_at(i)
            taps = small[S_CONV : S_CONV + 4]
            block = ext[rows_at(i, 8)]
            d_pre = taps[0:1, : INNER_DEV + 256] * block[3 : 3 + STEP]
            for t in range(1, 4):
                d_pre = d_pre + taps[t : t + 1, : INNER_DEV + 256] * block[3 - t : 3 - t + STEP]
            d_zx[at, :INNER_DEV] = d_z_ref[at]
            d_zx[at, INNER_DEV:] = d_pre[:, :INNER_DEV].astype(BF)
            d_bd[at, :256] = d_pre[:, INNER_DEV:].astype(BF)

        if s:
            wait_weight(0)
            wait_weight(1)
        else:
            next(wide)
            next(loose)
            wait_weight(0)
            wait_weight(1)

        @pl.loop(0, 6)
        def _(j):
            got = dot_last(d_zx[...], zx_w[tile_at(j), :]) + dot_last(d_bd[...], bd_w[tile_at(j), :])
            part[:, tile_at(j)] = got.astype(BF)

        if s:
            load_weight(0, 0)
            load_weight(0, 1)
        copies = []
        for d in range(1, 4):
            src = part.at[:, quarter(shifted(place, d, 4))]
            copies.append(send(src, sum_in.at[d - 1], s_sems[0].at[s, d], s_sems[1].at[s, d], heads[d - 1]))
        for d in range(1, 4):
            copies.append(
                send(taps_all, taps_in.at[d - 1], s_sems[0].at[s, d + 4], s_sems[1].at[s, d + 4], heads[d - 1])
            )
        for stage, h in zip(stages, (core, 1 - core)):

            @pl.when(h == 1)
            def _():
                @pl.loop(0, 4)
                def _(j):
                    got = dot_first(normed[RIM:, tile_at(j, 384)], d_zx[:, INNER_DEV:]).astype(BF)
                    for i in range(4):
                        stage[j, i, 0:ZX] = got[ZX * i : ZX * i + ZX]

        cross(s, 1).start()
        for stage, cols in zip(stages, half_cols):
            got = dot_first(d_bd[...], normed[RIM:, cols])
            for i in range(16):
                stage[i // 4, i % 4, WIDE : WIDE + 16] = got[16 * i : 16 * i + 16].astype(BF)
            stage[0, 0, WIDE + 16 :] = got[256:272].astype(BF)
        if s == 0:
            next(wide)
            next(loose)
        finish(copies)
        total = taps_all[...]
        for d in range(3):
            total = total + taps_in[d]
        taps_ref[:, INNER_DEV:] = total

        @pl.loop(0, BLOCKS)
        def _(i):
            at = rows_at(i)
            total = part[at, quarter(place)].astype(F32)
            for d in range(3):
                total = total + sum_in[d, at].astype(F32)
            total = total.astype(BF)
            sum_own[at] = total
            d_normed_ref[at, quarter(place)] = total

        copies = []
        for d in range(1, 4):
            dst = d_normed_ref.at[:, quarter(place)]
            copies.append(send(sum_own, dst, s_sems[2].at[s, d], s_sems[3].at[s, d], heads[d - 1]))
        old_loose, old_wide = loose, wide
        wide = reduction(s, 0)
        next(wide)
        finish(copies)
        norm_ref[...] = jnp.zeros_like(norm_ref)

        @pl.loop(0, BLOCKS)
        def _(i):
            at = rows_at(i)
            v = v_ref[at].astype(F32)
            scale = lax.rsqrt(jnp.mean(v * v, axis=-1, keepdims=True) + EPS)
            d_normed = d_normed_ref[at].astype(F32)
            scaled = v * scale
            norm_ref[0:1] += jnp.sum(scaled * d_normed, axis=0, keepdims=True)
            weighted = d_normed * small[S_NORM : S_NORM + 1]
            mean = jnp.mean(v * weighted, axis=-1, keepdims=True) * scale * scale
            d_v[s, at] = (scale * weighted - scaled * mean + g_o_ref[at].astype(F32)).astype(BF)

        for h in range(2):
            small_rows[h, 0:1] = norm_ref[0:1, h * INNER_DEV : (h + 1) * INNER_DEV]
            small_rows[h, 1:5] = taps_ref[0:4, :INNER_DEV]
            small_rows[h, 5:9] = sums_ref[0:4]
            small_rows[h, 9:13, 0:256] = taps_ref[0:4, INNER_DEV:]
        for stage, h in zip(stages, (core, 1 - core)):
            stage[0, 1, WIDE + 16 :] = small_rows[h].astype(BF)
        cross(s, 2).start()
        loose = reduction(s, 1)

        @pl.when(core == 1 - s)
        def _():
            swapped(1, d_v.at[s], leaving_ref).start()

        @pl.when(core == s)
        def _():
            pltpu.make_async_copy(d_v.at[s], leaving_ref.at[s], move_sem.at[1]).start()

        if s:

            @pl.when(core == 0)
            def _():
                pltpu.make_async_copy(v_all.at[1], section_ref.at[0], move_sem.at[0]).start()

            finish(load_rows(0))

            @pl.when(core == 1)
            def _():
                pltpu.make_async_copy(last_ref, g_o_buf, move_sem.at[0]).start()

    @pl.when(core == 1)
    def _():
        pltpu.make_async_copy(last_ref, g_o_buf, move_sem.at[0]).wait()
        pltpu.make_async_copy(g_o_buf, section_ref.at[1], move_sem.at[0]).start()

    order = (old_loose, loose, loose, loose, loose, wide, loose, wide, wide, wide, loose, old_wide, old_loose)
    for turn in order:
        next(turn)
    for piece in range(3):
        cross(0, piece).wait_send()
    swapped(0, last_ref, section_ref).wait()
    swapped(1, d_v.at[0], leaving_ref).wait()
    pltpu.make_async_copy(d_v.at[0], leaving_ref.at[0], move_sem.at[1]).wait()
    pltpu.make_async_copy(d_v.at[0], section_ref.at[0], move_sem.at[0]).wait()


def backward(cotangent, x_in, last, held, smalls, kept, number):
    dma = pltpu.SemaphoreType.DMA
    regular = pltpu.SemaphoreType.REGULAR
    sds = jax.ShapeDtypeStruct
    vm = pltpu.VMEM
    halves = (4, 4, SUB, INNER_DEV)
    rows_low = vm((ROWS, INNER_DEV), BF)
    rows_wide = vm((ROWS, INNER_DEV), F32)
    steps = vm((ROWS, 128), F32)
    scratch = [vm(*SHAPES[name]) for name in SLOT]
    scratch += [
        vm((2, ROWS + RIM, WIDTH), BF),
        vm((2, ROWS, WIDTH), BF),
        vm((2, ROWS, WIDTH), BF),
        vm((ROWS, WIDTH), BF),
        vm((WIDTH, WIDTH), BF),
        vm((WIDTH, 384), BF),
        vm((INNER_DEV, WIDTH), BF),
        vm((2,) + halves, BF),
        vm(halves, BF),
        vm(halves, BF),
        vm((3, 4, SUB, INNER_DEV), BF),
        vm((4, SUB, INNER_DEV), BF),
        vm((2, 3, SUB, INNER_DEV), BF),
        vm((2, 4, SUB, INNER_DEV), BF),
        rows_wide, rows_low, rows_wide, rows_low, rows_low, rows_low,
        vm((ROWS, ROWS), F32),
        vm((ROWS, ROWS), BF),
        vm((ROWS, 256), F32),
        steps, steps, steps, steps,
        vm((ROWS + 8, INNER_DEV + 256), F32),
        vm((ROWS, WIDTH), BF),
        vm((ROWS, 384), BF),
        vm((ROWS, WIDTH), BF),
        vm((3, ROWS, 384), BF),
        vm((ROWS, WIDTH), BF),
        vm((ROWS, 384), BF),
        vm((16, 16, 512), BF),
        vm((16, 16, 512), BF),
        vm((16, 16, 384), BF),
        vm((16, 16, 384), BF),
        vm((STATE, INNER_DEV), BF),
        vm((8, INNER_DEV + 256), F32),
        vm((8, INNER_DEV + 256), F32),
        vm((3, 8, 256), F32),
        vm((8, 256), F32),
        vm((8, WIDTH), F32),
        vm((8, INNER_DEV), F32),
        vm((2, 16, INNER_DEV), F32),
        vm((2, 3, 16, INNER_DEV), BF),
        dma((len(SLOT),)),
        dma((2, 3)),
        dma((3,)),
        dma((2,)),
    ]
    scratch += [dma((2, 16))] * 4 + [dma((2, 8))] * 2 + [dma((2, 4))] * 2
    scratch += [dma((2,))] * 4 + [dma((2, 3))] * 2
    scratch += [dma((2, 2, 4))] * 4 + [dma((2, 4))] * 2 + [dma((2, 2, 4))] * 2
    scratch += [dma((2, 2, 4)), dma((2, 2, 2, 4)), regular, regular]
    flat = [kept[s][name] for s in range(2) for name, _, _ in KEPT]
    return pl.pallas_call(
        backward_kernel,
        out_shape=[sds((2,) + halves, BF), sds((2, ROWS, WIDTH), BF), sds((2, ROWS, WIDTH), BF)],
        in_specs=[ANY] * 9 + [VM] + [ANY] * 32,
        out_specs=[ANY] * 3,
        scratch_shapes=scratch,
        compiler_params=comm_params(number),
        name="backward_layers",
    )(cotangent, x_in, last, *held, smalls, *flat)


def widen_kernel(a_ref, zx_ref, out_ref, bc_ref, rest_ref):
    for h in range(2):
        cols = slice(h * INNER_DEV, (h + 1) * INNER_DEV)
        zx_ref[:, h, :] = a_ref[h, 0, :ZX].astype(F32)
        out_ref[:, cols] = a_ref[h, 0, ZX:WIDE].astype(F32)
        bc_ref[:, cols] = a_ref[h, 0, WIDE : WIDE + 16].astype(F32)
        rest_ref[:, cols] = a_ref[h, 0, WIDE + 16 :].astype(F32)


def widen(total):
    total = total.reshape(2, 16, SUB, INNER_DEV)
    return pl.pallas_call(
        widen_kernel,
        grid=(16,),
        out_shape=[
            jax.ShapeDtypeStruct((WIDTH, 2, INNER_DEV), F32),
            jax.ShapeDtypeStruct((INNER_DEV, WIDTH), F32),
            jax.ShapeDtypeStruct((256, WIDTH), F32),
            jax.ShapeDtypeStruct((256, WIDTH), F32),
        ],
        in_specs=[pl.BlockSpec((2, 1, SUB, INNER_DEV), lambda i: (0, i, 0, 0))],
        out_specs=[
            pl.BlockSpec((ZX, 2, INNER_DEV), lambda i: (i, 0, 0)),
            pl.BlockSpec((OUT, WIDTH), lambda i: (i, 0)),
            pl.BlockSpec((16, WIDTH), lambda i: (i, 0)),
            pl.BlockSpec((16, WIDTH), lambda i: (i, 0)),
        ],
        compiler_params=pltpu.CompilerParams(vmem_limit_bytes=VMEM_CAP),
        name="widen",
    )(total)


def pack_small(norm_gain, gate_gain, conv_x, conv_bc, dt_bias, a_log, d_skip):
    def row(a):
        return jnp.pad(a.reshape(1, -1).astype(F32), ((0, 0), (0, WIDTH - a.size)))

    taps = jnp.concatenate([conv_x, conv_bc], axis=1).astype(F32)
    rows = [
        row(norm_gain),
        row(gate_gain),
        jnp.pad(taps, ((0, 0), (0, WIDTH - taps.shape[1]))),
        row(dt_bias),
        row(-jnp.exp(a_log)),
        row(d_skip),
        row(jnp.repeat(d_skip, HEAD_DIM)),
        jnp.zeros((6, WIDTH), F32),
    ]
    return jnp.concatenate(rows, axis=0)


def on_device(
    x_in,
    norm_gain,
    w_zx,
    w_bc,
    w_dt,
    dt_bias,
    a_log,
    d_skip,
    conv_x,
    conv_bc,
    gate_gain,
    w_out,
    cotangent,
):
    small = pack_small(norm_gain[0], gate_gain[0], conv_x[0], conv_bc[0], dt_bias[0], a_log[0], d_skip[0])
    zx_m = w_zx[0].reshape(WIDTH, WIDTH)
    bd_m = jnp.concatenate([w_bc[0], w_dt[0], jnp.zeros((WIDTH, 128 - HEADS_DEV), BF)], axis=1)
    out_m = w_out[0]
    kept, (zx_t, bd_t, out_t, smalls) = forward(x_in, zx_m, bd_m, out_m, small, 0)
    held = (zx_m, bd_m, out_m, zx_t, bd_t, out_t)
    total, section_out, grads_in = backward(
        cotangent, x_in, kept[1]["following"], held, smalls, kept, 1
    )
    g_zx, g_out, g_bc, rest = widen(total)
    own = rest[16:32, :INNER_DEV]
    return (
        section_out[None],
        grads_in[None],
        rest[16:17],
        g_zx[None],
        g_bc.T[None],
        rest[0:HEADS_DEV].T[None],
        own[8:9, :HEADS_DEV],
        own[7:8, :HEADS_DEV],
        own[6].reshape(1, HEADS_DEV, HEAD_DIM).sum(axis=2),
        own[1:5][None],
        own[9:13, :256][None],
        own[5:6],
        g_out[None],
    )


def solution(mesh):
    in_specs = (
        P(None, "seq", None),
        P("section", None),
        P("section", None, None, "head"),
        P("section", None, None),
        P("section", None, "head"),
        P("section", "head"),
        P("section", "head"),
        P("section", "head"),
        P("section", None, "head"),
        P("section", None, None),
        P("section", "head"),
        P("section", "head", None),
        P(None, "seq", None),
    )
    out_specs = (
        P("section", None, "seq", None),
        P("section", None, "seq", None),
        P("section", None),
        P("section", None, None, "head"),
        P("section", None, None),
        P("section", None, "head"),
        P("section", "head"),
        P("section", "head"),
        P("section", "head"),
        P("section", None, "head"),
        P("section", None, None),
        P("section", "head"),
        P("section", "head", None),
    )
    return jax.shard_map(
        on_device, mesh=mesh, in_specs=in_specs, out_specs=out_specs, check_vma=False
    )
```

```python
import functools

import jax
import jax.numpy as jnp
from jax import lax
from jax.experimental import pallas as pl
from jax.experimental.pallas import tpu as pltpu
from jax.sharding import PartitionSpec as P

MESH = pl.DeviceIdType.MESH
F32 = jnp.float32
BF = jnp.bfloat16
EPS = 1e-05
INNER = 3072
ROWS = 256
WIDTH = 1536
INNER_DEV = 768
HEADS_DEV = 12
HEAD_DIM = 64
STATE = 128
RIM = 16
VMEM_CAP = 60 << 20
FIRST = (((0,), (0,)), ((), ()))
LAST = (((1,), (1,)), ((), ()))


def dot(a, b):
    return jnp.dot(a, b, preferred_element_type=F32)


def dot_first(a, b):
    return lax.dot_general(a, b, FIRST, preferred_element_type=F32)


def dot_last(a, b):
    return lax.dot_general(a, b, LAST, preferred_element_type=F32)


def two_part(a):
    high = a.astype(BF)
    return high, (a - high.astype(F32)).astype(BF)


def silu(a):
    return a * jax.nn.sigmoid(a)


def silu_slope(a):
    sigma = jax.nn.sigmoid(a)
    return sigma * (1.0 + a * (1.0 - sigma))


def spread(a):
    rows = a.shape[0]
    low_half = lax.broadcasted_iota(jnp.int32, (rows, 128), 1) < HEAD_DIM
    return jnp.concatenate(
        [
            jnp.where(low_half, a[:, 2 * j : 2 * j + 1], a[:, 2 * j + 1 : 2 * j + 2])
            for j in range(HEADS_DEV // 2)
        ],
        axis=1,
    )


def triangle(keep_after):
    t = lax.broadcasted_iota(jnp.int32, (ROWS, ROWS), 0)
    s = lax.broadcasted_iota(jnp.int32, (ROWS, ROWS), 1)
    return jnp.where((s >= t) if keep_after else (t >= s), 1.0, 0.0).astype(BF)


def running(a, keep_after):
    weights = triangle(keep_after)
    high, low = two_part(a)
    return dot(weights, high) + dot(weights, low)


S_NORM, S_GATE, S_CONV, S_BIAS, S_RATE, S_SKIP = 0, 1, 2, 6, 7, 9
STEP = 32
BLOCKS = ROWS // STEP


def softplus(a):
    return jnp.maximum(a, 0.0) + jnp.log1p(jnp.exp(-jnp.abs(a)))


def rows_at(i, more=0):
    return pl.ds(pl.multiple_of(i * STEP, STEP), STEP + more)


def tile_at(i, width=256, base=0):
    return pl.ds(pl.multiple_of(base + i * width, width), width)


def conv_rows(pre, taps):
    total = taps[0:1] * pre[RIM - 3 : RIM - 3 + STEP]
    for k in range(1, 4):
        total = total + taps[k : k + 1] * pre[RIM - 3 + k : RIM - 3 + k + STEP]
    return total


def shifted(place, distance, count):
    return lax.rem(place + distance + count, count)


def meet(targets):
    barrier = pltpu.get_barrier_semaphore()
    for target in targets:
        pl.semaphore_signal(barrier, inc=1, device_id=target, device_id_type=MESH)
    pl.semaphore_wait(barrier, len(targets))


def send(src, dst, send_sem, recv_sem, target):
    copy = pltpu.make_async_remote_copy(
        src_ref=src,
        dst_ref=dst,
        send_sem=send_sem,
        recv_sem=recv_sem,
        device_id=target,
        device_id_type=MESH,
    )
    copy.start()
    return copy


def comm_params(number):
    return pltpu.CompilerParams(
        collective_id=number, has_side_effects=True, vmem_limit_bytes=VMEM_CAP
    )


ANY = pl.BlockSpec(memory_space=pl.ANY)
VM = pl.BlockSpec(memory_space=pltpu.VMEM)


def quarter(place):
    return pl.ds(pl.multiple_of(place * 384, 384), 384)


KEPT = (
    ("normed", (ROWS + RIM, WIDTH), BF),
    ("z", (ROWS, INNER_DEV), F32),
    ("x_pre", (ROWS + RIM, INNER_DEV), F32),
    ("bc_pre", (ROWS + RIM, 256), F32),
    ("dt_pre", (ROWS, 128), F32),
    ("la", (ROWS, 128), F32),
    ("la_t", (128, ROWS), F32),
    ("xd", (ROWS, INNER_DEV), BF),
    ("bc_act", (ROWS, 256), BF),
    ("x_act", (ROWS, INNER_DEV), F32),
    ("y", (ROWS, INNER_DEV), F32),
    ("decay", (8, INNER_DEV), F32),
    ("state", (STATE, INNER_DEV), BF),
    ("scale", (ROWS, 128), F32),
    ("out", (ROWS, WIDTH), BF),
    ("following", (ROWS, WIDTH), BF),
)


def chain_load(own, decay, out_buf):
    for j in range(16):
        rows = own[8 * j : 8 * j + 8]
        out_buf[j, :, 0:384] = jnp.concatenate([rows[:, :384], rows[:, 384:]], axis=0).astype(BF)
    six = jnp.concatenate([decay[0:1, 128 * k : 128 * k + 128] for k in range(6)] * 3, axis=0)
    six = six[0:16].astype(BF)
    for j in range(16):
        out_buf[j, :, 384:512] = six


def chain_scan(forward, in_buf, back_buf):
    state = jnp.zeros((16, 384), F32)
    for step in range(16):
        i = step if forward else 15 - step
        back_buf[i] = state.astype(BF)
        part = in_buf[i].astype(F32)
        decay = jnp.concatenate(
            [
                jnp.concatenate(
                    [
                        jnp.broadcast_to(part[3 * half + k : 3 * half + k + 1, 384:512], (8, 128))
                        for k in range(3)
                    ],
                    axis=1,
                )
                for half in range(2)
            ],
            axis=0,
        )
        state = decay * state + part[:, 0:384]


def chain_unload(got_buf, state_ref):
    for j in range(8):
        first, second = got_buf[2 * j].astype(F32), got_buf[2 * j + 1].astype(F32)
        for half in range(2):
            rows = jnp.concatenate(
                [first[8 * half : 8 * half + 8], second[8 * half : 8 * half + 8]], axis=0
            )
            state_ref[16 * j : 16 * j + 16, 384 * half : 384 * half + 384] = rows.astype(BF)


def spread_send(src, dst, me, send_sem, recv_sem):
    copies = []
    for d in range(1, 16):
        to = shifted(me, d, 16)
        copies.append(send(src.at[to], dst.at[me], send_sem.at[d], recv_sem.at[d], {"seq": to}))
    dst[me] = src[me]
    return copies


def finish(copies):
    for copy in copies:
        copy.wait()


def norm_rows(v, gain):
    v = v.astype(F32)
    scale = lax.rsqrt(jnp.mean(v * v, axis=-1, keepdims=True) + EPS)
    return (v * scale * gain).astype(BF)


def forward_kernel(*refs):
    x_ref, zx_m, bc_m, out_m, dt_m = refs[:5]
    norm_gain, gate_gain, conv_x, conv_bc, dt_bias, a_log, d_skip = refs[5:12]
    kept = [{name: refs[12 + 16 * s + i] for i, (name, _, _) in enumerate(KEPT)} for s in range(2)]
    zx_t, bc_t, out_t, small_w, dt_w = refs[44:49]
    v_buf, rim_buf, zx_w, bc_w, out_w = refs[49:54]
    tail_x, scores, dt_buf, tail, low, sq, part = refs[54:61]
    chain_out, chain_in, chain_back, chain_got = refs[61:65]
    sum_in, square_out, square_in, sum_own, next_own = refs[65:70]
    w_send, w_recv, w_own, rim_send, rim_recv = refs[70:75]
    c_sems, s_sems, t_sem, v_sem = refs[75:79], refs[79:83], refs[83], refs[84]

    core, me, place = lax.axis_index("section"), lax.axis_index("seq"), lax.axis_index("head")
    other = {"section": 1 - core}
    later = shifted(me, 1, 16)
    barrier = pltpu.get_barrier_semaphore()
    targets = [other]
    targets += [{"seq": shifted(me, d, 16)} for d in range(1, 16)]
    heads = [{"head": shifted(place, d, 4)} for d in range(1, 4)]
    targets += heads
    targets += [{"head": shifted(place, d, 4), "seq": shifted(me, -1, 16)} for d in range(1, 4)]
    for target in targets:
        pl.semaphore_signal(barrier, inc=1, device_id=target, device_id_type=MESH)

    moves = [
        (bc_m, bc_w.at[core]),
        (zx_m.at[:, INNER_DEV:], zx_w.at[core, :, INNER_DEV:]),
        (zx_m.at[:, :INNER_DEV], zx_w.at[core, :, :INNER_DEV]),
        (out_m, out_w.at[core]),
    ]
    own_moves = [pltpu.make_async_copy(src, dst, w_own.at[i]) for i, (src, dst) in enumerate(moves)]
    for move in own_moves:
        move.start()
    load_v = pltpu.make_async_copy(x_ref.at[core], v_buf, v_sem)
    load_v.start()
    small_w[core] = jnp.zeros((16, WIDTH), F32)
    small_w[core, S_NORM : S_NORM + 1] = norm_gain[...]
    small_w[core, S_GATE : S_GATE + 1, :INNER_DEV] = gate_gain[...]
    small_w[core, S_CONV : S_CONV + 4, :INNER_DEV] = conv_x[...].astype(F32)
    small_w[core, S_CONV : S_CONV + 4, INNER_DEV : INNER_DEV + 256] = conv_bc[...].astype(F32)
    small_w[core, S_BIAS : S_BIAS + 1, 0:HEADS_DEV] = dt_bias[...]
    small_w[core, S_RATE : S_RATE + 1, 0:HEADS_DEV] = -jnp.exp(a_log[...])
    small_w[core, 8:9, 0:HEADS_DEV] = d_skip[...]
    skip_wide = spread(small_w[core, 8:16, 0:128])
    small_w[core, S_SKIP : S_SKIP + 1, :INNER_DEV] = skip_wide[0:1]
    dt_rows = jnp.concatenate([dt_m[...].astype(F32), jnp.zeros((4, WIDTH), F32)], axis=0)
    dt_w[core, 0:16] = dt_rows.astype(BF)
    for s in range(2):
        dt_w[s, 16:] = jnp.zeros((112, WIDTH), BF)
    pl.semaphore_wait(barrier, len(targets))
    rim_copy = send(x_ref.at[core, ROWS - RIM :], rim_buf.at[0], rim_send.at[0], rim_recv.at[0], {"seq": later})
    across = [
        send(small_w.at[core], small_w.at[core], w_send.at[4], w_recv.at[4], other),
        send(dt_w.at[core, 0:16], dt_w.at[core, 0:16], w_send.at[5], w_recv.at[5], other),
    ]
    for i, (src, dst) in enumerate(moves):
        across.append(send(src, dst, w_send.at[i], w_recv.at[i], other))

    def arrive(section, i):
        @pl.when(core == section)
        def _():
            own_moves[i].wait()

        @pl.when(core != section)
        def _():
            across[i + 2].wait_recv()

    load_v.wait()
    rim_copy.wait()

    @pl.when(me == 0)
    def _():
        rim_buf[0] = jnp.zeros((RIM, WIDTH), BF)

    across[0].wait_recv()
    across[1].wait_recv()
    entering = v_buf
    for s in range(2):
        k = kept[s]
        small = small_w.at[s]
        normed, z_ref, x_pre, bc_pre, la_ref, la_t_ref = (
            k["normed"], k["z"], k["x_pre"], k["bc_pre"], k["la"], k["la_t"]
        )
        xd_ref, bc_act, x_act, y_ref = k["xd"], k["bc_act"], k["x_act"], k["y"]
        gain = small[S_NORM : S_NORM + 1]
        if s:
            finish(rim_in)

            @pl.when(me == 0)
            def _():
                rim_buf[1] = jnp.zeros((RIM, WIDTH), BF)

        normed[0:RIM] = norm_rows(rim_buf[s], gain)

        @pl.loop(0, ROWS // 16)
        def _(i):
            at = pl.ds(pl.multiple_of(i * 16, 16), 16)
            normed[pl.ds(pl.multiple_of(i * 16 + RIM, 16), 16)] = norm_rows(entering[at], gain)

        arrive(s, 0)
        bc_pre[...] = dot(normed[...], bc_w[s])
        dt_raw = dot_last(normed[RIM:], dt_w[s])
        k["dt_pre"][...] = dt_raw
        arrive(s, 1)

        @pl.loop(0, 3)
        def _(j):
            x_pre[:, tile_at(j)] = dot(normed[...], zx_w[s, :, tile_at(j, 256, INNER_DEV)])

        dt = softplus(dt_raw + small[S_BIAS : S_BIAS + 1, :128])
        dt_buf[...] = dt
        la = running(dt * small[S_RATE : S_RATE + 1, :128], False)
        la_ref[...] = la
        la_t_ref[...] = la.T
        tail[...] = jnp.exp(la[ROWS - 1 : ROWS] - la)
        decay = jnp.broadcast_to(spread(jnp.exp(la[ROWS - 8 : ROWS]))[7:8], (8, INNER_DEV))
        k["decay"][...] = decay

        @pl.loop(0, BLOCKS)
        def _(i):
            taps = small[S_CONV : S_CONV + 4]
            act = silu(conv_rows(x_pre[rows_at(i, RIM)], taps[:, :INNER_DEV]))
            x_act[rows_at(i)] = act
            xd = (act * spread(dt_buf[rows_at(i)])).astype(BF)
            xd_ref[rows_at(i)] = xd
            tail_x[rows_at(i)] = (xd.astype(F32) * spread(tail[rows_at(i)])).astype(BF)
            bc = conv_rows(bc_pre[rows_at(i, RIM)], taps[:, INNER_DEV : INNER_DEV + 256])
            bc_act[rows_at(i)] = silu(bc).astype(BF)

        b_rows, c_rows = bc_act[:, :STATE], bc_act[:, STATE:]
        chain_load(dot_first(b_rows, tail_x[...]), decay, chain_out.at[s])
        copies = spread_send(chain_out.at[s], chain_in.at[s], me, c_sems[0].at[s], c_sems[1].at[s])
        arrive(s, 2)

        @pl.loop(0, 3)
        def _(j):
            z_ref[:, tile_at(j)] = dot(normed[RIM:], zx_w[s, :, tile_at(j)])

        scores[...] = dot_last(c_rows, b_rows)

        def heads_of(half):
            span = (half + 1) * 128
            rows = slice(half * 128, span)
            t = lax.broadcasted_iota(jnp.int32, (128, span), 0) + half * 128
            causal = t >= lax.broadcasted_iota(jnp.int32, (128, span), 1)
            for pair in range(HEADS_DEV // 2):
                parts = []
                for h in (2 * pair, 2 * pair + 1):
                    gap = la_ref[rows, h : h + 1] - la_t_ref[h : h + 1, :span]
                    mixing = scores[rows, :span] * jnp.exp(jnp.where(causal, gap, -1e30))
                    cols = slice(h * HEAD_DIM, (h + 1) * HEAD_DIM)
                    parts.append(dot(mixing.astype(BF), xd_ref[:span, cols]))
                y_ref[rows, pair * 128 : pair * 128 + 128] = jnp.concatenate(parts, axis=1)

        heads_of(0)
        finish(copies)
        chain_scan(True, chain_in.at[s], chain_back.at[s])
        copies = spread_send(chain_back.at[s], chain_got.at[s], me, c_sems[2].at[s], c_sems[3].at[s])
        heads_of(1)
        finish(copies)
        chain_unload(chain_got.at[s], k["state"])

        @pl.loop(0, BLOCKS)
        def _(i):
            at = rows_at(i)
            y = y_ref[at] + spread(jnp.exp(la_ref[at])) * dot(bc_act[at, STATE:], k["state"][...])
            y_ref[at] = y
            ssd = y + small[S_SKIP : S_SKIP + 1, :INNER_DEV] * x_act[at]
            gated = ssd * silu(z_ref[at])
            sq[at] = jnp.broadcast_to(jnp.sum(gated * gated, axis=-1, keepdims=True), (STEP, 128))
            low[at] = (gated * small[S_GATE : S_GATE + 1, :INNER_DEV]).astype(BF)

        square_out[s] = sq[...].T[0:8]
        arrive(s, 3)
        if s:
            for move in store_theirs(core, (bc_w, zx_w, out_w), (bc_t, zx_t, out_t), t_sem):
                move.start()

        @pl.loop(0, 6)
        def _(j):
            part[s, :, tile_at(j)] = dot(low[...], out_w[s, :, tile_at(j)]).astype(BF)

        copies = []
        for d in range(1, 4):
            src = part.at[s, :, quarter(shifted(place, d, 4))]
            copies.append(send(src, sum_in.at[s, d], s_sems[0].at[s, d], s_sems[1].at[s, d], heads[d - 1]))
        for d in range(1, 4):
            copies.append(
                send(square_out.at[s], square_in.at[s, d], s_sems[0].at[s, d + 4], s_sems[1].at[s, d + 4], heads[d - 1])
            )
        finish(copies)
        square = square_out[s]
        for d in range(1, 4):
            square = square + square_in[s, d]
        column = lax.rsqrt(square * (1.0 / INNER) + EPS).T[:, 0:1]
        k["scale"][...] = jnp.broadcast_to(column, (ROWS, 128))

        @pl.loop(0, BLOCKS)
        def _(i):
            at = rows_at(i)
            total = part[s, at, quarter(place)].astype(F32)
            for d in range(1, 4):
                total = total + sum_in[s, d, at].astype(F32)
            total = (total * k["scale"][at][:, 0:1]).astype(BF)
            sum_own[s, at] = total
            k["out"][at, quarter(place)] = total

        copies = []
        for d in range(1, 4):
            copies.append(
                send(sum_own.at[s], k["out"].at[:, quarter(place)], s_sems[2].at[s, d], s_sems[3].at[s, d], heads[d - 1])
            )
        if s == 0:
            edge = slice(ROWS - RIM, ROWS)
            next_own[...] = (
                v_buf[edge, quarter(place)].astype(F32) + sum_own[0, edge].astype(F32)
            ).astype(BF)
            rim_in = []
            for d in range(4):
                dst = rim_buf.at[1, :, quarter(place)]
                target = {"head": shifted(place, d, 4), "seq": later}
                rim_in.append(send(next_own, dst, rim_send.at[1 + d], rim_recv.at[1 + d], target))
        finish(copies)

        @pl.loop(0, BLOCKS)
        def _(i):
            at = rows_at(i)
            k["following"][at] = (entering[at].astype(F32) + k["out"][at].astype(F32)).astype(BF)

        entering = k["following"]

    for copy in across:
        copy.wait_send()
    for move in store_theirs(core, (bc_w, zx_w, out_w), (bc_t, zx_t, out_t), t_sem):
        move.wait()


def store_theirs(core, held, dst, sem):
    return [
        pltpu.make_async_copy(held[i].at[1 - core], dst[i], sem.at[i]) for i in range(3)
    ]


def forward(x_in, zx_m, bc_m, out_m, dt_m, smalls, number):
    dma = pltpu.SemaphoreType.DMA
    sds = jax.ShapeDtypeStruct
    vm = pltpu.VMEM
    got = pl.pallas_call(
        forward_kernel,
        out_shape=[sds(shape, kind) for _, shape, kind in KEPT * 2]
        + [sds(zx_m.shape, BF), sds(bc_m.shape, BF), sds(out_m.shape, BF)]
        + [sds((2, 16, WIDTH), F32), sds((2, 128, WIDTH), BF)],
        in_specs=[ANY] * 4 + [VM] * 8,
        out_specs=[VM] * 32 + [ANY] * 3 + [VM] * 2,
        scratch_shapes=[
            vm((ROWS, WIDTH), BF),
            vm((2, RIM, WIDTH), BF),
            vm((2, WIDTH, WIDTH), BF),
            vm((2, WIDTH, 256), BF),
            vm((2, INNER_DEV, WIDTH), BF),
            vm((ROWS, INNER_DEV), BF),
            vm((ROWS, ROWS), F32),
            vm((ROWS, 128), F32),
            vm((ROWS, 128), F32),
            vm((ROWS, INNER_DEV), BF),
            vm((ROWS, 128), F32),
            vm((2, ROWS, WIDTH), BF),
            vm((2, 16, 16, 512), BF),
            vm((2, 16, 16, 512), BF),
            vm((2, 16, 16, 384), BF),
            vm((2, 16, 16, 384), BF),
            vm((2, 4, ROWS, 384), BF),
            vm((2, 8, ROWS), F32),
            vm((2, 4, 8, ROWS), F32),
            vm((2, ROWS, 384), BF),
            vm((RIM, 384), BF),
            dma((6,)),
            dma((6,)),
            dma((4,)),
            dma((5,)),
            dma((5,)),
            dma((2, 16)),
            dma((2, 16)),
            dma((2, 16)),
            dma((2, 16)),
            dma((2, 8)),
            dma((2, 8)),
            dma((2, 4)),
            dma((2, 4)),
            dma((3,)),
            dma,
        ],
        compiler_params=comm_params(number),
        name="forward_layers",
    )(x_in, zx_m, bc_m, out_m, dt_m, *smalls)
    kept = [{name: got[16 * s + i] for i, (name, _, _) in enumerate(KEPT)} for s in range(2)]
    return kept, got[32:37]


PART = 48
EARLY, WIDE = 2 * PART, 3 * PART
SUB = WIDE + 32
GROUPS = ((0, EARLY), (EARLY, WIDE), (WIDE, SUB))
SLOT = ("z", "x_pre", "bc_pre", "dt_pre", "la", "la_t", "xd", "bc_act", "x_act", "y", "decay", "state", "scale", "out")
SHAPES = {name: (shape, kind) for name, shape, kind in KEPT}


def add_rows(total, more):
    return total.astype(F32) + more.astype(F32)


def backward_kernel(*refs):
    cot_ref, x_ref, last_ref = refs[:3]
    held = (refs[3:6], refs[6:9])
    small_all, dt_all = refs[9:11]
    saved = [{name: refs[11 + 16 * s + i] for i, (name, _, _) in enumerate(KEPT)} for s in range(2)]
    grads_ref, section_ref, leaving_ref = refs[43:46]
    rest = list(refs[46:])

    def take(count):
        got = rest[:count]
        del rest[:count]
        return got

    k = dict(zip(SLOT, take(len(SLOT))))
    normed_all, v_all, d_v, g_o_buf = take(4)
    zx_w, bc_w, out_w = take(3)
    own, spare, theirs, first, mid, second, ring = take(7)
    d_y_ref, d_z_ref, d_xd, d_y_low, wide_x, wide_y = take(6)
    scores_t, d_scores_t, d_bc, terms, direct, tail_ref, dt_ref = take(7)
    ext, d_zx, d_bd, part, sum_in, d_normed_ref, sum_own = take(7)
    chain_out, chain_in, chain_back, chain_got, state_grad = take(5)
    rim_buf, taps_ref, taps_in, taps_all, norm_ref, sums_ref, small_rows, head_in = take(8)
    k_sem, n_sem, w_sem, move_sem = take(4)
    c_sems, s_sems, rim_sems, swap_sems = take(4), take(4), take(2), take(2)
    cross_sems, one_sems, two_sems, head_sems, back_sems, last_sems = (
        take(2), take(2), take(2), take(2), take(2), take(2)
    )
    theirs_free, first_free = take(2)

    core, me, place = lax.axis_index("section"), lax.axis_index("seq"), lax.axis_index("head")
    x, z = lax.div(me, 4), lax.rem(me, 4)
    a = x + core * (z - x)
    b = z + core * (x - z)

    def at_place(i, j):
        return i * (4 - 3 * core) + j * (1 + 3 * core)

    other = {"section": 1 - core}
    heads = [{"head": shifted(place, d, 4)} for d in range(1, 4)]
    near = [{"seq": at_place(a, shifted(b, d, 4))} for d in range(1, 4)]
    far = [{"seq": at_place(shifted(a, d, 4), b)} for d in range(1, 4)]
    targets = [other] + [{"seq": shifted(me, d, 16)} for d in range(1, 16)] + heads
    targets += [{"section": 1 - core, "seq": at_place(shifted(a, d, 4), b)} for d in range(1, 4)]
    barrier = pltpu.get_barrier_semaphore()
    for target in targets:
        pl.semaphore_signal(barrier, inc=1, device_id=target, device_id_type=MESH)

    def load_kept(s):
        return [
            pltpu.make_async_copy(saved[s][name], k[name], k_sem.at[i]) for i, name in enumerate(SLOT)
        ]

    def load_rows(s):
        source = x_ref.at[core] if s == 0 else saved[0]["following"]
        return [
            pltpu.make_async_copy(saved[s]["normed"], normed_all.at[s], n_sem.at[s, 0]),
            pltpu.make_async_copy(source, v_all.at[s], n_sem.at[s, 1]),
        ]

    weight_slots = (zx_w, bc_w, out_w)

    def load_weight(s, i):
        @pl.when(core == s)
        def _():
            pltpu.make_async_copy(held[0][i], weight_slots[i], w_sem.at[i]).start()

        @pl.when(core != s)
        def _():
            pltpu.make_async_copy(held[1][i], weight_slots[i], w_sem.at[i]).start()

    def wait_weight(i):
        pltpu.make_async_copy(held[0][i], weight_slots[i], w_sem.at[i]).wait()

    load_g_o = pltpu.make_async_copy(cot_ref.at[core], g_o_buf, n_sem.at[0, 2])
    load_g_o.start()
    load_weight(1, 2)
    for move in load_kept(1):
        move.start()
    load_weight(1, 0)
    load_weight(1, 1)
    for s in (1, 0):
        for move in load_rows(s):
            move.start()

    @pl.loop(0, 4)
    def _(i):
        @pl.loop(0, 4)
        def _(j):
            blank = jnp.zeros((16, INNER_DEV), BF)
            own[0, i, j, WIDE + 16 :] = blank
            own[1, i, j, WIDE + 16 :] = blank
            spare[i, j, WIDE + 16 :] = blank

    small_rows[...] = jnp.zeros_like(small_rows)
    pl.semaphore_wait(barrier, len(targets))

    def swapped(i, src, dst):
        return pltpu.make_async_remote_copy(
            src_ref=src,
            dst_ref=dst.at[core],
            send_sem=swap_sems[0].at[i],
            recv_sem=swap_sems[1].at[i],
            device_id=other,
            device_id_type=MESH,
        )

    @pl.when(core == 0)
    def _():
        swapped(0, last_ref, section_ref).start()

    @pl.when(core == 1)
    def _():
        swapped(0, saved[0]["following"], section_ref).start()

    def cross(s, piece):
        lo, hi = GROUPS[piece]
        return pltpu.make_async_remote_copy(
            src_ref=spare.at[:, :, lo:hi],
            dst_ref=theirs.at[:, :, lo:hi],
            send_sem=cross_sems[0].at[s, piece],
            recv_sem=cross_sems[1].at[s, piece],
            device_id=other,
            device_id_type=MESH,
        )

    def reduction(s, group):
        lo, hi = GROUPS[group]
        cross(s, group).wait_recv()

        @pl.loop(0, 4)
        def _(i):
            @pl.loop(0, 4)
            def _(j):
                own[s, i, j, lo:hi] = add_rows(own[s, i, j, lo:hi], theirs[i, j, lo:hi]).astype(BF)

        if s == 0 and group < 2:
            pl.semaphore_wait(first_free.at[group], 3)
        copies = []
        for d in range(1, 4):
            src = own.at[s, :, shifted(b, d, 4), lo:hi]
            dst = first.at[d - 1, :, lo:hi]
            copies.append(
                send(src, dst, one_sems[0].at[s, group, d], one_sems[1].at[s, group, d], near[d - 1])
            )
        yield
        finish(copies)

        @pl.loop(0, 4)
        def _(i):
            total = own[s, i, b, lo:hi].astype(F32)
            for d in range(3):
                total = total + first[d, i, lo:hi].astype(F32)
            mid[i, lo:hi] = total.astype(BF)

        copies = []
        for d in range(1, 4):
            src = mid.at[shifted(a, d, 4), lo:hi]
            dst = second.at[s, d - 1, lo:hi]
            copies.append(
                send(src, dst, two_sems[0].at[s, group, d], two_sems[1].at[s, group, d], far[d - 1])
            )
        yield
        finish(copies)
        total = mid[a, lo:hi].astype(F32)
        for d in range(3):
            total = total + second[s, d, lo:hi].astype(F32)
        ring[s, a, lo:hi] = total.astype(BF)
        if group == 2:
            copies = []
            for d in range(1, 4):
                src = ring.at[s, a, WIDE : WIDE + 16]
                copies.append(
                    send(src, head_in.at[s, d - 1], head_sems[0].at[s, d], head_sems[1].at[s, d], heads[d - 1])
                )
            yield
            finish(copies)
            total = ring[s, a, WIDE : WIDE + 16].astype(F32)
            for d in range(3):
                total = total + head_in[s, d].astype(F32)
            ring[s, a, WIDE : WIDE + 16] = total.astype(BF)
        copies = []
        for d in range(1, 4):
            block = ring.at[s, a, lo:hi]
            copies.append(
                send(block, block, back_sems[0].at[s, group, d], back_sems[1].at[s, group, d], far[d - 1])
            )
        yield
        finish(copies)
        src = ring.at[s, :, lo:hi]

        def last(d, half, spot):
            return pltpu.make_async_remote_copy(
                src_ref=src,
                dst_ref=grads_ref.at[half, :, spot, lo:hi],
                send_sem=last_sems[0].at[s, group, d],
                recv_sem=last_sems[1].at[s, group, half, d],
                device_id={"section": s, "seq": at_place(a, shifted(b, d, 4))},
                device_id_type=MESH,
            )

        stay = pltpu.make_async_copy(src, grads_ref.at[core, :, b, lo:hi], last_sems[0].at[s, group, 0])
        for d in range(1, 4):
            last(d, core, b).start()

        @pl.when(core == s)
        def _():
            stay.start()

        @pl.when(core != s)
        def _():
            last(0, core, b).start()

        yield
        for d in range(1, 4):
            last(d, core, b).wait_send()

        @pl.when(core == s)
        def _():
            stay.wait()
            for d in range(1, 4):
                last(d, s, b).wait_recv()
            for d in range(4):
                last(d, 1 - s, b).wait_recv()

        @pl.when(core != s)
        def _():
            last(0, core, b).wait_send()

        yield

    member_rows = lax.broadcasted_iota(jnp.int32, (INNER_DEV, 128), 0)
    member_lanes = lax.broadcasted_iota(jnp.int32, (INNER_DEV, 128), 1) * HEAD_DIM
    inside = (member_rows >= member_lanes) & (member_rows < member_lanes + HEAD_DIM)
    member = jnp.where(inside, 1.0, 0.0).astype(BF)

    def sums_of(value):
        high, low = two_part(value)
        return dot(high, member) + dot(low, member)

    half_rows = [
        [pl.ds(pl.multiple_of(h * INNER_DEV + 384 * j, 384), 384) for j in range(2)] for h in (core, 1 - core)
    ]
    half_cols = [pl.ds(pl.multiple_of(h * INNER_DEV, INNER_DEV), INNER_DEV) for h in (core, 1 - core)]
    early, late, loose = None, None, None
    load_g_o.wait()
    for s in (1, 0):
        small = small_all.at[s]
        normed, v_ref = normed_all.at[s], v_all.at[s]
        g_o_ref = g_o_buf if s else d_v.at[1]
        y_ref, z_ref, la_ref, la_t_ref = k["y"], k["z"], k["la"], k["la_t"]
        xd_ref, bc_act, x_act = k["xd"], k["bc_act"], k["x_act"]
        x_pre, bc_pre = k["x_pre"], k["bc_pre"]
        stages = (own.at[s], spare)

        sums_ref[...] = jnp.zeros_like(sums_ref)
        wait_weight(2)

        @pl.loop(0, 3)
        def _(j):
            d_xd[:, tile_at(j)] = dot_last(g_o_ref[...], out_w[tile_at(j), :])

        if s:
            load_weight(0, 2)
        finish(load_kept(s))
        if s:
            finish(load_rows(1))

        @pl.loop(0, BLOCKS)
        def _(i):
            at = rows_at(i)
            gain = small[S_GATE : S_GATE + 1, :INNER_DEV]
            scale = k["scale"][at][:, 0:1]
            act, gate, dm = x_act[at], z_ref[at], d_xd[at]
            ssd = y_ref[at] + small[S_SKIP : S_SKIP + 1, :INNER_DEV] * act
            sigma = jax.nn.sigmoid(gate)
            gate_silu = gate * sigma
            gated = ssd * gate_silu
            scaled = gated * scale
            mean = jnp.sum(g_o_ref[at].astype(F32) * k["out"][at].astype(F32), axis=-1, keepdims=True)
            mean = mean * scale * scale * (1.0 / INNER)
            wide_x[at] = (scaled * gain).astype(BF)
            d_gated = scale * gain * dm - gated * mean
            d_y = d_gated * gate_silu
            d_y_ref[at] = d_y
            d_y_low[at] = d_y.astype(BF)
            d_z_ref[at] = (d_gated * ssd * sigma * (1.0 + gate * (1.0 - sigma))).astype(BF)
            wide_y[at] = (spread(jnp.exp(la_ref[at])) * d_y).astype(BF)
            sums_ref[0:1] += jnp.sum(scaled * dm, axis=0, keepdims=True)
            sums_ref[1:2] += jnp.sum(d_y * act, axis=0, keepdims=True)

        b_rows, c_rows = bc_act[:, :STATE], bc_act[:, STATE:]
        chain_load(dot_first(c_rows, wide_y[...]), k["decay"], chain_out)
        copies = spread_send(chain_out, chain_in, me, c_sems[0].at[s], c_sems[1].at[s])

        if s == 0:
            for piece in range(3):
                cross(1, piece).wait_send()
        for stage, cols, rows in zip(stages, half_cols, half_rows):
            for j in range(2):
                got = dot_first(wide_x[:, 384 * j : 384 * j + 384], g_o_ref[:, cols]).astype(BF)
                for i in range(8):
                    sub = 8 * j + i
                    stage[sub // 4, sub % 4, 0:PART] = got[PART * i : PART * i + PART]
            for j in range(2):
                got = dot_first(normed[RIM:, rows[j]], d_z_ref[...]).astype(BF)
                for i in range(8):
                    sub = 8 * j + i
                    stage[sub // 4, sub % 4, PART:EARLY] = got[PART * i : PART * i + PART]
        if s == 0:
            next(loose)
            pl.semaphore_signal(theirs_free, inc=1, device_id=other, device_id_type=MESH)
            pl.semaphore_wait(theirs_free, 1)
        cross(s, 0).start()
        if s == 0:
            next(late)
            next(loose)
            for target in near:
                pl.semaphore_signal(first_free.at[1], inc=1, device_id=target, device_id_type=MESH)

        la = la_ref[...]
        tail_ref[...] = jnp.exp(la[ROWS - 1 : ROWS] - la)
        dt_in = k["dt_pre"][...] + small[S_BIAS : S_BIAS + 1, :128]
        dt_ref[...] = softplus(dt_in)
        scores_t[...] = dot_last(b_rows, c_rows)

        def heads_of(half):
            base = half * 128
            rows = slice(base, base + 128)
            t = lax.broadcasted_iota(jnp.int32, (128, ROWS - base), 1)
            later = t >= lax.broadcasted_iota(jnp.int32, (128, ROWS - base), 0)
            total = jnp.zeros((128, ROWS - base), F32)
            for pair in range(HEADS_DEV // 2):
                parts = []
                for h in (2 * pair, 2 * pair + 1):
                    cols = slice(h * HEAD_DIM, (h + 1) * HEAD_DIM)
                    gap = la_t_ref[h : h + 1, base:] - la_ref[rows, h : h + 1]
                    decay = jnp.exp(jnp.where(later, gap, -1e30))
                    total = total + decay * dot_last(xd_ref[rows, cols], d_y_low[base:, cols])
                    mixing = (scores_t[rows, base:] * decay).astype(BF)
                    parts.append(dot(mixing, d_y_low[base:, cols]))
                d_xd[rows, pair * 128 : pair * 128 + 128] = jnp.concatenate(parts, axis=1)
            if half:
                d_scores_t[rows, 0:128] = jnp.zeros((128, 128), BF)
            d_scores_t[rows, base:] = total.astype(BF)

        heads_of(0)
        finish(copies)
        chain_scan(False, chain_in, chain_back)
        copies = spread_send(chain_back, chain_got, me, c_sems[2].at[s], c_sems[3].at[s])
        if s == 0:
            next(early)
            old_early = early
        early = reduction(s, 0)
        next(early)
        heads_of(1)
        if s == 0:
            next(late)
            next(loose)
        finish(copies)
        chain_unload(chain_got, state_grad)
        norm_ref[...] = jnp.zeros_like(norm_ref)
        taps_ref[...] = jnp.zeros_like(taps_ref)

        @pl.loop(0, BLOCKS)
        def _(i):
            at = rows_at(i)
            tail = spread(tail_ref[at])
            xd = xd_ref[at].astype(F32)
            wide_x[at] = (tail * xd).astype(BF)
            state_part = tail * dot(bc_act[at, :STATE], state_grad[...])
            got = d_xd[at] + state_part
            d_xd[at] = got
            norm_ref[1:2, :INNER_DEV] += jnp.sum(xd * state_part, axis=0, keepdims=True)
            terms[at] = sums_of(d_y_low[at].astype(F32) * y_ref[at] - xd * got)
            direct[at] = sums_of(x_act[at] * got)

        d_bc[:, :STATE] = dot(d_scores_t[...], c_rows) + dot_last(wide_x[...], state_grad[...])
        d_bc[:, STATE:] = dot_first(d_scores_t[...], b_rows) + dot_last(wide_y[...], k["state"][...])
        end_wide = spread(jnp.exp(la[ROWS - 8 : ROWS]))[7:8]
        both = state_grad[...].astype(F32) * k["state"][...].astype(F32)
        tail_sum = norm_ref[1:2, :INNER_DEV] + end_wide * jnp.sum(both, axis=0, keepdims=True)
        tail_sum = sums_of(jnp.broadcast_to(tail_sum, (16, INNER_DEV)))[0:1]
        d_log = running(terms[...], True) + tail_sum
        rate = small[S_RATE : S_RATE + 1, :128]
        d_dt = direct[...] + rate * d_log
        d_dt_pre = d_dt * jax.nn.sigmoid(dt_in)
        d_bd[:, 256:] = d_dt_pre.astype(BF)
        sums_ref[2:3, :128] = jnp.sum(dt_ref[...] * d_log, axis=0, keepdims=True) * rate
        sums_ref[3:4, :128] = jnp.sum(d_dt_pre, axis=0, keepdims=True)

        @pl.loop(0, BLOCKS)
        def _(i):
            at = rows_at(i)
            taps = small[S_CONV : S_CONV + 4]
            pre = x_pre[rows_at(i, RIM)]
            d_x = spread(dt_ref[at]) * d_xd[at] + small[S_SKIP : S_SKIP + 1, :INNER_DEV] * d_y_ref[at]
            d_xc = d_x * silu_slope(conv_rows(pre, taps[:, :INNER_DEV]))
            ext[at, :INNER_DEV] = d_xc
            for t in range(4):
                moved = pre[RIM - 3 + t : RIM - 3 + t + STEP]
                taps_ref[t : t + 1, :INNER_DEV] += jnp.sum(moved * d_xc, axis=0, keepdims=True)
            pre = bc_pre[rows_at(i, RIM)]
            d_bcc = d_bc[at] * silu_slope(conv_rows(pre, taps[:, INNER_DEV : INNER_DEV + 256]))
            ext[at, INNER_DEV:] = d_bcc
            for t in range(4):
                moved = pre[RIM - 3 + t : RIM - 3 + t + STEP]
                taps_ref[t : t + 1, INNER_DEV:] += jnp.sum(moved * d_bcc, axis=0, keepdims=True)

        rim = send(
            ext.at[0:8], rim_buf, rim_sems[0].at[s], rim_sems[1].at[s], {"seq": shifted(me, -1, 16)}
        )
        if s:
            for move in load_kept(0):
                move.start()
        taps_all[...] = taps_ref[:, INNER_DEV:]

        if s == 0:
            next(loose)
            next(late)
        rim.wait()

        @pl.when(me == 15)
        def _():
            rim_buf[...] = jnp.zeros_like(rim_buf)

        ext[ROWS : ROWS + 8] = rim_buf[...]

        @pl.loop(0, BLOCKS)
        def _(i):
            at = rows_at(i)
            taps = small[S_CONV : S_CONV + 4]
            block = ext[rows_at(i, 8)]
            d_pre = taps[0:1, : INNER_DEV + 256] * block[3 : 3 + STEP]
            for t in range(1, 4):
                d_pre = d_pre + taps[t : t + 1, : INNER_DEV + 256] * block[3 - t : 3 - t + STEP]
            d_zx[at, :INNER_DEV] = d_z_ref[at]
            d_zx[at, INNER_DEV:] = d_pre[:, :INNER_DEV].astype(BF)
            d_bd[at, :256] = d_pre[:, INNER_DEV:].astype(BF)

        wait_weight(0)
        wait_weight(1)

        @pl.loop(0, 6)
        def _(j):
            got = dot_last(d_zx[...], zx_w[tile_at(j), :])
            got = got + dot_last(d_bd[:, :256], bc_w[tile_at(j), :])
            got = got + dot(d_bd[:, 256:], dt_all[s, :, tile_at(j)])
            part[:, tile_at(j)] = got.astype(BF)

        if s:
            load_weight(0, 0)
            load_weight(0, 1)
        copies = []
        for d in range(1, 4):
            src = part.at[:, quarter(shifted(place, d, 4))]
            copies.append(send(src, sum_in.at[d - 1], s_sems[0].at[s, d], s_sems[1].at[s, d], heads[d - 1]))
        for d in range(1, 4):
            copies.append(
                send(taps_all, taps_in.at[d - 1], s_sems[0].at[s, d + 4], s_sems[1].at[s, d + 4], heads[d - 1])
            )
        for stage, rows in zip(stages, half_rows):
            for j in range(2):
                got = dot_first(normed[RIM:, rows[j]], d_zx[:, INNER_DEV:]).astype(BF)
                for i in range(8):
                    sub = 8 * j + i
                    stage[sub // 4, sub % 4, EARLY:WIDE] = got[PART * i : PART * i + PART]

        cross(s, 1).start()
        for stage, cols in zip(stages, half_cols):
            got = dot_first(d_bd[...], normed[RIM:, cols])
            for i in range(16):
                stage[i // 4, i % 4, WIDE : WIDE + 16] = got[16 * i : 16 * i + 16].astype(BF)
            stage[0, 0, WIDE + 16 :] = got[256:272].astype(BF)
        next(early)
        if s:
            for target in near:
                pl.semaphore_signal(first_free.at[0], inc=1, device_id=target, device_id_type=MESH)
        else:
            next(loose)
        finish(copies)
        total = taps_all[...]
        for d in range(3):
            total = total + taps_in[d]
        taps_ref[:, INNER_DEV:] = total

        @pl.loop(0, BLOCKS)
        def _(i):
            at = rows_at(i)
            total = part[at, quarter(place)].astype(F32)
            for d in range(3):
                total = total + sum_in[d, at].astype(F32)
            total = total.astype(BF)
            sum_own[at] = total
            d_normed_ref[at, quarter(place)] = total

        copies = []
        for d in range(1, 4):
            dst = d_normed_ref.at[:, quarter(place)]
            copies.append(send(sum_own, dst, s_sems[2].at[s, d], s_sems[3].at[s, d], heads[d - 1]))
        old_loose, old_late = loose, late
        late = reduction(s, 1)
        next(late)
        next(early)
        finish(copies)
        norm_ref[...] = jnp.zeros_like(norm_ref)

        @pl.loop(0, BLOCKS)
        def _(i):
            at = rows_at(i)
            v = v_ref[at].astype(F32)
            scale = lax.rsqrt(jnp.mean(v * v, axis=-1, keepdims=True) + EPS)
            d_normed = d_normed_ref[at].astype(F32)
            scaled = v * scale
            norm_ref[0:1] += jnp.sum(scaled * d_normed, axis=0, keepdims=True)
            weighted = d_normed * small[S_NORM : S_NORM + 1]
            mean = jnp.mean(v * weighted, axis=-1, keepdims=True) * scale * scale
            d_v[s, at] = (scale * weighted - scaled * mean + g_o_ref[at].astype(F32)).astype(BF)

        for h in range(2):
            small_rows[h, 0:1] = norm_ref[0:1, h * INNER_DEV : (h + 1) * INNER_DEV]
            small_rows[h, 1:5] = taps_ref[0:4, :INNER_DEV]
            small_rows[h, 5:9] = sums_ref[0:4]
            small_rows[h, 9:13, 0:256] = taps_ref[0:4, INNER_DEV:]
        for stage, h in zip(stages, (core, 1 - core)):
            stage[0, 1, WIDE + 16 :] = small_rows[h].astype(BF)
        cross(s, 2).start()
        loose = reduction(s, 2)

        @pl.when(core == 1 - s)
        def _():
            swapped(1, d_v.at[s], leaving_ref).start()

        @pl.when(core == s)
        def _():
            pltpu.make_async_copy(d_v.at[s], leaving_ref.at[s], move_sem.at[1]).start()

        if s:

            @pl.when(core == 0)
            def _():
                pltpu.make_async_copy(v_all.at[1], section_ref.at[0], move_sem.at[0]).start()

            finish(load_rows(0))

            @pl.when(core == 1)
            def _():
                pltpu.make_async_copy(last_ref, g_o_buf, move_sem.at[0]).start()

    @pl.when(core == 1)
    def _():
        pltpu.make_async_copy(last_ref, g_o_buf, move_sem.at[0]).wait()
        pltpu.make_async_copy(g_o_buf, section_ref.at[1], move_sem.at[0]).start()

    order = (early, loose, late, loose, late, loose, loose, late, loose, early, late, loose)
    order += (old_early, old_late, old_loose)
    for turn in order:
        next(turn)
    for piece in range(3):
        cross(0, piece).wait_send()
    swapped(0, last_ref, section_ref).wait()
    swapped(1, d_v.at[0], leaving_ref).wait()
    pltpu.make_async_copy(d_v.at[0], leaving_ref.at[0], move_sem.at[1]).wait()
    pltpu.make_async_copy(d_v.at[0], section_ref.at[0], move_sem.at[0]).wait()


def backward(cotangent, x_in, last, held, smalls, dt_all, kept, number):
    dma = pltpu.SemaphoreType.DMA
    regular = pltpu.SemaphoreType.REGULAR
    sds = jax.ShapeDtypeStruct
    vm = pltpu.VMEM
    halves = (4, 4, SUB, INNER_DEV)
    rows_low = vm((ROWS, INNER_DEV), BF)
    rows_wide = vm((ROWS, INNER_DEV), F32)
    steps = vm((ROWS, 128), F32)
    scratch = [vm(*SHAPES[name]) for name in SLOT]
    scratch += [
        vm((2, ROWS + RIM, WIDTH), BF),
        vm((2, ROWS, WIDTH), BF),
        vm((2, ROWS, WIDTH), BF),
        vm((ROWS, WIDTH), BF),
        vm((WIDTH, WIDTH), BF),
        vm((WIDTH, 256), BF),
        vm((INNER_DEV, WIDTH), BF),
        vm((2,) + halves, BF),
        vm(halves, BF),
        vm(halves, BF),
        vm((3, 4, SUB, INNER_DEV), BF),
        vm((4, SUB, INNER_DEV), BF),
        vm((2, 3, SUB, INNER_DEV), BF),
        vm((2, 4, SUB, INNER_DEV), BF),
        rows_wide, rows_low, rows_wide, rows_low, rows_low, rows_low,
        vm((ROWS, ROWS), F32),
        vm((ROWS, ROWS), BF),
        vm((ROWS, 256), F32),
        steps, steps, steps, steps,
        vm((ROWS + 8, INNER_DEV + 256), F32),
        vm((ROWS, WIDTH), BF),
        vm((ROWS, 384), BF),
        vm((ROWS, WIDTH), BF),
        vm((3, ROWS, 384), BF),
        vm((ROWS, WIDTH), BF),
        vm((ROWS, 384), BF),
        vm((16, 16, 512), BF),
        vm((16, 16, 512), BF),
        vm((16, 16, 384), BF),
        vm((16, 16, 384), BF),
        vm((STATE, INNER_DEV), BF),
        vm((8, INNER_DEV + 256), F32),
        vm((8, INNER_DEV + 256), F32),
        vm((3, 8, 256), F32),
        vm((8, 256), F32),
        vm((8, WIDTH), F32),
        vm((8, INNER_DEV), F32),
        vm((2, 16, INNER_DEV), F32),
        vm((2, 3, 16, INNER_DEV), BF),
        dma((len(SLOT),)),
        dma((2, 3)),
        dma((3,)),
        dma((2,)),
    ]
    scratch += [dma((2, 16))] * 4 + [dma((2, 8))] * 2 + [dma((2, 4))] * 2
    scratch += [dma((2,))] * 4 + [dma((2, 3))] * 2
    scratch += [dma((2, 3, 4))] * 4 + [dma((2, 4))] * 2 + [dma((2, 3, 4))] * 2
    scratch += [dma((2, 3, 4)), dma((2, 3, 2, 4)), regular, regular((2,))]
    flat = [kept[s][name] for s in range(2) for name, _, _ in KEPT]
    return pl.pallas_call(
        backward_kernel,
        out_shape=[sds((2,) + halves, BF), sds((2, ROWS, WIDTH), BF), sds((2, ROWS, WIDTH), BF)],
        in_specs=[ANY] * 9 + [VM] * 2 + [ANY] * 32,
        out_specs=[ANY] * 3,
        scratch_shapes=scratch,
        compiler_params=comm_params(number),
        name="backward_layers",
    )(cotangent, x_in, last, *held, smalls, dt_all, *flat)


def widen_kernel(
    a_ref, zx_ref, out_ref, bc_ref, dt_ref, norm_ref, bias_ref, rate_ref, skip_ref, conv_ref, conv_bc_ref, gate_ref,
    bc_all,
):
    step = pl.program_id(0)
    for h in range(2):
        cols = slice(h * INNER_DEV, (h + 1) * INNER_DEV)
        zx_ref[h, :, 0, :] = a_ref[h, 0, PART:EARLY].astype(F32)
        zx_ref[h, :, 1, :] = a_ref[h, 0, EARLY:WIDE].astype(F32)
        out_ref[:, cols] = a_ref[h, 0, 0:PART].astype(F32)
        at = pl.ds(pl.multiple_of(step * 16, 16), 16)
        bc_all[at, cols] = a_ref[h, 0, WIDE : WIDE + 16].astype(F32)

    @pl.when(step == 0)
    def _():
        for h in range(2):
            cols = slice(h * INNER_DEV, (h + 1) * INNER_DEV)
            dt_ref[:, cols] = a_ref[h, 0, WIDE + 16 :].astype(F32)[0:HEADS_DEV]

    @pl.when(step == 1)
    def _():
        rows = a_ref[0, 0, WIDE + 16 :].astype(F32)
        norm_ref[:, :INNER_DEV] = rows[0:1]
        norm_ref[:, INNER_DEV:] = a_ref[1, 0, WIDE + 16 :].astype(F32)[0:1]
        conv_ref[...] = rows[1:5]
        gate_ref[...] = rows[5:6]
        heads = jnp.concatenate(
            [
                jnp.sum(rows[0:8, h * HEAD_DIM : (h + 1) * HEAD_DIM], axis=1, keepdims=True)
                for h in range(HEADS_DEV)
            ],
            axis=1,
        )
        skip_ref[...] = heads[6:7]
        rate_ref[...] = rows[7:8, 0:HEADS_DEV]
        bias_ref[...] = rows[8:9, 0:HEADS_DEV]
        conv_bc_ref[...] = rows[9:13, 0:256]

    @pl.when(step == 15)
    def _():
        bc_ref[...] = bc_all[...].T


def widen(total):
    total = total.reshape(2, 16, SUB, INNER_DEV)
    fixed = ((WIDTH, 256), (HEADS_DEV, WIDTH), (1, WIDTH)) + ((1, HEADS_DEV),) * 3
    fixed += ((4, INNER_DEV), (4, 256), (1, INNER_DEV))
    shapes = ((2, INNER_DEV, 2, INNER_DEV), (INNER_DEV, WIDTH)) + fixed
    return pl.pallas_call(
        widen_kernel,
        grid=(16,),
        out_shape=[jax.ShapeDtypeStruct(shape, F32) for shape in shapes],
        in_specs=[pl.BlockSpec((2, 1, SUB, INNER_DEV), lambda i: (0, i, 0, 0))],
        out_specs=[
            pl.BlockSpec((2, PART, 2, INNER_DEV), lambda i: (0, i, 0, 0)),
            pl.BlockSpec((PART, WIDTH), lambda i: (i, 0)),
        ]
        + [pl.BlockSpec(shape, lambda i: (0, 0)) for shape in fixed],
        scratch_shapes=[pltpu.VMEM((256, WIDTH), F32)],
        compiler_params=pltpu.CompilerParams(vmem_limit_bytes=VMEM_CAP),
        name="widen",
    )(total)


def on_device(
    x_in,
    norm_gain,
    w_zx,
    w_bc,
    w_dt,
    dt_bias,
    a_log,
    d_skip,
    conv_x,
    conv_bc,
    gate_gain,
    w_out,
    cotangent,
):
    zx_m = w_zx[0].reshape(WIDTH, WIDTH)
    bc_m, out_m, dt_m = w_bc[0], w_out[0], w_dt[0].T
    small_args = (norm_gain, gate_gain, conv_x[0], conv_bc[0], dt_bias, a_log, d_skip)
    kept, (zx_t, bc_t, out_t, smalls, dt_all) = forward(x_in, zx_m, bc_m, out_m, dt_m, small_args, 0)
    held = (zx_m, bc_m, out_m, zx_t, bc_t, out_t)
    total, section_out, grads_in = backward(
        cotangent, x_in, kept[1]["following"], held, smalls, dt_all, kept, 1
    )
    g_zx, g_out, g_bc, g_dt, g_norm, g_bias, g_rate, g_skip, g_conv_x, g_conv_bc, g_gate = widen(total)
    return (
        section_out[None],
        grads_in[None],
        g_norm,
        g_zx.reshape(1, WIDTH, 2, INNER_DEV),
        g_bc[None],
        g_dt.T[None],
        g_bias,
        g_rate,
        g_skip,
        g_conv_x[None],
        g_conv_bc[None],
        g_gate,
        g_out[None],
    )


def solution(mesh):
    in_specs = (
        P(None, "seq", None),
        P("section", None),
        P("section", None, None, "head"),
        P("section", None, None),
        P("section", None, "head"),
        P("section", "head"),
        P("section", "head"),
        P("section", "head"),
        P("section", None, "head"),
        P("section", None, None),
        P("section", "head"),
        P("section", "head", None),
        P(None, "seq", None),
    )
    out_specs = (
        P("section", None, "seq", None),
        P("section", None, "seq", None),
        P("section", None),
        P("section", None, None, "head"),
        P("section", None, None),
        P("section", None, "head"),
        P("section", "head"),
        P("section", "head"),
        P("section", "head"),
        P("section", None, "head"),
        P("section", None, None),
        P("section", "head"),
        P("section", "head", None),
    )
    return jax.shard_map(
        on_device, mesh=mesh, in_specs=in_specs, out_specs=out_specs, check_vma=False
    )
```

```python
import functools

import jax
import jax.numpy as jnp
from jax import lax
from jax.experimental import pallas as pl
from jax.experimental.pallas import tpu as pltpu
from jax.sharding import PartitionSpec as P

MESH = pl.DeviceIdType.MESH
F32 = jnp.float32
BF = jnp.bfloat16
EPS = 1e-05
INNER = 3072
ROWS = 256
WIDTH = 1536
INNER_DEV = 768
HEADS_DEV = 12
HEAD_DIM = 64
STATE = 128
RIM = 16
VMEM_CAP = 60 << 20
FIRST = (((0,), (0,)), ((), ()))
LAST = (((1,), (1,)), ((), ()))


def dot(a, b):
    return jnp.dot(a, b, preferred_element_type=F32)


def dot_first(a, b):
    return lax.dot_general(a, b, FIRST, preferred_element_type=F32)


def dot_last(a, b):
    return lax.dot_general(a, b, LAST, preferred_element_type=F32)


def two_part(a):
    high = a.astype(BF)
    return high, (a - high.astype(F32)).astype(BF)


def silu(a):
    return a * jax.nn.sigmoid(a)


def silu_slope(a):
    sigma = jax.nn.sigmoid(a)
    return sigma * (1.0 + a * (1.0 - sigma))


def spread(a):
    rows = a.shape[0]
    low_half = lax.broadcasted_iota(jnp.int32, (rows, 128), 1) < HEAD_DIM
    return jnp.concatenate(
        [
            jnp.where(low_half, a[:, 2 * j : 2 * j + 1], a[:, 2 * j + 1 : 2 * j + 2])
            for j in range(HEADS_DEV // 2)
        ],
        axis=1,
    )


def triangle(keep_after):
    t = lax.broadcasted_iota(jnp.int32, (ROWS, ROWS), 0)
    s = lax.broadcasted_iota(jnp.int32, (ROWS, ROWS), 1)
    return jnp.where((s >= t) if keep_after else (t >= s), 1.0, 0.0).astype(BF)


def running(a, keep_after):
    weights = triangle(keep_after)
    high, low = two_part(a)
    return dot(weights, high) + dot(weights, low)


S_NORM, S_GATE, S_CONV, S_BIAS, S_RATE, S_SKIP = 0, 1, 2, 6, 7, 9
STEP = 32
BLOCKS = ROWS // STEP


def softplus(a):
    return jnp.maximum(a, 0.0) + jnp.log1p(jnp.exp(-jnp.abs(a)))


def rows_at(i, more=0):
    return pl.ds(pl.multiple_of(i * STEP, STEP), STEP + more)


def tile_at(i, width=256, base=0):
    return pl.ds(pl.multiple_of(base + i * width, width), width)


def conv_rows(pre, taps):
    total = taps[0:1] * pre[RIM - 3 : RIM - 3 + STEP]
    for k in range(1, 4):
        total = total + taps[k : k + 1] * pre[RIM - 3 + k : RIM - 3 + k + STEP]
    return total


def shifted(place, distance, count):
    return lax.rem(place + distance + count, count)


def meet(targets):
    barrier = pltpu.get_barrier_semaphore()
    for target in targets:
        pl.semaphore_signal(barrier, inc=1, device_id=target, device_id_type=MESH)
    pl.semaphore_wait(barrier, len(targets))


def send(src, dst, send_sem, recv_sem, target):
    copy = pltpu.make_async_remote_copy(
        src_ref=src,
        dst_ref=dst,
        send_sem=send_sem,
        recv_sem=recv_sem,
        device_id=target,
        device_id_type=MESH,
    )
    copy.start()
    return copy


def comm_params(number):
    return pltpu.CompilerParams(
        collective_id=number, has_side_effects=True, vmem_limit_bytes=VMEM_CAP
    )


ANY = pl.BlockSpec(memory_space=pl.ANY)
VM = pl.BlockSpec(memory_space=pltpu.VMEM)


def quarter(place):
    return pl.ds(pl.multiple_of(place * 384, 384), 384)


KEPT = (
    ("normed", (ROWS + RIM, WIDTH), BF),
    ("z", (ROWS, INNER_DEV), F32),
    ("x_pre", (ROWS + RIM, INNER_DEV), F32),
    ("bc_pre", (ROWS + RIM, 256), F32),
    ("dt_pre", (ROWS, 128), F32),
    ("la", (ROWS, 128), F32),
    ("la_t", (128, ROWS), F32),
    ("xd", (ROWS, INNER_DEV), BF),
    ("bc_act", (ROWS, 256), BF),
    ("x_act", (ROWS, INNER_DEV), F32),
    ("y", (ROWS, INNER_DEV), F32),
    ("decay", (8, INNER_DEV), F32),
    ("state", (STATE, INNER_DEV), BF),
    ("scale", (ROWS, 128), F32),
    ("out", (ROWS, WIDTH), BF),
    ("following", (ROWS, WIDTH), BF),
)


def chain_load(own, decay, out_buf):
    for j in range(16):
        rows = own[8 * j : 8 * j + 8]
        out_buf[j, :, 0:384] = jnp.concatenate([rows[:, :384], rows[:, 384:]], axis=0).astype(BF)
    six = jnp.concatenate([decay[0:1, 128 * k : 128 * k + 128] for k in range(6)] * 3, axis=0)
    six = six[0:16].astype(BF)
    for j in range(16):
        out_buf[j, :, 384:512] = six


def chain_scan(forward, in_buf, back_buf):
    state = jnp.zeros((16, 384), F32)
    for step in range(16):
        i = step if forward else 15 - step
        back_buf[i] = state.astype(BF)
        part = in_buf[i].astype(F32)
        decay = jnp.concatenate(
            [
                jnp.concatenate(
                    [
                        jnp.broadcast_to(part[3 * half + k : 3 * half + k + 1, 384:512], (8, 128))
                        for k in range(3)
                    ],
                    axis=1,
                )
                for half in range(2)
            ],
            axis=0,
        )
        state = decay * state + part[:, 0:384]


def chain_unload(got_buf, state_ref):
    for j in range(8):
        first, second = got_buf[2 * j].astype(F32), got_buf[2 * j + 1].astype(F32)
        for half in range(2):
            rows = jnp.concatenate(
                [first[8 * half : 8 * half + 8], second[8 * half : 8 * half + 8]], axis=0
            )
            state_ref[16 * j : 16 * j + 16, 384 * half : 384 * half + 384] = rows.astype(BF)


def spread_send(src, dst, me, send_sem, recv_sem):
    copies = []
    for d in range(1, 16):
        to = shifted(me, d, 16)
        copies.append(send(src.at[to], dst.at[me], send_sem.at[d], recv_sem.at[d], {"seq": to}))
    dst[me] = src[me]
    return copies


def finish(copies):
    for copy in copies:
        copy.wait()


def norm_rows(v, gain):
    v = v.astype(F32)
    scale = lax.rsqrt(jnp.mean(v * v, axis=-1, keepdims=True) + EPS)
    return (v * scale * gain).astype(BF)


def forward_kernel(*refs):
    x_ref, zx_m, bc_m, out_m, dt_m = refs[:5]
    norm_gain, gate_gain, conv_x, conv_bc, dt_bias, a_log, d_skip = refs[5:12]
    kept = [{name: refs[12 + 16 * s + i] for i, (name, _, _) in enumerate(KEPT)} for s in range(2)]
    zx_t, bc_t, out_t, small_w, dt_w = refs[44:49]
    v_buf, rim_buf, zx_w, bc_w, out_w = refs[49:54]
    tail_x, scores, dt_buf, tail, low, sq, part = refs[54:61]
    chain_out, chain_in, chain_back, chain_got = refs[61:65]
    sum_in, square_out, square_in, sum_own, next_own = refs[65:70]
    w_send, w_recv, w_own, rim_send, rim_recv = refs[70:75]
    c_sems, s_sems, t_sem, v_sem = refs[75:79], refs[79:83], refs[83], refs[84]

    core, me, place = lax.axis_index("section"), lax.axis_index("seq"), lax.axis_index("head")
    other = {"section": 1 - core}
    later = shifted(me, 1, 16)
    barrier = pltpu.get_barrier_semaphore()
    targets = [other]
    targets += [{"seq": shifted(me, d, 16)} for d in range(1, 16)]
    heads = [{"head": shifted(place, d, 4)} for d in range(1, 4)]
    targets += heads
    targets += [{"head": shifted(place, d, 4), "seq": shifted(me, -1, 16)} for d in range(1, 4)]
    for target in targets:
        pl.semaphore_signal(barrier, inc=1, device_id=target, device_id_type=MESH)

    moves = [
        (bc_m, bc_w.at[core]),
        (zx_m.at[:, INNER_DEV:], zx_w.at[core, :, INNER_DEV:]),
        (zx_m.at[:, :INNER_DEV], zx_w.at[core, :, :INNER_DEV]),
        (out_m, out_w.at[core]),
    ]
    own_moves = [pltpu.make_async_copy(src, dst, w_own.at[i]) for i, (src, dst) in enumerate(moves)]
    for move in own_moves:
        move.start()
    load_v = pltpu.make_async_copy(x_ref.at[core], v_buf, v_sem)
    load_v.start()
    small_w[core] = jnp.zeros((16, WIDTH), F32)
    small_w[core, S_NORM : S_NORM + 1] = norm_gain[...]
    small_w[core, S_GATE : S_GATE + 1, :INNER_DEV] = gate_gain[...]
    small_w[core, S_CONV : S_CONV + 4, :INNER_DEV] = conv_x[...].astype(F32)
    small_w[core, S_CONV : S_CONV + 4, INNER_DEV : INNER_DEV + 256] = conv_bc[...].astype(F32)
    small_w[core, S_BIAS : S_BIAS + 1, 0:HEADS_DEV] = dt_bias[...]
    small_w[core, S_RATE : S_RATE + 1, 0:HEADS_DEV] = -jnp.exp(a_log[...])
    small_w[core, 8:9, 0:HEADS_DEV] = d_skip[...]
    skip_wide = spread(small_w[core, 8:16, 0:128])
    small_w[core, S_SKIP : S_SKIP + 1, :INNER_DEV] = skip_wide[0:1]
    dt_rows = jnp.concatenate([dt_m[...].astype(F32), jnp.zeros((4, WIDTH), F32)], axis=0)
    dt_w[core, 0:16] = dt_rows.astype(BF)
    for s in range(2):
        dt_w[s, 16:] = jnp.zeros((112, WIDTH), BF)
    pl.semaphore_wait(barrier, len(targets))
    rim_copy = send(x_ref.at[core, ROWS - RIM :], rim_buf.at[0], rim_send.at[0], rim_recv.at[0], {"seq": later})
    across = [
        send(small_w.at[core], small_w.at[core], w_send.at[4], w_recv.at[4], other),
        send(dt_w.at[core, 0:16], dt_w.at[core, 0:16], w_send.at[5], w_recv.at[5], other),
    ]
    for i, (src, dst) in enumerate(moves):
        across.append(send(src, dst, w_send.at[i], w_recv.at[i], other))

    def arrive(section, i):
        @pl.when(core == section)
        def _():
            own_moves[i].wait()

        @pl.when(core != section)
        def _():
            across[i + 2].wait_recv()

    load_v.wait()
    rim_copy.wait()

    @pl.when(me == 0)
    def _():
        rim_buf[0] = jnp.zeros((RIM, WIDTH), BF)

    across[0].wait_recv()
    across[1].wait_recv()
    entering = v_buf
    for s in range(2):
        k = kept[s]
        small = small_w.at[s]
        normed, z_ref, x_pre, bc_pre, la_ref, la_t_ref = (
            k["normed"], k["z"], k["x_pre"], k["bc_pre"], k["la"], k["la_t"]
        )
        xd_ref, bc_act, x_act, y_ref = k["xd"], k["bc_act"], k["x_act"], k["y"]
        gain = small[S_NORM : S_NORM + 1]
        if s:
            finish(rim_in)

            @pl.when(me == 0)
            def _():
                rim_buf[1] = jnp.zeros((RIM, WIDTH), BF)

        normed[0:RIM] = norm_rows(rim_buf[s], gain)

        @pl.loop(0, ROWS // 16)
        def _(i):
            at = pl.ds(pl.multiple_of(i * 16, 16), 16)
            normed[pl.ds(pl.multiple_of(i * 16 + RIM, 16), 16)] = norm_rows(entering[at], gain)

        arrive(s, 0)
        bc_pre[...] = dot(normed[...], bc_w[s])
        dt_raw = dot_last(normed[RIM:], dt_w[s])
        k["dt_pre"][...] = dt_raw
        arrive(s, 1)

        @pl.loop(0, 3)
        def _(j):
            x_pre[:, tile_at(j)] = dot(normed[...], zx_w[s, :, tile_at(j, 256, INNER_DEV)])

        dt = softplus(dt_raw + small[S_BIAS : S_BIAS + 1, :128])
        dt_buf[...] = dt
        la = running(dt * small[S_RATE : S_RATE + 1, :128], False)
        la_ref[...] = la
        la_t_ref[...] = la.T
        tail[...] = jnp.exp(la[ROWS - 1 : ROWS] - la)
        decay = jnp.broadcast_to(spread(jnp.exp(la[ROWS - 8 : ROWS]))[7:8], (8, INNER_DEV))
        k["decay"][...] = decay

        @pl.loop(0, BLOCKS)
        def _(i):
            taps = small[S_CONV : S_CONV + 4]
            act = silu(conv_rows(x_pre[rows_at(i, RIM)], taps[:, :INNER_DEV]))
            x_act[rows_at(i)] = act
            xd = (act * spread(dt_buf[rows_at(i)])).astype(BF)
            xd_ref[rows_at(i)] = xd
            tail_x[rows_at(i)] = (xd.astype(F32) * spread(tail[rows_at(i)])).astype(BF)
            bc = conv_rows(bc_pre[rows_at(i, RIM)], taps[:, INNER_DEV : INNER_DEV + 256])
            bc_act[rows_at(i)] = silu(bc).astype(BF)

        b_rows, c_rows = bc_act[:, :STATE], bc_act[:, STATE:]
        chain_load(dot_first(b_rows, tail_x[...]), decay, chain_out.at[s])
        copies = spread_send(chain_out.at[s], chain_in.at[s], me, c_sems[0].at[s], c_sems[1].at[s])
        arrive(s, 2)

        @pl.loop(0, 3)
        def _(j):
            z_ref[:, tile_at(j)] = dot(normed[RIM:], zx_w[s, :, tile_at(j)])

        scores[...] = dot_last(c_rows, b_rows)

        def heads_of(half):
            span = (half + 1) * 128
            rows = slice(half * 128, span)
            t = lax.broadcasted_iota(jnp.int32, (128, span), 0) + half * 128
            causal = t >= lax.broadcasted_iota(jnp.int32, (128, span), 1)
            for pair in range(HEADS_DEV // 2):
                parts = []
                for h in (2 * pair, 2 * pair + 1):
                    gap = la_ref[rows, h : h + 1] - la_t_ref[h : h + 1, :span]
                    mixing = scores[rows, :span] * jnp.exp(jnp.where(causal, gap, -1e30))
                    cols = slice(h * HEAD_DIM, (h + 1) * HEAD_DIM)
                    parts.append(dot(mixing.astype(BF), xd_ref[:span, cols]))
                y_ref[rows, pair * 128 : pair * 128 + 128] = jnp.concatenate(parts, axis=1)

        heads_of(0)
        finish(copies)
        chain_scan(True, chain_in.at[s], chain_back.at[s])
        copies = spread_send(chain_back.at[s], chain_got.at[s], me, c_sems[2].at[s], c_sems[3].at[s])
        heads_of(1)
        finish(copies)
        chain_unload(chain_got.at[s], k["state"])

        @pl.loop(0, BLOCKS)
        def _(i):
            at = rows_at(i)
            y = y_ref[at] + spread(jnp.exp(la_ref[at])) * dot(bc_act[at, STATE:], k["state"][...])
            y_ref[at] = y
            ssd = y + small[S_SKIP : S_SKIP + 1, :INNER_DEV] * x_act[at]
            gated = ssd * silu(z_ref[at])
            sq[at] = jnp.broadcast_to(jnp.sum(gated * gated, axis=-1, keepdims=True), (STEP, 128))
            low[at] = (gated * small[S_GATE : S_GATE + 1, :INNER_DEV]).astype(BF)

        square_out[s] = sq[...].T[0:8]
        arrive(s, 3)
        if s:
            for move in store_theirs(core, (bc_w, zx_w, out_w), (bc_t, zx_t, out_t), t_sem):
                move.start()

        @pl.loop(0, 6)
        def _(j):
            part[s, :, tile_at(j)] = dot(low[...], out_w[s, :, tile_at(j)]).astype(BF)

        copies = []
        for d in range(1, 4):
            src = part.at[s, :, quarter(shifted(place, d, 4))]
            copies.append(send(src, sum_in.at[s, d], s_sems[0].at[s, d], s_sems[1].at[s, d], heads[d - 1]))
        for d in range(1, 4):
            copies.append(
                send(square_out.at[s], square_in.at[s, d], s_sems[0].at[s, d + 4], s_sems[1].at[s, d + 4], heads[d - 1])
            )
        finish(copies)
        square = square_out[s]
        for d in range(1, 4):
            square = square + square_in[s, d]
        column = lax.rsqrt(square * (1.0 / INNER) + EPS).T[:, 0:1]
        k["scale"][...] = jnp.broadcast_to(column, (ROWS, 128))

        @pl.loop(0, BLOCKS)
        def _(i):
            at = rows_at(i)
            total = part[s, at, quarter(place)].astype(F32)
            for d in range(1, 4):
                total = total + sum_in[s, d, at].astype(F32)
            total = (total * k["scale"][at][:, 0:1]).astype(BF)
            sum_own[s, at] = total
            k["out"][at, quarter(place)] = total

        copies = []
        for d in range(1, 4):
            copies.append(
                send(sum_own.at[s], k["out"].at[:, quarter(place)], s_sems[2].at[s, d], s_sems[3].at[s, d], heads[d - 1])
            )
        if s == 0:
            edge = slice(ROWS - RIM, ROWS)
            next_own[...] = (
                v_buf[edge, quarter(place)].astype(F32) + sum_own[0, edge].astype(F32)
            ).astype(BF)
            rim_in = []
            for d in range(4):
                dst = rim_buf.at[1, :, quarter(place)]
                target = {"head": shifted(place, d, 4), "seq": later}
                rim_in.append(send(next_own, dst, rim_send.at[1 + d], rim_recv.at[1 + d], target))
        finish(copies)

        @pl.loop(0, BLOCKS)
        def _(i):
            at = rows_at(i)
            k["following"][at] = (entering[at].astype(F32) + k["out"][at].astype(F32)).astype(BF)

        entering = k["following"]

    for copy in across:
        copy.wait_send()
    for move in store_theirs(core, (bc_w, zx_w, out_w), (bc_t, zx_t, out_t), t_sem):
        move.wait()


def store_theirs(core, held, dst, sem):
    return [
        pltpu.make_async_copy(held[i].at[1 - core], dst[i], sem.at[i]) for i in range(3)
    ]


def forward(x_in, zx_m, bc_m, out_m, dt_m, smalls, number):
    dma = pltpu.SemaphoreType.DMA
    sds = jax.ShapeDtypeStruct
    vm = pltpu.VMEM
    got = pl.pallas_call(
        forward_kernel,
        out_shape=[sds(shape, kind) for _, shape, kind in KEPT * 2]
        + [sds(zx_m.shape, BF), sds(bc_m.shape, BF), sds(out_m.shape, BF)]
        + [sds((2, 16, WIDTH), F32), sds((2, 128, WIDTH), BF)],
        in_specs=[ANY] * 4 + [VM] * 8,
        out_specs=[VM] * 32 + [ANY] * 3 + [VM] * 2,
        scratch_shapes=[
            vm((ROWS, WIDTH), BF),
            vm((2, RIM, WIDTH), BF),
            vm((2, WIDTH, WIDTH), BF),
            vm((2, WIDTH, 256), BF),
            vm((2, INNER_DEV, WIDTH), BF),
            vm((ROWS, INNER_DEV), BF),
            vm((ROWS, ROWS), F32),
            vm((ROWS, 128), F32),
            vm((ROWS, 128), F32),
            vm((ROWS, INNER_DEV), BF),
            vm((ROWS, 128), F32),
            vm((2, ROWS, WIDTH), BF),
            vm((2, 16, 16, 512), BF),
            vm((2, 16, 16, 512), BF),
            vm((2, 16, 16, 384), BF),
            vm((2, 16, 16, 384), BF),
            vm((2, 4, ROWS, 384), BF),
            vm((2, 8, ROWS), F32),
            vm((2, 4, 8, ROWS), F32),
            vm((2, ROWS, 384), BF),
            vm((RIM, 384), BF),
            dma((6,)),
            dma((6,)),
            dma((4,)),
            dma((5,)),
            dma((5,)),
            dma((2, 16)),
            dma((2, 16)),
            dma((2, 16)),
            dma((2, 16)),
            dma((2, 8)),
            dma((2, 8)),
            dma((2, 4)),
            dma((2, 4)),
            dma((3,)),
            dma,
        ],
        compiler_params=comm_params(number),
        name="forward_layers",
    )(x_in, zx_m, bc_m, out_m, dt_m, *smalls)
    kept = [{name: got[16 * s + i] for i, (name, _, _) in enumerate(KEPT)} for s in range(2)]
    return kept, got[32:37]


PART = 48
EARLY, WIDE = 2 * PART, 3 * PART
SUB = WIDE + 16
GROUPS = (((0, PART), (PART, EARLY)), ((EARLY, EARLY + 32), (EARLY + 32, SUB)))
REST = 32
SLOT = ("z", "x_pre", "bc_pre", "dt_pre", "la", "la_t", "xd", "bc_act", "x_act", "y", "decay", "state", "scale", "out")
SHAPES = {name: (shape, kind) for name, shape, kind in KEPT}


def add_rows(total, more):
    return total.astype(F32) + more.astype(F32)


def backward_kernel(*refs):
    cot_ref, x_ref, last_ref = refs[:3]
    held = (refs[3:6], refs[6:9])
    small_all, dt_all = refs[9:11]
    saved = [{name: refs[11 + 16 * s + i] for i, (name, _, _) in enumerate(KEPT)} for s in range(2)]
    grads_ref, rest_ref, section_ref, leaving_ref = refs[43:47]
    rest = list(refs[47:])

    def take(count):
        got = rest[:count]
        del rest[:count]
        return got

    k = dict(zip(SLOT, take(len(SLOT))))
    normed_all, v_all, d_v, g_o_buf = take(4)
    zx_w, bc_w, out_w = take(3)
    own, spare, theirs, first, mid, second, ring = take(7)
    d_y_ref, d_z_ref, d_xd, d_y_low, wide_x, wide_y = take(6)
    scores_t, d_scores_t, d_bc, terms, direct, tail_ref, dt_ref = take(7)
    ext, d_zx, d_bd, part, sum_in, d_normed_ref, sum_own = take(7)
    chain_out, chain_in, chain_back, chain_got, state_grad = take(5)
    rim_buf, taps_ref, bc_out, bc_in, norm_ref, sums_ref, small_rows = take(7)
    rest_out, rest_cross, rest_near, rest_far, rest_low = take(5)
    k_sem, n_sem, w_sem, move_sem = take(4)
    c_sems, s_sems, rim_sems, swap_sems = take(4), take(4), take(2), take(2)
    cross_sems, one_sems, two_sems, back_sems, last_sems = take(2), take(2), take(2), take(2), take(2)
    bc_sems, rest_sems = take(2), take(2)
    theirs_free, first_free = take(2)

    core, me, place = lax.axis_index("section"), lax.axis_index("seq"), lax.axis_index("head")
    x, z = lax.div(me, 4), lax.rem(me, 4)
    along_z = [x * 4 + shifted(z, d, 4) for d in range(1, 4)]
    along_x = [shifted(x, d, 4) * 4 + z for d in range(1, 4)]
    ways = ((x, z, along_z, along_x), (z, x, along_x, along_z))
    other = {"section": 1 - core}
    heads = [{"head": shifted(place, d, 4)} for d in range(1, 4)]
    targets = [other] + [{"seq": shifted(me, d, 16)} for d in range(1, 16)] + heads
    targets += [{"section": 1 - core, "seq": seq} for seq in along_z + along_x]
    barrier = pltpu.get_barrier_semaphore()
    for target in targets:
        pl.semaphore_signal(barrier, inc=1, device_id=target, device_id_type=MESH)

    def load_kept(s):
        return [
            pltpu.make_async_copy(saved[s][name], k[name], k_sem.at[i]) for i, name in enumerate(SLOT)
        ]

    def load_rows(s):
        source = x_ref.at[core] if s == 0 else saved[0]["following"]
        return [
            pltpu.make_async_copy(saved[s]["normed"], normed_all.at[s], n_sem.at[s, 0]),
            pltpu.make_async_copy(source, v_all.at[s], n_sem.at[s, 1]),
        ]

    weight_slots = (zx_w, bc_w, out_w)

    def load_weight(s, i):
        @pl.when(core == s)
        def _():
            pltpu.make_async_copy(held[0][i], weight_slots[i], w_sem.at[i]).start()

        @pl.when(core != s)
        def _():
            pltpu.make_async_copy(held[1][i], weight_slots[i], w_sem.at[i]).start()

    def wait_weight(i):
        pltpu.make_async_copy(held[0][i], weight_slots[i], w_sem.at[i]).wait()

    load_g_o = pltpu.make_async_copy(cot_ref.at[core], g_o_buf, n_sem.at[0, 2])
    load_g_o.start()
    load_weight(1, 2)
    for move in load_kept(1):
        move.start()
    load_weight(1, 0)
    load_weight(1, 1)
    for s in (1, 0):
        for move in load_rows(s):
            move.start()

    small_rows[...] = jnp.zeros_like(small_rows)
    pl.semaphore_wait(barrier, len(targets))

    def swapped(i, src, dst):
        return pltpu.make_async_remote_copy(
            src_ref=src,
            dst_ref=dst.at[core],
            send_sem=swap_sems[0].at[i],
            recv_sem=swap_sems[1].at[i],
            device_id=other,
            device_id_type=MESH,
        )

    @pl.when(core == 0)
    def _():
        swapped(0, last_ref, section_ref).start()

    @pl.when(core == 1)
    def _():
        swapped(0, saved[0]["following"], section_ref).start()

    def cross(s, piece):
        lo, hi = GROUPS[piece][0][0], GROUPS[piece][1][1]
        return pltpu.make_async_remote_copy(
            src_ref=spare.at[:, :, lo:hi],
            dst_ref=theirs.at[:, :, lo:hi],
            send_sem=cross_sems[0].at[s, piece],
            recv_sem=cross_sems[1].at[s, piece],
            device_id=other,
            device_id_type=MESH,
        )

    def reduction(s, group):
        parts = [(n, lo, hi) + ways[n] for n, (lo, hi) in enumerate(GROUPS[group])]
        low, high = parts[0][1], parts[1][2]
        cross(s, group).wait_recv()

        @pl.loop(0, 4)
        def _(i):
            @pl.loop(0, 4)
            def _(j):
                own[s, i, j, low:high] = add_rows(own[s, i, j, low:high], theirs[i, j, low:high]).astype(BF)

        if s == 0:
            pl.semaphore_wait(first_free.at[group], 6)
        copies = []
        for d in range(3):
            for n, lo, hi, a, b, near, far in parts:
                src = own.at[s, :, shifted(b, d + 1, 4), lo:hi]
                dst = first.at[d, :, lo:hi]
                sems = one_sems[0].at[s, group, n, d], one_sems[1].at[s, group, n, d]
                copies.append(send(src, dst, *sems, {"seq": near[d]}))
        yield
        finish(copies)

        @pl.loop(0, 4)
        def _(i):
            for n, lo, hi, a, b, near, far in parts:
                total = own[s, i, b, lo:hi].astype(F32)
                for d in range(3):
                    total = total + first[d, i, lo:hi].astype(F32)
                mid[i, lo:hi] = total.astype(BF)

        copies = []
        for d in range(3):
            for n, lo, hi, a, b, near, far in parts:
                src = mid.at[shifted(a, d + 1, 4), lo:hi]
                dst = second.at[s, d, lo:hi]
                sems = two_sems[0].at[s, group, n, d], two_sems[1].at[s, group, n, d]
                copies.append(send(src, dst, *sems, {"seq": far[d]}))
        yield
        finish(copies)
        copies = []
        for n, lo, hi, a, b, near, far in parts:
            total = mid[a, lo:hi].astype(F32)
            for d in range(3):
                total = total + second[s, d, lo:hi].astype(F32)
            ring[s, a, lo:hi] = total.astype(BF)
            for d in range(3):
                block = ring.at[s, a, lo:hi]
                sems = back_sems[0].at[s, group, n, d], back_sems[1].at[s, group, n, d]
                copies.append(send(block, block, *sems, {"seq": far[d]}))
        yield
        finish(copies)

        def last(part, d, half):
            n, lo, hi, a, b, near, far = part
            return pltpu.make_async_remote_copy(
                src_ref=ring.at[s, :, lo:hi],
                dst_ref=grads_ref.at[half, :, b, lo:hi],
                send_sem=last_sems[0].at[s, group, n, d],
                recv_sem=last_sems[1].at[s, group, n, half, d],
                device_id={"section": s, "seq": near[d] if d < 3 else me},
                device_id_type=MESH,
            )

        def stay(part):
            n, lo, hi, a, b, near, far = part
            sem = last_sems[0].at[s, group, n, 3]
            return pltpu.make_async_copy(ring.at[s, :, lo:hi], grads_ref.at[core, :, b, lo:hi], sem)

        for d in range(3):
            for part in parts:
                last(part, d, core).start()

        @pl.when(core == s)
        def _():
            for part in parts:
                stay(part).start()

        @pl.when(core != s)
        def _():
            for part in parts:
                last(part, 3, core).start()

        yield
        for part in parts:
            for d in range(3):
                last(part, d, core).wait_send()

        @pl.when(core == s)
        def _():
            for part in parts:
                stay(part).wait()
                for d in range(3):
                    last(part, d, s).wait_recv()
                for d in range(4):
                    last(part, d, 1 - s).wait_recv()

        @pl.when(core != s)
        def _():
            for part in parts:
                last(part, 3, core).wait_send()

        yield

    def reduction_rest(s):
        def move(src, dst, i, target):
            return send(src, dst, rest_sems[0].at[s, i], rest_sems[1].at[s, i], target)

        def gather(bufs, first_sem, peers):
            return [move(rest_low.at[s], bufs.at[s, d], first_sem + d, {"seq": peers[d]}) for d in range(3)]

        copy = move(rest_out.at[1 - core], rest_cross.at[s], 0, other)
        yield
        copy.wait()
        total = add_rows(rest_out[core], rest_cross[s])
        rest_low[s] = total.astype(BF)
        copies = gather(rest_near, 1, along_z)
        yield
        finish(copies)
        for d in range(3):
            total = total + rest_near[s, d].astype(F32)
        rest_low[s] = total.astype(BF)
        copies = gather(rest_far, 4, along_x)
        yield
        finish(copies)
        for d in range(3):
            total = total + rest_far[s, d].astype(F32)
        rest_low[s] = total.astype(BF)

        def deliver():
            return pltpu.make_async_remote_copy(
                src_ref=rest_low.at[s],
                dst_ref=rest_ref.at[core],
                send_sem=rest_sems[0].at[s, 7],
                recv_sem=rest_sems[1].at[s, 7],
                device_id=other,
                device_id_type=MESH,
            )

        @pl.when(core != s)
        def _():
            deliver().start()

        @pl.when(core == s)
        def _():
            rest_ref[core] = rest_low[s]

        yield

        @pl.when(core != s)
        def _():
            deliver().wait_send()

        @pl.when(core == s)
        def _():
            deliver().wait_recv()

        yield

    member_rows = lax.broadcasted_iota(jnp.int32, (INNER_DEV, 128), 0)
    member_lanes = lax.broadcasted_iota(jnp.int32, (INNER_DEV, 128), 1) * HEAD_DIM
    inside = (member_rows >= member_lanes) & (member_rows < member_lanes + HEAD_DIM)
    member = jnp.where(inside, 1.0, 0.0).astype(BF)

    def sums_of(value):
        high, low = two_part(value)
        return dot(high, member) + dot(low, member)

    half_rows = [
        [pl.ds(pl.multiple_of(h * INNER_DEV + 384 * j, 384), 384) for j in range(2)] for h in (core, 1 - core)
    ]
    half_cols = [pl.ds(pl.multiple_of(h * INNER_DEV, INNER_DEV), INNER_DEV) for h in (core, 1 - core)]
    early, late, loose = None, None, None
    old_early, old_late = None, None
    load_g_o.wait()
    for s in (1, 0):
        small = small_all.at[s]
        normed, v_ref = normed_all.at[s], v_all.at[s]
        g_o_ref = g_o_buf if s else d_v.at[1]
        y_ref, z_ref, la_ref, la_t_ref = k["y"], k["z"], k["la"], k["la_t"]
        xd_ref, bc_act, x_act = k["xd"], k["bc_act"], k["x_act"]
        x_pre, bc_pre = k["x_pre"], k["bc_pre"]
        stages = (own.at[s], spare)

        sums_ref[...] = jnp.zeros_like(sums_ref)
        wait_weight(2)

        @pl.loop(0, 3)
        def _(j):
            d_xd[:, tile_at(j)] = dot_last(g_o_ref[...], out_w[tile_at(j), :])

        if s:
            load_weight(0, 2)
        finish(load_kept(s))
        if s:
            finish(load_rows(1))

        @pl.loop(0, BLOCKS)
        def _(i):
            at = rows_at(i)
            gain = small[S_GATE : S_GATE + 1, :INNER_DEV]
            scale = k["scale"][at][:, 0:1]
            act, gate, dm = x_act[at], z_ref[at], d_xd[at]
            ssd = y_ref[at] + small[S_SKIP : S_SKIP + 1, :INNER_DEV] * act
            sigma = jax.nn.sigmoid(gate)
            gate_silu = gate * sigma
            gated = ssd * gate_silu
            scaled = gated * scale
            mean = jnp.sum(g_o_ref[at].astype(F32) * k["out"][at].astype(F32), axis=-1, keepdims=True)
            mean = mean * scale * scale * (1.0 / INNER)
            wide_x[at] = (scaled * gain).astype(BF)
            d_gated = scale * gain * dm - gated * mean
            d_y = d_gated * gate_silu
            d_y_ref[at] = d_y
            d_y_low[at] = d_y.astype(BF)
            d_z_ref[at] = (d_gated * ssd * sigma * (1.0 + gate * (1.0 - sigma))).astype(BF)
            wide_y[at] = (spread(jnp.exp(la_ref[at])) * d_y).astype(BF)
            sums_ref[0:1] += jnp.sum(scaled * dm, axis=0, keepdims=True)
            sums_ref[1:2] += jnp.sum(d_y * act, axis=0, keepdims=True)

        b_rows, c_rows = bc_act[:, :STATE], bc_act[:, STATE:]
        chain_load(dot_first(c_rows, wide_y[...]), k["decay"], chain_out)
        copies = spread_send(chain_out, chain_in, me, c_sems[0].at[s], c_sems[1].at[s])

        if s == 0:
            for piece in range(2):
                cross(1, piece).wait_send()
        for stage, cols, rows in zip(stages, half_cols, half_rows):
            for j in range(2):
                got = dot_first(wide_x[:, 384 * j : 384 * j + 384], g_o_ref[:, cols]).astype(BF)
                for i in range(8):
                    sub = 8 * j + i
                    stage[sub // 4, sub % 4, 0:PART] = got[PART * i : PART * i + PART]
            for j in range(2):
                got = dot_first(normed[RIM:, rows[j]], d_z_ref[...]).astype(BF)
                for i in range(8):
                    sub = 8 * j + i
                    stage[sub // 4, sub % 4, PART:EARLY] = got[PART * i : PART * i + PART]
        if s == 0:
            pl.semaphore_wait(theirs_free, 1)
        cross(s, 0).start()
        if s == 0:
            next(late)
            for seq in along_z + along_x:
                pl.semaphore_signal(first_free.at[1], inc=1, device_id={"seq": seq}, device_id_type=MESH)
            next(loose)

        la = la_ref[...]
        tail_ref[...] = jnp.exp(la[ROWS - 1 : ROWS] - la)
        dt_in = k["dt_pre"][...] + small[S_BIAS : S_BIAS + 1, :128]
        dt_ref[...] = softplus(dt_in)
        scores_t[...] = dot_last(b_rows, c_rows)

        def heads_of(half):
            base = half * 128
            rows = slice(base, base + 128)
            t = lax.broadcasted_iota(jnp.int32, (128, ROWS - base), 1)
            later = t >= lax.broadcasted_iota(jnp.int32, (128, ROWS - base), 0)
            total = jnp.zeros((128, ROWS - base), F32)
            for pair in range(HEADS_DEV // 2):
                parts = []
                for h in (2 * pair, 2 * pair + 1):
                    cols = slice(h * HEAD_DIM, (h + 1) * HEAD_DIM)
                    gap = la_t_ref[h : h + 1, base:] - la_ref[rows, h : h + 1]
                    decay = jnp.exp(jnp.where(later, gap, -1e30))
                    total = total + decay * dot_last(xd_ref[rows, cols], d_y_low[base:, cols])
                    mixing = (scores_t[rows, base:] * decay).astype(BF)
                    parts.append(dot(mixing, d_y_low[base:, cols]))
                d_xd[rows, pair * 128 : pair * 128 + 128] = jnp.concatenate(parts, axis=1)
            if half:
                d_scores_t[rows, 0:128] = jnp.zeros((128, 128), BF)
            d_scores_t[rows, base:] = total.astype(BF)

        heads_of(0)
        finish(copies)
        chain_scan(False, chain_in, chain_back)
        copies = spread_send(chain_back, chain_got, me, c_sems[2].at[s], c_sems[3].at[s])
        old_early, early = early, reduction(s, 0)
        next(early)
        heads_of(1)
        finish(copies)
        if s == 0:
            next(late)
            next(loose)
        chain_unload(chain_got, state_grad)
        norm_ref[...] = jnp.zeros_like(norm_ref)
        taps_ref[...] = jnp.zeros_like(taps_ref)

        @pl.loop(0, BLOCKS)
        def _(i):
            at = rows_at(i)
            tail = spread(tail_ref[at])
            xd = xd_ref[at].astype(F32)
            wide_x[at] = (tail * xd).astype(BF)
            state_part = tail * dot(bc_act[at, :STATE], state_grad[...])
            got = d_xd[at] + state_part
            d_xd[at] = got
            norm_ref[1:2, :INNER_DEV] += jnp.sum(xd * state_part, axis=0, keepdims=True)
            terms[at] = sums_of(d_y_low[at].astype(F32) * y_ref[at] - xd * got)
            direct[at] = sums_of(x_act[at] * got)

        d_bc[:, :STATE] = dot(d_scores_t[...], c_rows) + dot_last(wide_x[...], state_grad[...])
        d_bc[:, STATE:] = dot_first(d_scores_t[...], b_rows) + dot_last(wide_y[...], k["state"][...])
        end_wide = spread(jnp.exp(la[ROWS - 8 : ROWS]))[7:8]
        both = state_grad[...].astype(F32) * k["state"][...].astype(F32)
        tail_sum = norm_ref[1:2, :INNER_DEV] + end_wide * jnp.sum(both, axis=0, keepdims=True)
        tail_sum = sums_of(jnp.broadcast_to(tail_sum, (16, INNER_DEV)))[0:1]

        @pl.loop(0, BLOCKS)
        def _(i):
            at = rows_at(i)
            taps = small[S_CONV : S_CONV + 4, INNER_DEV : INNER_DEV + 256]
            d_bcc = d_bc[at] * silu_slope(conv_rows(bc_pre[rows_at(i, RIM)], taps))
            d_bc[at] = d_bcc
            bc_out[at] = d_bcc.astype(BF)

        copies = [
            send(bc_out, bc_in.at[d], bc_sems[0].at[s, d], bc_sems[1].at[s, d], heads[d]) for d in range(3)
        ]
        d_log = running(terms[...], True) + tail_sum
        rate = small[S_RATE : S_RATE + 1, :128]
        d_dt = direct[...] + rate * d_log
        d_dt_pre = d_dt * jax.nn.sigmoid(dt_in)
        d_bd[:, 256:] = d_dt_pre.astype(BF)
        sums_ref[2:3, :128] = jnp.sum(dt_ref[...] * d_log, axis=0, keepdims=True) * rate
        sums_ref[3:4, :128] = jnp.sum(d_dt_pre, axis=0, keepdims=True)

        @pl.loop(0, BLOCKS)
        def _(i):
            at = rows_at(i)
            taps = small[S_CONV : S_CONV + 4]
            pre = x_pre[rows_at(i, RIM)]
            d_x = spread(dt_ref[at]) * d_xd[at] + small[S_SKIP : S_SKIP + 1, :INNER_DEV] * d_y_ref[at]
            d_xc = d_x * silu_slope(conv_rows(pre, taps[:, :INNER_DEV]))
            ext[at, :INNER_DEV] = d_xc
            for t in range(4):
                moved = pre[RIM - 3 + t : RIM - 3 + t + STEP]
                taps_ref[t : t + 1, :INNER_DEV] += jnp.sum(moved * d_xc, axis=0, keepdims=True)

        finish(copies)

        @pl.loop(0, BLOCKS)
        def _(i):
            at = rows_at(i)
            d_bcc = d_bc[at]
            for d in range(3):
                d_bcc = d_bcc + bc_in[d, at].astype(F32)
            ext[at, INNER_DEV:] = d_bcc
            pre = bc_pre[rows_at(i, RIM)]
            for t in range(4):
                moved = pre[RIM - 3 + t : RIM - 3 + t + STEP]
                taps_ref[t : t + 1, INNER_DEV:] += jnp.sum(moved * d_bcc, axis=0, keepdims=True)

        rim = send(
            ext.at[0:8], rim_buf, rim_sems[0].at[s], rim_sems[1].at[s], {"seq": shifted(me, -1, 16)}
        )
        if s:
            for move in load_kept(0):
                move.start()

        if s == 0:
            next(loose)
            next(late)
        else:
            next(early)
            for seq in along_z + along_x:
                pl.semaphore_signal(first_free.at[0], inc=1, device_id={"seq": seq}, device_id_type=MESH)
        rim.wait()

        @pl.when(me == 15)
        def _():
            rim_buf[...] = jnp.zeros_like(rim_buf)

        ext[ROWS : ROWS + 8] = rim_buf[...]

        @pl.loop(0, BLOCKS)
        def _(i):
            at = rows_at(i)
            taps = small[S_CONV : S_CONV + 4]
            block = ext[rows_at(i, 8)]
            d_pre = taps[0:1, : INNER_DEV + 256] * block[3 : 3 + STEP]
            for t in range(1, 4):
                d_pre = d_pre + taps[t : t + 1, : INNER_DEV + 256] * block[3 - t : 3 - t + STEP]
            d_zx[at, :INNER_DEV] = d_z_ref[at]
            d_zx[at, INNER_DEV:] = d_pre[:, :INNER_DEV].astype(BF)
            d_bd[at, :256] = d_pre[:, INNER_DEV:].astype(BF)

        wait_weight(0)
        wait_weight(1)

        @pl.loop(0, 6)
        def _(j):
            got = dot_last(d_zx[...], zx_w[tile_at(j), :])
            got = got + dot_last(d_bd[:, :256], bc_w[tile_at(j), :]) * 0.25
            got = got + dot(d_bd[:, 256:], dt_all[s, :, tile_at(j)])
            part[:, tile_at(j)] = got.astype(BF)

        if s:
            load_weight(0, 0)
            load_weight(0, 1)
        copies = []
        for d in range(1, 4):
            src = part.at[:, quarter(shifted(place, d, 4))]
            copies.append(send(src, sum_in.at[d - 1], s_sems[0].at[s, d], s_sems[1].at[s, d], heads[d - 1]))
        for stage, rows in zip(stages, half_rows):
            for j in range(2):
                got = dot_first(normed[RIM:, rows[j]], d_zx[:, INNER_DEV:]).astype(BF)
                for i in range(8):
                    sub = 8 * j + i
                    stage[sub // 4, sub % 4, EARLY:WIDE] = got[PART * i : PART * i + PART]

        for n, (stage, cols) in enumerate(zip(stages, half_cols)):
            got = dot_first(d_bd[...], normed[RIM:, cols])
            for i in range(16):
                stage[i // 4, i % 4, WIDE:SUB] = got[16 * i : 16 * i + 16].astype(BF)
            rest_out[core if n == 0 else 1 - core, 0:16] = got[256:272].astype(BF)
        cross(s, 1).start()
        next(early)
        finish(copies)

        @pl.loop(0, BLOCKS)
        def _(i):
            at = rows_at(i)
            total = part[at, quarter(place)].astype(F32)
            for d in range(3):
                total = total + sum_in[d, at].astype(F32)
            total = total.astype(BF)
            sum_own[at] = total
            d_normed_ref[at, quarter(place)] = total

        copies = []
        for d in range(1, 4):
            dst = d_normed_ref.at[:, quarter(place)]
            copies.append(send(sum_own, dst, s_sems[2].at[s, d], s_sems[3].at[s, d], heads[d - 1]))
        old_late, late = late, reduction(s, 1)
        next(early)
        if s == 0:
            next(late)
        finish(copies)
        if s == 0:
            next(early)
        norm_ref[...] = jnp.zeros_like(norm_ref)

        @pl.loop(0, BLOCKS)
        def _(i):
            at = rows_at(i)
            v = v_ref[at].astype(F32)
            scale = lax.rsqrt(jnp.mean(v * v, axis=-1, keepdims=True) + EPS)
            d_normed = d_normed_ref[at].astype(F32)
            scaled = v * scale
            norm_ref[0:1] += jnp.sum(scaled * d_normed, axis=0, keepdims=True)
            weighted = d_normed * small[S_NORM : S_NORM + 1]
            mean = jnp.mean(v * weighted, axis=-1, keepdims=True) * scale * scale
            d_v[s, at] = (scale * weighted - scaled * mean + g_o_ref[at].astype(F32)).astype(BF)

        for h in range(2):
            small_rows[h, 0:1] = norm_ref[0:1, h * INNER_DEV : (h + 1) * INNER_DEV]
            small_rows[h, 1:5] = taps_ref[0:4, :INNER_DEV]
            small_rows[h, 5:9] = sums_ref[0:4]
            small_rows[h, 9:13, 0:256] = taps_ref[0:4, INNER_DEV:]
            rest_out[h, 16:] = small_rows[h].astype(BF)
        old_loose, loose = loose, reduction_rest(s)
        next(loose)
        if s:
            next(late)
            pl.semaphore_signal(theirs_free, inc=1, device_id=other, device_id_type=MESH)

        @pl.when(core == 1 - s)
        def _():
            swapped(1, d_v.at[s], leaving_ref).start()

        @pl.when(core == s)
        def _():
            pltpu.make_async_copy(d_v.at[s], leaving_ref.at[s], move_sem.at[1]).start()

        if s:

            @pl.when(core == 0)
            def _():
                pltpu.make_async_copy(v_all.at[1], section_ref.at[0], move_sem.at[0]).start()

            finish(load_rows(0))

            @pl.when(core == 1)
            def _():
                pltpu.make_async_copy(last_ref, g_o_buf, move_sem.at[0]).start()

    @pl.when(core == 1)
    def _():
        pltpu.make_async_copy(last_ref, g_o_buf, move_sem.at[0]).wait()
        pltpu.make_async_copy(g_o_buf, section_ref.at[1], move_sem.at[0]).start()

    for turn in (loose, late, loose, late, loose, late, loose, early, late, old_early, old_late, old_loose):
        next(turn)
    for piece in range(2):
        cross(0, piece).wait_send()
    swapped(0, last_ref, section_ref).wait()
    swapped(1, d_v.at[0], leaving_ref).wait()
    pltpu.make_async_copy(d_v.at[0], leaving_ref.at[0], move_sem.at[1]).wait()
    pltpu.make_async_copy(d_v.at[0], section_ref.at[0], move_sem.at[0]).wait()


def backward(cotangent, x_in, last, held, smalls, dt_all, kept, number):
    dma = pltpu.SemaphoreType.DMA
    regular = pltpu.SemaphoreType.REGULAR
    sds = jax.ShapeDtypeStruct
    vm = pltpu.VMEM
    halves = (4, 4, SUB, INNER_DEV)
    rows_low = vm((ROWS, INNER_DEV), BF)
    rows_wide = vm((ROWS, INNER_DEV), F32)
    steps = vm((ROWS, 128), F32)
    scratch = [vm(*SHAPES[name]) for name in SLOT]
    scratch += [
        vm((2, ROWS + RIM, WIDTH), BF),
        vm((2, ROWS, WIDTH), BF),
        vm((2, ROWS, WIDTH), BF),
        vm((ROWS, WIDTH), BF),
        vm((WIDTH, WIDTH), BF),
        vm((WIDTH, 256), BF),
        vm((INNER_DEV, WIDTH), BF),
        vm((2,) + halves, BF),
        vm(halves, BF),
        vm(halves, BF),
        vm((3, 4, SUB, INNER_DEV), BF),
        vm((4, SUB, INNER_DEV), BF),
        vm((2, 3, SUB, INNER_DEV), BF),
        vm((2, 4, SUB, INNER_DEV), BF),
        rows_wide, rows_low, rows_wide, rows_low, rows_low, rows_low,
        vm((ROWS, ROWS), F32),
        vm((ROWS, ROWS), BF),
        vm((ROWS, 256), F32),
        steps, steps, steps, steps,
        vm((ROWS + 8, INNER_DEV + 256), F32),
        vm((ROWS, WIDTH), BF),
        vm((ROWS, 384), BF),
        vm((ROWS, WIDTH), BF),
        vm((3, ROWS, 384), BF),
        vm((ROWS, WIDTH), BF),
        vm((ROWS, 384), BF),
        vm((16, 16, 512), BF),
        vm((16, 16, 512), BF),
        vm((16, 16, 384), BF),
        vm((16, 16, 384), BF),
        vm((STATE, INNER_DEV), BF),
        vm((8, INNER_DEV + 256), F32),
        vm((8, INNER_DEV + 256), F32),
        vm((ROWS, 256), BF),
        vm((3, ROWS, 256), BF),
        vm((8, WIDTH), F32),
        vm((8, INNER_DEV), F32),
        vm((2, 16, INNER_DEV), F32),
        vm((2, REST, INNER_DEV), BF),
        vm((2, REST, INNER_DEV), BF),
        vm((2, 3, REST, INNER_DEV), BF),
        vm((2, 3, REST, INNER_DEV), BF),
        vm((2, REST, INNER_DEV), BF),
        dma((len(SLOT),)),
        dma((2, 3)),
        dma((3,)),
        dma((2,)),
    ]
    scratch += [dma((2, 16))] * 4 + [dma((2, 8))] * 2 + [dma((2, 4))] * 2
    scratch += [dma((2,))] * 4 + [dma((2, 2))] * 2
    scratch += [dma((2, 2, 2, 4))] * 7 + [dma((2, 2, 2, 2, 4))]
    scratch += [dma((2, 3))] * 2 + [dma((2, 8))] * 2 + [regular, regular((2,))]
    flat = [kept[s][name] for s in range(2) for name, _, _ in KEPT]
    return pl.pallas_call(
        backward_kernel,
        out_shape=[
            sds((2,) + halves, BF),
            sds((2, REST, INNER_DEV), BF),
            sds((2, ROWS, WIDTH), BF),
            sds((2, ROWS, WIDTH), BF),
        ],
        in_specs=[ANY] * 9 + [VM] * 2 + [ANY] * 32,
        out_specs=[ANY, VM, ANY, ANY],
        scratch_shapes=scratch,
        compiler_params=comm_params(number),
        name="backward_layers",
    )(cotangent, x_in, last, *held, smalls, dt_all, *flat)


def widen_kernel(
    a_ref, rest_ref, zx_ref, out_ref, bc_ref, dt_ref, norm_ref, bias_ref, rate_ref, skip_ref, conv_ref, conv_bc_ref,
    gate_ref, bc_all,
):
    step = pl.program_id(0)
    for h in range(2):
        cols = slice(h * INNER_DEV, (h + 1) * INNER_DEV)
        zx_ref[h, :, 0, :] = a_ref[h, 0, PART:EARLY].astype(F32)
        zx_ref[h, :, 1, :] = a_ref[h, 0, EARLY:WIDE].astype(F32)
        out_ref[:, cols] = a_ref[h, 0, 0:PART].astype(F32)
        at = pl.ds(pl.multiple_of(step * 16, 16), 16)
        bc_all[at, cols] = a_ref[h, 0, WIDE:SUB].astype(F32)

    @pl.when(step == 0)
    def _():
        rows = rest_ref[0].astype(F32)
        more = rest_ref[1].astype(F32)
        dt_ref[:, :INNER_DEV] = rows[0:HEADS_DEV]
        dt_ref[:, INNER_DEV:] = more[0:HEADS_DEV]
        rows = rows[16:]
        norm_ref[:, :INNER_DEV] = rows[0:1]
        norm_ref[:, INNER_DEV:] = more[16:17]
        conv_ref[...] = rows[1:5]
        gate_ref[...] = rows[5:6]
        heads = jnp.concatenate(
            [
                jnp.sum(rows[0:8, h * HEAD_DIM : (h + 1) * HEAD_DIM], axis=1, keepdims=True)
                for h in range(HEADS_DEV)
            ],
            axis=1,
        )
        skip_ref[...] = heads[6:7]
        rate_ref[...] = rows[7:8, 0:HEADS_DEV]
        bias_ref[...] = rows[8:9, 0:HEADS_DEV]
        conv_bc_ref[...] = rows[9:13, 0:256]

    @pl.when(step == 15)
    def _():
        bc_ref[...] = bc_all[...].T


def widen(total, rest):
    total = total.reshape(2, 16, SUB, INNER_DEV)
    fixed = ((WIDTH, 256), (HEADS_DEV, WIDTH), (1, WIDTH)) + ((1, HEADS_DEV),) * 3
    fixed += ((4, INNER_DEV), (4, 256), (1, INNER_DEV))
    shapes = ((2, INNER_DEV, 2, INNER_DEV), (INNER_DEV, WIDTH)) + fixed
    return pl.pallas_call(
        widen_kernel,
        grid=(16,),
        out_shape=[jax.ShapeDtypeStruct(shape, F32) for shape in shapes],
        in_specs=[
            pl.BlockSpec((2, 1, SUB, INNER_DEV), lambda i: (0, i, 0, 0)),
            pl.BlockSpec((2, REST, INNER_DEV), lambda i: (0, 0, 0)),
        ],
        out_specs=[
            pl.BlockSpec((2, PART, 2, INNER_DEV), lambda i: (0, i, 0, 0)),
            pl.BlockSpec((PART, WIDTH), lambda i: (i, 0)),
        ]
        + [pl.BlockSpec(shape, lambda i: (0, 0)) for shape in fixed],
        scratch_shapes=[pltpu.VMEM((256, WIDTH), F32)],
        compiler_params=pltpu.CompilerParams(vmem_limit_bytes=VMEM_CAP),
        name="widen",
    )(total, rest)


def on_device(
    x_in,
    norm_gain,
    w_zx,
    w_bc,
    w_dt,
    dt_bias,
    a_log,
    d_skip,
    conv_x,
    conv_bc,
    gate_gain,
    w_out,
    cotangent,
):
    zx_m = w_zx[0].reshape(WIDTH, WIDTH)
    bc_m, out_m, dt_m = w_bc[0], w_out[0], w_dt[0].T
    small_args = (norm_gain, gate_gain, conv_x[0], conv_bc[0], dt_bias, a_log, d_skip)
    kept, (zx_t, bc_t, out_t, smalls, dt_all) = forward(x_in, zx_m, bc_m, out_m, dt_m, small_args, 0)
    held = (zx_m, bc_m, out_m, zx_t, bc_t, out_t)
    total, rest, section_out, grads_in = backward(
        cotangent, x_in, kept[1]["following"], held, smalls, dt_all, kept, 1
    )
    g_zx, g_out, g_bc, g_dt, g_norm, g_bias, g_rate, g_skip, g_conv_x, g_conv_bc, g_gate = widen(total, rest)
    return (
        section_out[None],
        grads_in[None],
        g_norm,
        g_zx.reshape(1, WIDTH, 2, INNER_DEV),
        g_bc[None],
        g_dt.T[None],
        g_bias,
        g_rate,
        g_skip,
        g_conv_x[None],
        g_conv_bc[None],
        g_gate,
        g_out[None],
    )


def solution(mesh):
    in_specs = (
        P(None, "seq", None),
        P("section", None),
        P("section", None, None, "head"),
        P("section", None, None),
        P("section", None, "head"),
        P("section", "head"),
        P("section", "head"),
        P("section", "head"),
        P("section", None, "head"),
        P("section", None, None),
        P("section", "head"),
        P("section", "head", None),
        P(None, "seq", None),
    )
    out_specs = (
        P("section", None, "seq", None),
        P("section", None, "seq", None),
        P("section", None),
        P("section", None, None, "head"),
        P("section", None, None),
        P("section", None, "head"),
        P("section", "head"),
        P("section", "head"),
        P("section", "head"),
        P("section", None, "head"),
        P("section", None, None),
        P("section", "head"),
        P("section", "head", None),
    )
    return jax.shard_map(
        on_device, mesh=mesh, in_specs=in_specs, out_specs=out_specs, check_vma=False
    )
```

```python
import functools

import jax
import jax.numpy as jnp
from jax import lax
from jax.experimental import pallas as pl
from jax.experimental.pallas import tpu as pltpu
from jax.sharding import PartitionSpec as P

MESH = pl.DeviceIdType.MESH
F32 = jnp.float32
BF = jnp.bfloat16
EPS = 1e-05
INNER = 3072
ROWS = 256
WIDTH = 1536
INNER_DEV = 768
HEADS_DEV = 12
HEAD_DIM = 64
STATE = 128
RIM = 16
VMEM_CAP = 60 << 20
FIRST = (((0,), (0,)), ((), ()))
LAST = (((1,), (1,)), ((), ()))


def dot(a, b):
    return jnp.dot(a, b, preferred_element_type=F32)


def dot_first(a, b):
    return lax.dot_general(a, b, FIRST, preferred_element_type=F32)


def dot_last(a, b):
    return lax.dot_general(a, b, LAST, preferred_element_type=F32)


def two_part(a):
    high = a.astype(BF)
    return high, (a - high.astype(F32)).astype(BF)


def silu(a):
    return a * jax.nn.sigmoid(a)


def silu_slope(a):
    sigma = jax.nn.sigmoid(a)
    return sigma * (1.0 + a * (1.0 - sigma))


def spread(a):
    rows = a.shape[0]
    low_half = lax.broadcasted_iota(jnp.int32, (rows, 128), 1) < HEAD_DIM
    return jnp.concatenate(
        [
            jnp.where(low_half, a[:, 2 * j : 2 * j + 1], a[:, 2 * j + 1 : 2 * j + 2])
            for j in range(HEADS_DEV // 2)
        ],
        axis=1,
    )


def triangle(keep_after):
    t = lax.broadcasted_iota(jnp.int32, (ROWS, ROWS), 0)
    s = lax.broadcasted_iota(jnp.int32, (ROWS, ROWS), 1)
    return jnp.where((s >= t) if keep_after else (t >= s), 1.0, 0.0).astype(BF)


def running(a, keep_after):
    weights = triangle(keep_after)
    high, low = two_part(a)
    return dot(weights, high) + dot(weights, low)


S_NORM, S_GATE, S_CONV, S_BIAS, S_RATE, S_SKIP = 0, 1, 2, 6, 7, 9
STEP = 32
BLOCKS = ROWS // STEP


def softplus(a):
    return jnp.maximum(a, 0.0) + jnp.log1p(jnp.exp(-jnp.abs(a)))


def rows_at(i, more=0):
    return pl.ds(pl.multiple_of(i * STEP, STEP), STEP + more)


def tile_at(i, width=256, base=0):
    return pl.ds(pl.multiple_of(base + i * width, width), width)


def conv_rows(pre, taps):
    total = taps[0:1] * pre[RIM - 3 : RIM - 3 + STEP]
    for k in range(1, 4):
        total = total + taps[k : k + 1] * pre[RIM - 3 + k : RIM - 3 + k + STEP]
    return total


def shifted(place, distance, count):
    return lax.rem(place + distance + count, count)


def meet(targets):
    barrier = pltpu.get_barrier_semaphore()
    for target in targets:
        pl.semaphore_signal(barrier, inc=1, device_id=target, device_id_type=MESH)
    pl.semaphore_wait(barrier, len(targets))


def send(src, dst, send_sem, recv_sem, target):
    copy = pltpu.make_async_remote_copy(
        src_ref=src,
        dst_ref=dst,
        send_sem=send_sem,
        recv_sem=recv_sem,
        device_id=target,
        device_id_type=MESH,
    )
    copy.start()
    return copy


def comm_params(number):
    return pltpu.CompilerParams(
        collective_id=number, has_side_effects=True, vmem_limit_bytes=VMEM_CAP
    )


ANY = pl.BlockSpec(memory_space=pl.ANY)
VM = pl.BlockSpec(memory_space=pltpu.VMEM)


def quarter(place):
    return pl.ds(pl.multiple_of(place * 384, 384), 384)


KEPT = (
    ("normed", (ROWS + RIM, WIDTH), BF),
    ("z", (ROWS, INNER_DEV), F32),
    ("x_pre", (ROWS + RIM, INNER_DEV), F32),
    ("bc_pre", (ROWS + RIM, 256), F32),
    ("dt_pre", (ROWS, 128), F32),
    ("la", (ROWS, 128), F32),
    ("la_t", (128, ROWS), F32),
    ("xd", (ROWS, INNER_DEV), BF),
    ("bc_act", (ROWS, 256), BF),
    ("x_act", (ROWS, INNER_DEV), F32),
    ("y", (ROWS, INNER_DEV), F32),
    ("decay", (8, INNER_DEV), F32),
    ("state", (STATE, INNER_DEV), BF),
    ("scale", (ROWS, 128), F32),
    ("out", (ROWS, WIDTH), BF),
    ("following", (ROWS, WIDTH), BF),
)


def chain_load(own, decay, out_buf):
    for j in range(16):
        rows = own[8 * j : 8 * j + 8]
        out_buf[j, :, 0:384] = jnp.concatenate([rows[:, :384], rows[:, 384:]], axis=0).astype(BF)
    six = jnp.concatenate([decay[0:1, 128 * k : 128 * k + 128] for k in range(6)] * 3, axis=0)
    six = six[0:16].astype(BF)
    for j in range(16):
        out_buf[j, :, 384:512] = six


def chain_scan(forward, in_buf, back_buf):
    state = jnp.zeros((16, 384), F32)
    for step in range(16):
        i = step if forward else 15 - step
        back_buf[i] = state.astype(BF)
        part = in_buf[i].astype(F32)
        decay = jnp.concatenate(
            [
                jnp.concatenate(
                    [
                        jnp.broadcast_to(part[3 * half + k : 3 * half + k + 1, 384:512], (8, 128))
                        for k in range(3)
                    ],
                    axis=1,
                )
                for half in range(2)
            ],
            axis=0,
        )
        state = decay * state + part[:, 0:384]


def chain_unload(got_buf, state_ref):
    for j in range(8):
        first, second = got_buf[2 * j].astype(F32), got_buf[2 * j + 1].astype(F32)
        for half in range(2):
            rows = jnp.concatenate(
                [first[8 * half : 8 * half + 8], second[8 * half : 8 * half + 8]], axis=0
            )
            state_ref[16 * j : 16 * j + 16, 384 * half : 384 * half + 384] = rows.astype(BF)


def spread_send(src, dst, me, send_sem, recv_sem):
    copies = []
    for d in range(1, 16):
        to = shifted(me, d, 16)
        copies.append(send(src.at[to], dst.at[me], send_sem.at[d], recv_sem.at[d], {"seq": to}))
    dst[me] = src[me]
    return copies


def finish(copies):
    for copy in copies:
        copy.wait()


def norm_rows(v, gain):
    v = v.astype(F32)
    scale = lax.rsqrt(jnp.mean(v * v, axis=-1, keepdims=True) + EPS)
    return (v * scale * gain).astype(BF)


def forward_kernel(*refs):
    x_ref, zx_m, bc_m, out_m, dt_m = refs[:5]
    norm_gain, gate_gain, conv_x, conv_bc, dt_bias, a_log, d_skip = refs[5:12]
    stored = [{name: refs[12 + 16 * s + i] for i, (name, _, _) in enumerate(KEPT)} for s in range(2)]
    zx_t, bc_t, out_t, small_w, dt_w, part_ref = refs[44:50]
    v_buf, rim_buf, zx_w, bc_w, out_w = refs[50:55]
    tail_x, scores, dt_buf, tail, low, sq, part = refs[55:62]
    chain_out, chain_in, chain_back, chain_got = refs[62:66]
    sum_in, square_out, square_in, sum_own, next_own = refs[66:71]
    w_send, w_recv, w_own, rim_send, rim_recv = refs[71:76]
    c_sems, s_sems, t_sem, v_sem, k_sem = refs[76:80], refs[80:84], refs[84], refs[85], refs[86]
    kept = [{name: refs[87 + 16 * s + i] for i, (name, _, _) in enumerate(KEPT)} for s in range(2)]

    core, me, place = lax.axis_index("section"), lax.axis_index("seq"), lax.axis_index("head")
    other = {"section": 1 - core}
    later = shifted(me, 1, 16)
    barrier = pltpu.get_barrier_semaphore()
    targets = [other]
    targets += [{"seq": shifted(me, d, 16)} for d in range(1, 16)]
    heads = [{"head": shifted(place, d, 4)} for d in range(1, 4)]
    targets += heads
    targets += [{"head": shifted(place, d, 4), "seq": shifted(me, -1, 16)} for d in range(1, 4)]
    for target in targets:
        pl.semaphore_signal(barrier, inc=1, device_id=target, device_id_type=MESH)

    moves = [
        (bc_m, bc_w.at[core]),
        (zx_m.at[:, INNER_DEV:], zx_w.at[core, :, INNER_DEV:]),
        (zx_m.at[:, :INNER_DEV], zx_w.at[core, :, :INNER_DEV]),
        (out_m, out_w.at[core]),
    ]
    own_moves = [pltpu.make_async_copy(src, dst, w_own.at[i]) for i, (src, dst) in enumerate(moves)]
    for move in own_moves:
        move.start()
    load_v = pltpu.make_async_copy(x_ref.at[core], v_buf, v_sem)
    load_v.start()
    small_w[core] = jnp.zeros((16, WIDTH), F32)
    small_w[core, S_NORM : S_NORM + 1] = norm_gain[...]
    small_w[core, S_GATE : S_GATE + 1, :INNER_DEV] = gate_gain[...]
    small_w[core, S_CONV : S_CONV + 4, :INNER_DEV] = conv_x[...].astype(F32)
    small_w[core, S_CONV : S_CONV + 4, INNER_DEV : INNER_DEV + 256] = conv_bc[...].astype(F32)
    small_w[core, S_BIAS : S_BIAS + 1, 0:HEADS_DEV] = dt_bias[...]
    small_w[core, S_RATE : S_RATE + 1, 0:HEADS_DEV] = -jnp.exp(a_log[...])
    small_w[core, 8:9, 0:HEADS_DEV] = d_skip[...]
    skip_wide = spread(small_w[core, 8:16, 0:128])
    small_w[core, S_SKIP : S_SKIP + 1, :INNER_DEV] = skip_wide[0:1]
    dt_rows = jnp.concatenate([dt_m[...].astype(F32), jnp.zeros((4, WIDTH), F32)], axis=0)
    dt_w[core, 0:16] = dt_rows.astype(BF)
    for s in range(2):
        dt_w[s, 16:] = jnp.zeros((112, WIDTH), BF)
    pl.semaphore_wait(barrier, len(targets))
    rim_copy = send(x_ref.at[core, ROWS - RIM :], rim_buf.at[0], rim_send.at[0], rim_recv.at[0], {"seq": later})
    across = [
        send(small_w.at[core], small_w.at[core], w_send.at[4], w_recv.at[4], other),
        send(dt_w.at[core, 0:16], dt_w.at[core, 0:16], w_send.at[5], w_recv.at[5], other),
    ]
    for i, (src, dst) in enumerate(moves):
        across.append(
            pltpu.make_async_remote_copy(
                src_ref=src,
                dst_ref=dst,
                send_sem=w_send.at[i],
                recv_sem=w_recv.at[i],
                device_id=other,
                device_id_type=MESH,
            )
        )
    across[2].start()
    across[3].start()

    def arrive(section, i):
        @pl.when(core == section)
        def _():
            own_moves[i].wait()

        @pl.when(core != section)
        def _():
            across[i + 2].wait_recv()

    load_v.wait()
    rim_copy.wait()

    @pl.when(me == 0)
    def _():
        rim_buf[0] = jnp.zeros((RIM, WIDTH), BF)

    across[0].wait_recv()
    across[1].wait_recv()
    def store(s, names):
        moves = []
        for i, (name, _, _) in enumerate(KEPT):
            if name in names:
                moves.append(pltpu.make_async_copy(kept[s][name], stored[s][name], k_sem.at[s, i]))
        return moves

    first_names = ("normed", "x_pre", "bc_pre", "dt_pre", "la", "la_t", "xd", "bc_act", "x_act", "decay")
    next_names = ("z", "y", "state")
    last_names = ("scale", "out", "following")
    for s in range(2):
        k = kept[s]
        small = small_w.at[s]
        normed, z_ref, x_pre, bc_pre, la_ref, la_t_ref = (
            k["normed"], k["z"], k["x_pre"], k["bc_pre"], k["la"], k["la_t"]
        )
        xd_ref, bc_act, x_act, y_ref = k["xd"], k["bc_act"], k["x_act"], k["y"]
        gain = small[S_NORM : S_NORM + 1]
        if s:
            finish(rim_in)

            @pl.when(me == 0)
            def _():
                rim_buf[1] = jnp.zeros((RIM, WIDTH), BF)

        normed[0:RIM] = norm_rows(rim_buf[s], gain)
        if s == 0:

            @pl.loop(0, ROWS // 16)
            def _(i):
                at = pl.ds(pl.multiple_of(i * 16, 16), 16)
                normed[pl.ds(pl.multiple_of(i * 16 + RIM, 16), 16)] = norm_rows(v_buf[at], gain)

        arrive(s, 0)
        bc_pre[...] = dot(normed[...], bc_w[s])
        dt_raw = dot_last(normed[RIM:], dt_w[s])
        k["dt_pre"][...] = dt_raw
        arrive(s, 1)

        @pl.loop(0, 3)
        def _(j):
            x_pre[:, tile_at(j)] = dot(normed[...], zx_w[s, :, tile_at(j, 256, INNER_DEV)])

        if s == 0:
            across[3].wait_send()
            across[4].start()
        dt = softplus(dt_raw + small[S_BIAS : S_BIAS + 1, :128])
        dt_buf[...] = dt
        la = running(dt * small[S_RATE : S_RATE + 1, :128], False)
        la_ref[...] = la
        la_t_ref[...] = la.T
        tail[...] = jnp.exp(la[ROWS - 1 : ROWS] - la)
        decay = jnp.broadcast_to(spread(jnp.exp(la[ROWS - 8 : ROWS]))[7:8], (8, INNER_DEV))
        k["decay"][...] = decay

        @pl.loop(0, BLOCKS)
        def _(i):
            taps = small[S_CONV : S_CONV + 4]
            act = silu(conv_rows(x_pre[rows_at(i, RIM)], taps[:, :INNER_DEV]))
            x_act[rows_at(i)] = act
            xd = (act * spread(dt_buf[rows_at(i)])).astype(BF)
            xd_ref[rows_at(i)] = xd
            tail_x[rows_at(i)] = (xd.astype(F32) * spread(tail[rows_at(i)])).astype(BF)
            bc = conv_rows(bc_pre[rows_at(i, RIM)], taps[:, INNER_DEV : INNER_DEV + 256])
            bc_act[rows_at(i)] = silu(bc).astype(BF)

        b_rows, c_rows = bc_act[:, :STATE], bc_act[:, STATE:]
        if s == 0:
            across[5].start()
        for move in store(s, first_names):
            move.start()
        chain_load(dot_first(b_rows, tail_x[...]), decay, chain_out.at[s])
        copies = spread_send(chain_out.at[s], chain_in.at[s], me, c_sems[0].at[s], c_sems[1].at[s])
        arrive(s, 2)

        @pl.loop(0, 3)
        def _(j):
            z_ref[:, tile_at(j)] = dot(normed[RIM:], zx_w[s, :, tile_at(j)])

        scores[...] = dot_last(c_rows, b_rows)

        def heads_of(half):
            span = (half + 1) * 128
            rows = slice(half * 128, span)
            t = lax.broadcasted_iota(jnp.int32, (128, span), 0) + half * 128
            causal = t >= lax.broadcasted_iota(jnp.int32, (128, span), 1)
            for pair in range(HEADS_DEV // 2):
                parts = []
                for h in (2 * pair, 2 * pair + 1):
                    gap = la_ref[rows, h : h + 1] - la_t_ref[h : h + 1, :span]
                    mixing = scores[rows, :span] * jnp.exp(jnp.where(causal, gap, -1e30))
                    cols = slice(h * HEAD_DIM, (h + 1) * HEAD_DIM)
                    parts.append(dot(mixing.astype(BF), xd_ref[:span, cols]))
                y_ref[rows, pair * 128 : pair * 128 + 128] = jnp.concatenate(parts, axis=1)

        heads_of(0)
        finish(copies)
        chain_scan(True, chain_in.at[s], chain_back.at[s])
        copies = spread_send(chain_back.at[s], chain_got.at[s], me, c_sems[2].at[s], c_sems[3].at[s])
        heads_of(1)
        finish(copies)
        chain_unload(chain_got.at[s], k["state"])

        copies = []
        for half in range(2):
            rows = slice(half * 128, half * 128 + 128)

            @pl.loop(half * BLOCKS // 2, (half + 1) * BLOCKS // 2)
            def _(i):
                at = rows_at(i)
                y = y_ref[at] + spread(jnp.exp(la_ref[at])) * dot(bc_act[at, STATE:], k["state"][...])
                y_ref[at] = y
                ssd = y + small[S_SKIP : S_SKIP + 1, :INNER_DEV] * x_act[at]
                gated = ssd * silu(z_ref[at])
                if s == 0:
                    sq[at] = jnp.broadcast_to(jnp.sum(gated * gated, axis=-1, keepdims=True), (STEP, 128))
                low[at] = (gated * small[S_GATE : S_GATE + 1, :INNER_DEV]).astype(BF)

            if s == 0:
                square_out[half] = sq[rows].T[0:8]
            if half == 0:
                arrive(s, 3)
                if s:
                    for move in store_theirs(core, (bc_w, zx_w, out_w), (bc_t, zx_t, out_t), t_sem):
                        move.start()

            @pl.loop(0, 6)
            def _(j):
                part[rows, tile_at(j)] = dot(low[rows], out_w[s, :, tile_at(j)]).astype(BF)

            if s:
                continue
            batch = []
            for d in range(3):
                src = part.at[rows, quarter(shifted(place, d + 1, 4))]
                sems = s_sems[0].at[half, d], s_sems[1].at[half, d]
                batch.append(send(src, sum_in.at[d, rows], *sems, heads[d]))
                sems = s_sems[0].at[half, d + 3], s_sems[1].at[half, d + 3]
                batch.append(send(square_out.at[half], square_in.at[half, d], *sems, heads[d]))
            copies.append(batch)

        for move in store(s, next_names):
            move.start()
        if s:
            break
        for half in range(2):
            rows = slice(half * 128, half * 128 + 128)
            finish(copies[half])
            square = square_out[half]
            for d in range(3):
                square = square + square_in[half, d]
            column = lax.rsqrt(square * (1.0 / INNER) + EPS).T[:, 0:1]
            k["scale"][rows] = jnp.broadcast_to(column, (128, 128))

            @pl.loop(half * BLOCKS // 2, (half + 1) * BLOCKS // 2)
            def _(i):
                at = rows_at(i)
                total = part[at, quarter(place)].astype(F32)
                for d in range(3):
                    total = total + sum_in[d, at].astype(F32)
                total = (total * k["scale"][at][:, 0:1]).astype(BF)
                sum_own[at] = total
                k["out"][at, quarter(place)] = total

            copies[half] = []
            for d in range(3):
                sems = s_sems[2].at[half, d], s_sems[3].at[half, d]
                dst = k["out"].at[rows, quarter(place)]
                copies[half].append(send(sum_own.at[rows], dst, *sems, heads[d]))
        edge = slice(ROWS - RIM, ROWS)
        next_own[...] = (v_buf[edge, quarter(place)].astype(F32) + sum_own[edge].astype(F32)).astype(BF)
        rim_in = []
        for d in range(4):
            dst = rim_buf.at[1, :, quarter(place)]
            target = {"head": shifted(place, d, 4), "seq": later}
            rim_in.append(send(next_own, dst, rim_send.at[1 + d], rim_recv.at[1 + d], target))
        for half in range(2):
            finish(copies[half])

            @pl.loop(half * 8, half * 8 + 8)
            def _(i):
                at = pl.ds(pl.multiple_of(i * 16, 16), 16)
                following = (v_buf[at].astype(F32) + k["out"][at].astype(F32)).astype(BF)
                k["following"][at] = following
                at = pl.ds(pl.multiple_of(i * 16 + RIM, 16), 16)
                kept[1]["normed"][at] = norm_rows(following, small_w[1, S_NORM : S_NORM + 1])

        for move in store(s, last_names):
            move.start()

    store_part = pltpu.make_async_copy(part, part_ref, v_sem)
    store_part.start()
    finish(store(0, first_names + next_names + last_names))
    finish(store(1, first_names + next_names))
    store_part.wait()
    for i in (0, 1, 2, 4, 5):
        across[i].wait_send()
    for move in store_theirs(core, (bc_w, zx_w, out_w), (bc_t, zx_t, out_t), t_sem):
        move.wait()


def store_theirs(core, held, dst, sem):
    return [
        pltpu.make_async_copy(held[i].at[1 - core], dst[i], sem.at[i]) for i in range(3)
    ]


def forward(x_in, zx_m, bc_m, out_m, dt_m, smalls, number):
    dma = pltpu.SemaphoreType.DMA
    sds = jax.ShapeDtypeStruct
    vm = pltpu.VMEM
    got = pl.pallas_call(
        forward_kernel,
        out_shape=[sds(shape, kind) for _, shape, kind in KEPT * 2]
        + [sds(zx_m.shape, BF), sds(bc_m.shape, BF), sds(out_m.shape, BF)]
        + [sds((2, 16, WIDTH), F32), sds((2, 128, WIDTH), BF), sds((ROWS, WIDTH), BF)],
        in_specs=[ANY] * 4 + [VM] * 8,
        out_specs=[ANY] * 35 + [VM] * 2 + [ANY],
        scratch_shapes=[
            vm((ROWS, WIDTH), BF),
            vm((2, RIM, WIDTH), BF),
            vm((2, WIDTH, WIDTH), BF),
            vm((2, WIDTH, 256), BF),
            vm((2, INNER_DEV, WIDTH), BF),
            vm((ROWS, INNER_DEV), BF),
            vm((ROWS, ROWS), F32),
            vm((ROWS, 128), F32),
            vm((ROWS, 128), F32),
            vm((ROWS, INNER_DEV), BF),
            vm((ROWS, 128), F32),
            vm((ROWS, WIDTH), BF),
            vm((2, 16, 16, 512), BF),
            vm((2, 16, 16, 512), BF),
            vm((2, 16, 16, 384), BF),
            vm((2, 16, 16, 384), BF),
            vm((3, ROWS, 384), BF),
            vm((2, 8, 128), F32),
            vm((2, 3, 8, 128), F32),
            vm((ROWS, 384), BF),
            vm((RIM, 384), BF),
            dma((6,)),
            dma((6,)),
            dma((4,)),
            dma((5,)),
            dma((5,)),
            dma((2, 16)),
            dma((2, 16)),
            dma((2, 16)),
            dma((2, 16)),
            dma((2, 6)),
            dma((2, 6)),
            dma((2, 3)),
            dma((2, 3)),
            dma((3,)),
            dma,
            dma((2, len(KEPT))),
        ]
        + [vm(shape, kind) for _, shape, kind in KEPT * 2],
        compiler_params=comm_params(number),
        name="forward_layers",
    )(x_in, zx_m, bc_m, out_m, dt_m, *smalls)
    kept = [{name: got[16 * s + i] for i, (name, _, _) in enumerate(KEPT)} for s in range(2)]
    return kept, got[32:38]


PART = 48
EARLY, WIDE = 2 * PART, 3 * PART
SUB = WIDE + 16
GROUPS = (((0, PART), (PART, EARLY)), ((EARLY, EARLY + 32), (EARLY + 32, SUB)))
REST = 32
SLOT = ("z", "x_pre", "bc_pre", "dt_pre", "la", "la_t", "xd", "bc_act", "x_act", "y", "decay", "state", "scale", "out")
SHAPES = {name: (shape, kind) for name, shape, kind in KEPT}


def add_rows(total, more):
    return total.astype(F32) + more.astype(F32)


def backward_kernel(*refs):
    cot_ref, x_ref, part_ref = refs[:3]
    held = (refs[3:6], refs[6:9])
    small_all, dt_all = refs[9:11]
    saved = [{name: refs[11 + 16 * s + i] for i, (name, _, _) in enumerate(KEPT)} for s in range(2)]
    grads_ref, rest_ref, section_ref, leaving_ref = refs[43:47]
    rest = list(refs[47:])

    def take(count):
        got = rest[:count]
        del rest[:count]
        return got

    k = dict(zip(SLOT, take(len(SLOT))))
    normed_all, v_all, d_v, g_o_buf = take(4)
    zx_w, bc_w, out_w = take(3)
    own, spare, theirs, first, mid, second, ring = take(7)
    d_y_ref, d_z_ref, d_xd, d_y_low, wide_x, wide_y = take(6)
    scores_t, d_scores_t, d_bc, terms, direct, tail_ref, dt_ref = take(7)
    ext, d_zx, d_bd, part, sum_in, d_normed_ref, sum_own = take(7)
    chain_out, chain_in, chain_back, chain_got, state_grad = take(5)
    rim_buf, taps_ref, bc_out, bc_in, norm_ref, sums_ref, small_rows = take(7)
    rest_out, rest_cross, rest_near, rest_far, rest_low = take(5)
    k_sem, n_sem, w_sem, move_sem = take(4)
    c_sems, s_sems, rim_sems, swap_sems = take(4), take(4), take(2), take(2)
    cross_sems, one_sems, two_sems, back_sems, last_sems = take(2), take(2), take(2), take(2), take(2)
    bc_sems, rest_sems = take(2), take(2)
    row_out, row_in, final_in, final_own = take(4)
    row_sems, final_sems = take(2), take(4)
    theirs_free, first_free = take(2)

    core, me, place = lax.axis_index("section"), lax.axis_index("seq"), lax.axis_index("head")
    x, z = lax.div(me, 4), lax.rem(me, 4)
    along_z = [x * 4 + shifted(z, d, 4) for d in range(1, 4)]
    along_x = [shifted(x, d, 4) * 4 + z for d in range(1, 4)]
    ways = ((x, z, along_z, along_x), (z, x, along_x, along_z))
    other = {"section": 1 - core}
    heads = [{"head": shifted(place, d, 4)} for d in range(1, 4)]
    targets = [other] + [{"seq": shifted(me, d, 16)} for d in range(1, 16)] + heads
    targets += [{"section": 1 - core, "seq": seq} for seq in along_z + along_x]
    targets += [{"section": 1 - core, "head": shifted(place, d, 4)} for d in range(1, 4)]
    barrier = pltpu.get_barrier_semaphore()
    for target in targets:
        pl.semaphore_signal(barrier, inc=1, device_id=target, device_id_type=MESH)

    def load_kept(s):
        return [
            pltpu.make_async_copy(saved[s][name], k[name], k_sem.at[i])
            for i, name in enumerate(SLOT)
            if s == 0 or name not in ("scale", "out")
        ]

    def load_rows(s):
        source = x_ref.at[core] if s == 0 else saved[0]["following"]
        return [
            pltpu.make_async_copy(saved[s]["normed"], normed_all.at[s], n_sem.at[s, 0]),
            pltpu.make_async_copy(source, v_all.at[s], n_sem.at[s, 1]),
        ]

    weight_slots = (zx_w, bc_w, out_w)

    def load_weight(s, i):
        @pl.when(core == s)
        def _():
            pltpu.make_async_copy(held[0][i], weight_slots[i], w_sem.at[i]).start()

        @pl.when(core != s)
        def _():
            pltpu.make_async_copy(held[1][i], weight_slots[i], w_sem.at[i]).start()

    def wait_weight(i):
        pltpu.make_async_copy(held[0][i], weight_slots[i], w_sem.at[i]).wait()

    load_g_o = pltpu.make_async_copy(cot_ref.at[core], g_o_buf, n_sem.at[0, 2])
    load_g_o.start()
    load_weight(1, 2)
    for move in load_kept(1):
        move.start()
    load_weight(1, 0)
    load_weight(1, 1)
    for s in (1, 0):
        for move in load_rows(s):
            move.start()

    small_rows[...] = jnp.zeros_like(small_rows)
    def swapped(i, src, dst):
        return pltpu.make_async_remote_copy(
            src_ref=src,
            dst_ref=dst.at[core],
            send_sem=swap_sems[0].at[i],
            recv_sem=swap_sems[1].at[i],
            device_id=other,
            device_id_type=MESH,
        )

    def final(d, micro):
        return pltpu.make_async_remote_copy(
            src_ref=final_own,
            dst_ref=section_ref.at[micro, :, quarter(place)],
            send_sem=final_sems[2].at[d],
            recv_sem=final_sems[3].at[micro, d],
            device_id={"section": 1, "head": shifted(place, d + 1, 4)},
            device_id_type=MESH,
        )

    def final_stay():
        return pltpu.make_async_copy(final_own, section_ref.at[1, :, quarter(place)], move_sem.at[0])

    def cross(s, piece):
        lo, hi = GROUPS[piece][0][0], GROUPS[piece][1][1]
        return pltpu.make_async_remote_copy(
            src_ref=spare.at[:, :, lo:hi],
            dst_ref=theirs.at[:, :, lo:hi],
            send_sem=cross_sems[0].at[s, piece],
            recv_sem=cross_sems[1].at[s, piece],
            device_id=other,
            device_id_type=MESH,
        )

    def reduction(s, group):
        parts = [(n, lo, hi) + ways[n] for n, (lo, hi) in enumerate(GROUPS[group])]
        low, high = parts[0][1], parts[1][2]
        cross(s, group).wait_recv()

        @pl.loop(0, 4)
        def _(i):
            @pl.loop(0, 4)
            def _(j):
                own[s, i, j, low:high] = own[s, i, j, low:high] + theirs[i, j, low:high]

        if s == 0:
            pl.semaphore_wait(first_free.at[group], 6)
        copies = []
        for d in range(3):
            for n, lo, hi, a, b, near, far in parts:
                src = own.at[s, :, shifted(b, d + 1, 4), lo:hi]
                dst = first.at[d, :, lo:hi]
                sems = one_sems[0].at[s, group, n, d], one_sems[1].at[s, group, n, d]
                copies.append(send(src, dst, *sems, {"seq": near[d]}))
        yield
        finish(copies)

        @pl.loop(0, 4)
        def _(i):
            for n, lo, hi, a, b, near, far in parts:
                total = own[s, i, b, lo:hi].astype(F32)
                for d in range(3):
                    total = total + first[d, i, lo:hi].astype(F32)
                mid[i, lo:hi] = total.astype(BF)

        copies = []
        for d in range(3):
            for n, lo, hi, a, b, near, far in parts:
                src = mid.at[shifted(a, d + 1, 4), lo:hi]
                dst = second.at[s, d, lo:hi]
                sems = two_sems[0].at[s, group, n, d], two_sems[1].at[s, group, n, d]
                copies.append(send(src, dst, *sems, {"seq": far[d]}))
        yield
        finish(copies)
        copies = []
        for n, lo, hi, a, b, near, far in parts:
            total = mid[a, lo:hi].astype(F32)
            for d in range(3):
                total = total + second[s, d, lo:hi].astype(F32)
            ring[s, a, lo:hi] = total.astype(BF)
            for d in range(3):
                block = ring.at[s, a, lo:hi]
                sems = back_sems[0].at[s, group, n, d], back_sems[1].at[s, group, n, d]
                copies.append(send(block, block, *sems, {"seq": far[d]}))
        yield
        finish(copies)

        def last(part, d, half):
            n, lo, hi, a, b, near, far = part
            return pltpu.make_async_remote_copy(
                src_ref=ring.at[s, :, lo:hi],
                dst_ref=grads_ref.at[half, :, b, lo:hi],
                send_sem=last_sems[0].at[s, group, n, d],
                recv_sem=last_sems[1].at[s, group, n, half, d],
                device_id={"section": s, "seq": near[d] if d < 3 else me},
                device_id_type=MESH,
            )

        def stay(part):
            n, lo, hi, a, b, near, far = part
            sem = last_sems[0].at[s, group, n, 3]
            return pltpu.make_async_copy(ring.at[s, :, lo:hi], grads_ref.at[core, :, b, lo:hi], sem)

        for d in range(3):
            for part in parts:
                last(part, d, core).start()

        @pl.when(core == s)
        def _():
            for part in parts:
                stay(part).start()

        @pl.when(core != s)
        def _():
            for part in parts:
                last(part, 3, core).start()

        yield
        for part in parts:
            for d in range(3):
                last(part, d, core).wait_send()

        @pl.when(core == s)
        def _():
            for part in parts:
                stay(part).wait()
                for d in range(3):
                    last(part, d, s).wait_recv()
                for d in range(4):
                    last(part, d, 1 - s).wait_recv()

        @pl.when(core != s)
        def _():
            for part in parts:
                last(part, 3, core).wait_send()

        yield

    def reduction_rest(s):
        def move(src, dst, i, target):
            return send(src, dst, rest_sems[0].at[s, i], rest_sems[1].at[s, i], target)

        def gather(bufs, first_sem, peers):
            return [move(rest_low.at[s], bufs.at[s, d], first_sem + d, {"seq": peers[d]}) for d in range(3)]

        copy = move(rest_out.at[1 - core], rest_cross.at[s], 0, other)
        yield
        copy.wait()
        total = add_rows(rest_out[core], rest_cross[s])
        rest_low[s] = total.astype(BF)
        copies = gather(rest_near, 1, along_z)
        yield
        finish(copies)
        for d in range(3):
            total = total + rest_near[s, d].astype(F32)
        rest_low[s] = total.astype(BF)
        copies = gather(rest_far, 4, along_x)
        yield
        finish(copies)
        for d in range(3):
            total = total + rest_far[s, d].astype(F32)
        rest_low[s] = total.astype(BF)

        def deliver():
            return pltpu.make_async_remote_copy(
                src_ref=rest_low.at[s],
                dst_ref=rest_ref.at[core],
                send_sem=rest_sems[0].at[s, 7],
                recv_sem=rest_sems[1].at[s, 7],
                device_id=other,
                device_id_type=MESH,
            )

        @pl.when(core != s)
        def _():
            deliver().start()

        @pl.when(core == s)
        def _():
            rest_ref[core] = rest_low[s]

        yield

        @pl.when(core != s)
        def _():
            deliver().wait_send()

        @pl.when(core == s)
        def _():
            deliver().wait_recv()

        yield

    member_rows = lax.broadcasted_iota(jnp.int32, (INNER_DEV, 128), 0)
    member_lanes = lax.broadcasted_iota(jnp.int32, (INNER_DEV, 128), 1) * HEAD_DIM
    inside = (member_rows >= member_lanes) & (member_rows < member_lanes + HEAD_DIM)
    member = jnp.where(inside, 1.0, 0.0).astype(BF)

    def sums_of(value):
        high, low = two_part(value)
        return dot(high, member) + dot(low, member)

    half_rows = [
        [pl.ds(pl.multiple_of(h * INNER_DEV + 384 * j, 384), 384) for j in range(2)] for h in (core, 1 - core)
    ]
    half_cols = [pl.ds(pl.multiple_of(h * INNER_DEV, INNER_DEV), INNER_DEV) for h in (core, 1 - core)]
    early, late, loose = None, None, None
    old_early, old_late = None, None
    load_g_o.wait()
    for s in (1, 0):
        small = small_all.at[s]
        normed, v_ref = normed_all.at[s], v_all.at[s]
        g_o_ref = g_o_buf if s else d_v.at[1]
        y_ref, z_ref, la_ref, la_t_ref = k["y"], k["z"], k["la"], k["la_t"]
        xd_ref, bc_act, x_act = k["xd"], k["bc_act"], k["x_act"]
        x_pre, bc_pre = k["x_pre"], k["bc_pre"]
        stages = (own.at[s], spare)

        sums_ref[...] = jnp.zeros_like(sums_ref)
        wait_weight(2)

        @pl.loop(0, 3)
        def _(j):
            d_xd[:, tile_at(j)] = dot_last(g_o_ref[...], out_w[tile_at(j), :])

        if s:
            load_weight(0, 2)
        finish(load_kept(s))
        if s:
            finish(load_rows(1))

            @pl.loop(0, BLOCKS)
            def _(i):
                at = rows_at(i)
                gain = small[S_GATE : S_GATE + 1, :INNER_DEV]
                ssd = y_ref[at] + small[S_SKIP : S_SKIP + 1, :INNER_DEV] * x_act[at]
                gated = ssd * silu(z_ref[at])
                square = jnp.sum(gated * gated, axis=-1, keepdims=True)
                mean = jnp.sum(gated * gain * d_xd[at], axis=-1, keepdims=True)
                lane = lax.broadcasted_iota(jnp.int32, (STEP, 128), 1)
                tail_ref[at] = jnp.where(lane == 0, square, mean)

            row_out[...] = tail_ref[...].T[0:8]
            pl.semaphore_wait(barrier, len(targets))
            copies = [
                send(row_out, row_in.at[d], row_sems[0].at[d], row_sems[1].at[d], heads[d]) for d in range(3)
            ]
            final_copies = []
            for d in range(3):
                src = part_ref.at[:, quarter(shifted(place, d + 1, 4))]
                sems = final_sems[0].at[d], final_sems[1].at[d]
                final_copies.append(send(src, final_in.at[d], *sems, heads[d]))
            load_final = pltpu.make_async_copy(part_ref.at[:, quarter(place)], final_own, move_sem.at[0])
            load_final.start()
            finish(copies)
            total = row_out[...]
            for d in range(3):
                total = total + row_in[d]
            total = jnp.concatenate([total] * 16, axis=0).T
            scale = lax.rsqrt(total[:, 0:1] * (1.0 / INNER) + EPS)
            mean = total[:, 1:2] * scale * scale * scale * (1.0 / INNER)
            lane = lax.broadcasted_iota(jnp.int32, (ROWS, 128), 1)
            k["scale"][...] = jnp.where(lane == 0, scale, mean)

        @pl.loop(0, BLOCKS)
        def _(i):
            at = rows_at(i)
            gain = small[S_GATE : S_GATE + 1, :INNER_DEV]
            scale = k["scale"][at][:, 0:1]
            act, gate, dm = x_act[at], z_ref[at], d_xd[at]
            ssd = y_ref[at] + small[S_SKIP : S_SKIP + 1, :INNER_DEV] * act
            sigma = jax.nn.sigmoid(gate)
            gate_silu = gate * sigma
            gated = ssd * gate_silu
            scaled = gated * scale
            if s:
                mean = k["scale"][at][:, 1:2]
            else:
                mean = jnp.sum(g_o_ref[at].astype(F32) * k["out"][at].astype(F32), axis=-1, keepdims=True)
                mean = mean * scale * scale * (1.0 / INNER)
            wide_x[at] = (scaled * gain).astype(BF)
            d_gated = scale * gain * dm - gated * mean
            d_y = d_gated * gate_silu
            d_y_ref[at] = d_y
            d_y_low[at] = d_y.astype(BF)
            d_z_ref[at] = (d_gated * ssd * sigma * (1.0 + gate * (1.0 - sigma))).astype(BF)
            wide_y[at] = (spread(jnp.exp(la_ref[at])) * d_y).astype(BF)
            sums_ref[0:1] += jnp.sum(scaled * dm, axis=0, keepdims=True)
            sums_ref[1:2] += jnp.sum(d_y * act, axis=0, keepdims=True)

        b_rows, c_rows = bc_act[:, :STATE], bc_act[:, STATE:]
        chain_load(dot_first(c_rows, wide_y[...]), k["decay"], chain_out)
        copies = spread_send(chain_out, chain_in, me, c_sems[0].at[s], c_sems[1].at[s])
        if s:

            @pl.when(core == 1)
            def _():
                swapped(0, saved[0]["following"], section_ref).start()

        if s == 0:
            for piece in range(2):
                cross(1, piece).wait_send()
        for stage, cols, rows in zip(stages, half_cols, half_rows):
            for j in range(2):
                got = dot_first(wide_x[:, 384 * j : 384 * j + 384], g_o_ref[:, cols]).astype(BF)
                for i in range(8):
                    sub = 8 * j + i
                    stage[sub // 4, sub % 4, 0:PART] = got[PART * i : PART * i + PART]
            for j in range(2):
                got = dot_first(normed[RIM:, rows[j]], d_z_ref[...]).astype(BF)
                for i in range(8):
                    sub = 8 * j + i
                    stage[sub // 4, sub % 4, PART:EARLY] = got[PART * i : PART * i + PART]
        if s == 0:
            pl.semaphore_wait(theirs_free, 1)
        cross(s, 0).start()
        if s == 0:
            next(late)
            for seq in along_z + along_x:
                pl.semaphore_signal(first_free.at[1], inc=1, device_id={"seq": seq}, device_id_type=MESH)
            next(loose)

        la = la_ref[...]
        tail_ref[...] = jnp.exp(la[ROWS - 1 : ROWS] - la)
        dt_in = k["dt_pre"][...] + small[S_BIAS : S_BIAS + 1, :128]
        dt_ref[...] = softplus(dt_in)
        scores_t[...] = dot_last(b_rows, c_rows)

        def heads_of(half):
            base = half * 128
            rows = slice(base, base + 128)
            t = lax.broadcasted_iota(jnp.int32, (128, ROWS - base), 1)
            later = t >= lax.broadcasted_iota(jnp.int32, (128, ROWS - base), 0)
            total = jnp.zeros((128, ROWS - base), F32)
            for pair in range(HEADS_DEV // 2):
                parts = []
                for h in (2 * pair, 2 * pair + 1):
                    cols = slice(h * HEAD_DIM, (h + 1) * HEAD_DIM)
                    gap = la_t_ref[h : h + 1, base:] - la_ref[rows, h : h + 1]
                    decay = jnp.exp(jnp.where(later, gap, -1e30))
                    total = total + decay * dot_last(xd_ref[rows, cols], d_y_low[base:, cols])
                    mixing = (scores_t[rows, base:] * decay).astype(BF)
                    parts.append(dot(mixing, d_y_low[base:, cols]))
                d_xd[rows, pair * 128 : pair * 128 + 128] = jnp.concatenate(parts, axis=1)
            if half:
                d_scores_t[rows, 0:128] = jnp.zeros((128, 128), BF)
            d_scores_t[rows, base:] = total.astype(BF)

        heads_of(0)
        finish(copies)
        chain_scan(False, chain_in, chain_back)
        copies = spread_send(chain_back, chain_got, me, c_sems[2].at[s], c_sems[3].at[s])
        old_early, early = early, reduction(s, 0)
        next(early)
        heads_of(1)
        finish(copies)
        if s == 0:
            next(late)
            next(loose)
        if s:
            load_final.wait()
            finish(final_copies)

            @pl.loop(0, BLOCKS)
            def _(i):
                at = rows_at(i)
                total = final_own[at].astype(F32)
                for d in range(3):
                    total = total + final_in[d, at].astype(F32)
                total = (total * k["scale"][at][:, 0:1]).astype(BF).astype(F32)
                final_own[at] = (v_ref[at, quarter(place)].astype(F32) + total).astype(BF)

            for d in range(3):
                final(d, core).start()

            @pl.when(core == 1)
            def _():
                final_stay().start()

            @pl.when(core == 0)
            def _():
                final(3, core).start()
                pltpu.make_async_copy(v_all.at[1], section_ref.at[0], move_sem.at[0]).start()

        chain_unload(chain_got, state_grad)
        norm_ref[...] = jnp.zeros_like(norm_ref)
        taps_ref[...] = jnp.zeros_like(taps_ref)

        @pl.loop(0, BLOCKS)
        def _(i):
            at = rows_at(i)
            tail = spread(tail_ref[at])
            xd = xd_ref[at].astype(F32)
            wide_x[at] = (tail * xd).astype(BF)
            state_part = tail * dot(bc_act[at, :STATE], state_grad[...])
            got = d_xd[at] + state_part
            d_xd[at] = got
            norm_ref[1:2, :INNER_DEV] += jnp.sum(xd * state_part, axis=0, keepdims=True)
            terms[at] = sums_of(d_y_low[at].astype(F32) * y_ref[at] - xd * got)
            direct[at] = sums_of(x_act[at] * got)

        d_bc[:, :STATE] = dot(d_scores_t[...], c_rows) + dot_last(wide_x[...], state_grad[...])
        d_bc[:, STATE:] = dot_first(d_scores_t[...], b_rows) + dot_last(wide_y[...], k["state"][...])
        end_wide = spread(jnp.exp(la[ROWS - 8 : ROWS]))[7:8]
        both = state_grad[...].astype(F32) * k["state"][...].astype(F32)
        tail_sum = norm_ref[1:2, :INNER_DEV] + end_wide * jnp.sum(both, axis=0, keepdims=True)
        tail_sum = sums_of(jnp.broadcast_to(tail_sum, (16, INNER_DEV)))[0:1]

        @pl.loop(0, BLOCKS)
        def _(i):
            at = rows_at(i)
            taps = small[S_CONV : S_CONV + 4, INNER_DEV : INNER_DEV + 256]
            d_bcc = d_bc[at] * silu_slope(conv_rows(bc_pre[rows_at(i, RIM)], taps))
            d_bc[at] = d_bcc
            bc_out[at] = d_bcc.astype(BF)

        copies = [
            send(bc_out, bc_in.at[d], bc_sems[0].at[s, d], bc_sems[1].at[s, d], heads[d]) for d in range(3)
        ]
        d_log = running(terms[...], True) + tail_sum
        rate = small[S_RATE : S_RATE + 1, :128]
        d_dt = direct[...] + rate * d_log
        d_dt_pre = d_dt * jax.nn.sigmoid(dt_in)
        d_bd[:, 256:] = d_dt_pre.astype(BF)
        sums_ref[2:3, :128] = jnp.sum(dt_ref[...] * d_log, axis=0, keepdims=True) * rate
        sums_ref[3:4, :128] = jnp.sum(d_dt_pre, axis=0, keepdims=True)

        @pl.loop(0, BLOCKS)
        def _(i):
            at = rows_at(i)
            taps = small[S_CONV : S_CONV + 4]
            pre = x_pre[rows_at(i, RIM)]
            d_x = spread(dt_ref[at]) * d_xd[at] + small[S_SKIP : S_SKIP + 1, :INNER_DEV] * d_y_ref[at]
            d_xc = d_x * silu_slope(conv_rows(pre, taps[:, :INNER_DEV]))
            ext[at, :INNER_DEV] = d_xc
            for t in range(4):
                moved = pre[RIM - 3 + t : RIM - 3 + t + STEP]
                taps_ref[t : t + 1, :INNER_DEV] += jnp.sum(moved * d_xc, axis=0, keepdims=True)

        finish(copies)

        @pl.loop(0, BLOCKS)
        def _(i):
            at = rows_at(i)
            d_bcc = d_bc[at]
            for d in range(3):
                d_bcc = d_bcc + bc_in[d, at].astype(F32)
            ext[at, INNER_DEV:] = d_bcc
            pre = bc_pre[rows_at(i, RIM)]
            for t in range(4):
                moved = pre[RIM - 3 + t : RIM - 3 + t + STEP]
                taps_ref[t : t + 1, INNER_DEV:] += jnp.sum(moved * d_bcc, axis=0, keepdims=True)

        rim = send(
            ext.at[0:8], rim_buf, rim_sems[0].at[s], rim_sems[1].at[s], {"seq": shifted(me, -1, 16)}
        )
        if s:
            for move in load_kept(0):
                move.start()

        if s == 0:
            next(loose)
            next(late)
        else:
            next(early)
            for seq in along_z + along_x:
                pl.semaphore_signal(first_free.at[0], inc=1, device_id={"seq": seq}, device_id_type=MESH)
        rim.wait()

        @pl.when(me == 15)
        def _():
            rim_buf[...] = jnp.zeros_like(rim_buf)

        ext[ROWS : ROWS + 8] = rim_buf[...]

        @pl.loop(0, BLOCKS)
        def _(i):
            at = rows_at(i)
            taps = small[S_CONV : S_CONV + 4]
            block = ext[rows_at(i, 8)]
            d_pre = taps[0:1, : INNER_DEV + 256] * block[3 : 3 + STEP]
            for t in range(1, 4):
                d_pre = d_pre + taps[t : t + 1, : INNER_DEV + 256] * block[3 - t : 3 - t + STEP]
            d_zx[at, :INNER_DEV] = d_z_ref[at]
            d_zx[at, INNER_DEV:] = d_pre[:, :INNER_DEV].astype(BF)
            d_bd[at, :256] = d_pre[:, INNER_DEV:].astype(BF)

        wait_weight(0)
        wait_weight(1)

        @pl.loop(0, 6)
        def _(j):
            got = dot_last(d_zx[...], zx_w[tile_at(j), :])
            got = got + dot_last(d_bd[:, :256], bc_w[tile_at(j), :]) * 0.25
            got = got + dot(d_bd[:, 256:], dt_all[s, :, tile_at(j)])
            part[:, tile_at(j)] = got.astype(BF)

        if s:
            load_weight(0, 0)
            load_weight(0, 1)
        copies = []
        for d in range(1, 4):
            src = part.at[:, quarter(shifted(place, d, 4))]
            copies.append(send(src, sum_in.at[d - 1], s_sems[0].at[s, d], s_sems[1].at[s, d], heads[d - 1]))
        for stage, rows in zip(stages, half_rows):
            for j in range(2):
                got = dot_first(normed[RIM:, rows[j]], d_zx[:, INNER_DEV:]).astype(BF)
                for i in range(8):
                    sub = 8 * j + i
                    stage[sub // 4, sub % 4, EARLY:WIDE] = got[PART * i : PART * i + PART]

        for n, (stage, cols) in enumerate(zip(stages, half_cols)):
            got = dot_first(d_bd[...], normed[RIM:, cols])
            for i in range(16):
                stage[i // 4, i % 4, WIDE:SUB] = got[16 * i : 16 * i + 16].astype(BF)
            rest_out[core if n == 0 else 1 - core, 0:16] = got[256:272].astype(BF)
        cross(s, 1).start()
        next(early)
        finish(copies)

        @pl.loop(0, BLOCKS)
        def _(i):
            at = rows_at(i)
            total = part[at, quarter(place)].astype(F32)
            for d in range(3):
                total = total + sum_in[d, at].astype(F32)
            total = total.astype(BF)
            sum_own[at] = total
            d_normed_ref[at, quarter(place)] = total

        copies = []
        for d in range(1, 4):
            dst = d_normed_ref.at[:, quarter(place)]
            copies.append(send(sum_own, dst, s_sems[2].at[s, d], s_sems[3].at[s, d], heads[d - 1]))
        old_late, late = late, reduction(s, 1)
        next(early)
        if s == 0:
            next(late)
        finish(copies)
        if s == 0:
            next(early)
        norm_ref[...] = jnp.zeros_like(norm_ref)

        @pl.loop(0, BLOCKS)
        def _(i):
            at = rows_at(i)
            v = v_ref[at].astype(F32)
            scale = lax.rsqrt(jnp.mean(v * v, axis=-1, keepdims=True) + EPS)
            d_normed = d_normed_ref[at].astype(F32)
            scaled = v * scale
            norm_ref[0:1] += jnp.sum(scaled * d_normed, axis=0, keepdims=True)
            weighted = d_normed * small[S_NORM : S_NORM + 1]
            mean = jnp.mean(v * weighted, axis=-1, keepdims=True) * scale * scale
            d_v[s, at] = (scale * weighted - scaled * mean + g_o_ref[at].astype(F32)).astype(BF)

        for h in range(2):
            small_rows[h, 0:1] = norm_ref[0:1, h * INNER_DEV : (h + 1) * INNER_DEV]
            small_rows[h, 1:5] = taps_ref[0:4, :INNER_DEV]
            small_rows[h, 5:9] = sums_ref[0:4]
            small_rows[h, 9:13, 0:256] = taps_ref[0:4, INNER_DEV:]
            rest_out[h, 16:] = small_rows[h].astype(BF)
        old_loose, loose = loose, reduction_rest(s)
        next(loose)
        if s:
            next(late)
            pl.semaphore_signal(theirs_free, inc=1, device_id=other, device_id_type=MESH)

        @pl.when(core == 1 - s)
        def _():
            swapped(1, d_v.at[s], leaving_ref).start()

        @pl.when(core == s)
        def _():
            pltpu.make_async_copy(d_v.at[s], leaving_ref.at[s], move_sem.at[1]).start()

        if s:
            finish(load_rows(0))

    for turn in (loose, late, loose, late, loose, late, loose, early, late, old_early, old_late, old_loose):
        next(turn)
    for piece in range(2):
        cross(0, piece).wait_send()
    for d in range(3):
        final(d, core).wait_send()

    @pl.when(core == 0)
    def _():
        swapped(0, d_v.at[0], section_ref).wait_recv()
        pltpu.make_async_copy(v_all.at[1], section_ref.at[0], move_sem.at[0]).wait()
        final(3, core).wait_send()

    @pl.when(core == 1)
    def _():
        swapped(0, saved[0]["following"], section_ref).wait_send()
        final_stay().wait()
        for d in range(3):
            final(d, 1).wait_recv()
        for d in range(4):
            final(d, 0).wait_recv()

    swapped(1, d_v.at[0], leaving_ref).wait()
    pltpu.make_async_copy(d_v.at[0], leaving_ref.at[0], move_sem.at[1]).wait()


def backward(cotangent, x_in, part, held, smalls, dt_all, kept, number):
    dma = pltpu.SemaphoreType.DMA
    regular = pltpu.SemaphoreType.REGULAR
    sds = jax.ShapeDtypeStruct
    vm = pltpu.VMEM
    halves = (4, 4, SUB, INNER_DEV)
    rows_low = vm((ROWS, INNER_DEV), BF)
    rows_wide = vm((ROWS, INNER_DEV), F32)
    steps = vm((ROWS, 128), F32)
    scratch = [vm(*SHAPES[name]) for name in SLOT]
    scratch += [
        vm((2, ROWS + RIM, WIDTH), BF),
        vm((2, ROWS, WIDTH), BF),
        vm((2, ROWS, WIDTH), BF),
        vm((ROWS, WIDTH), BF),
        vm((WIDTH, WIDTH), BF),
        vm((WIDTH, 256), BF),
        vm((INNER_DEV, WIDTH), BF),
        vm((2,) + halves, BF),
        vm(halves, BF),
        vm(halves, BF),
        vm((3, 4, SUB, INNER_DEV), BF),
        vm((4, SUB, INNER_DEV), BF),
        vm((2, 3, SUB, INNER_DEV), BF),
        vm((2, 4, SUB, INNER_DEV), BF),
        rows_wide, rows_low, rows_wide, rows_low, rows_low, rows_low,
        vm((ROWS, ROWS), F32),
        vm((ROWS, ROWS), BF),
        vm((ROWS, 256), F32),
        steps, steps, steps, steps,
        vm((ROWS + 8, INNER_DEV + 256), F32),
        vm((ROWS, WIDTH), BF),
        vm((ROWS, 384), BF),
        vm((ROWS, WIDTH), BF),
        vm((3, ROWS, 384), BF),
        vm((ROWS, WIDTH), BF),
        vm((ROWS, 384), BF),
        vm((16, 16, 512), BF),
        vm((16, 16, 512), BF),
        vm((16, 16, 384), BF),
        vm((16, 16, 384), BF),
        vm((STATE, INNER_DEV), BF),
        vm((8, INNER_DEV + 256), F32),
        vm((8, INNER_DEV + 256), F32),
        vm((ROWS, 256), BF),
        vm((3, ROWS, 256), BF),
        vm((8, WIDTH), F32),
        vm((8, INNER_DEV), F32),
        vm((2, 16, INNER_DEV), F32),
        vm((2, REST, INNER_DEV), BF),
        vm((2, REST, INNER_DEV), BF),
        vm((2, 3, REST, INNER_DEV), BF),
        vm((2, 3, REST, INNER_DEV), BF),
        vm((2, REST, INNER_DEV), BF),
        dma((len(SLOT),)),
        dma((2, 3)),
        dma((3,)),
        dma((2,)),
    ]
    scratch += [dma((2, 16))] * 4 + [dma((2, 8))] * 2 + [dma((2, 4))] * 2
    scratch += [dma((2,))] * 4 + [dma((2, 2))] * 2
    scratch += [dma((2, 2, 2, 4))] * 7 + [dma((2, 2, 2, 2, 4))]
    scratch += [dma((2, 3))] * 2 + [dma((2, 8))] * 2
    scratch += [vm((8, ROWS), F32), vm((3, 8, ROWS), F32), vm((3, ROWS, 384), BF), vm((ROWS, 384), BF)]
    scratch += [dma((3,))] * 4 + [dma((4,)), dma((2, 4)), regular, regular((2,))]
    flat = [kept[s][name] for s in range(2) for name, _, _ in KEPT]
    return pl.pallas_call(
        backward_kernel,
        out_shape=[
            sds((2,) + halves, BF),
            sds((2, REST, INNER_DEV), BF),
            sds((2, ROWS, WIDTH), BF),
            sds((2, ROWS, WIDTH), BF),
        ],
        in_specs=[ANY] * 9 + [VM] * 2 + [ANY] * 32,
        out_specs=[ANY, VM, ANY, ANY],
        scratch_shapes=scratch,
        compiler_params=comm_params(number),
        name="backward_layers",
    )(cotangent, x_in, part, *held, smalls, dt_all, *flat)


def widen_kernel(
    a_ref, rest_ref, zx_ref, out_ref, bc_ref, dt_ref, norm_ref, bias_ref, rate_ref, skip_ref, conv_ref, conv_bc_ref,
    gate_ref, bc_all, wide, sem,
):
    step = pl.program_id(0)
    slot = lax.rem(step, 2)

    def moves(step, slot):
        return [
            pltpu.make_async_copy(
                wide.at[slot, h, kind],
                zx_ref.at[pl.ds(h * INNER_DEV + step * 2 * PART, 2 * PART), kind, :],
                sem.at[slot, h, kind],
            )
            for h in range(2)
            for kind in range(2)
        ]

    @pl.when(step >= 2)
    def _():
        finish(moves(step - 2, slot))

    for h in range(2):
        cols = slice(h * INNER_DEV, (h + 1) * INNER_DEV)
        for n in range(2):
            rows = slice(n * PART, n * PART + PART)
            wide[slot, h, 0, rows] = a_ref[h, n, PART:EARLY].astype(F32)
            wide[slot, h, 1, rows] = a_ref[h, n, EARLY:WIDE].astype(F32)
            out_ref[rows, cols] = a_ref[h, n, 0:PART].astype(F32)
            at = pl.ds(pl.multiple_of(step * 32 + n * 16, 16), 16)
            bc_all[at, cols] = a_ref[h, n, WIDE:SUB].astype(F32)
    for move in moves(step, slot):
        move.start()

    @pl.when(step == 0)
    def _():
        rows = rest_ref[0].astype(F32)
        more = rest_ref[1].astype(F32)
        dt_ref[:, :INNER_DEV] = rows[0:HEADS_DEV]
        dt_ref[:, INNER_DEV:] = more[0:HEADS_DEV]
        rows = rows[16:]
        norm_ref[:, :INNER_DEV] = rows[0:1]
        norm_ref[:, INNER_DEV:] = more[16:17]
        conv_ref[...] = rows[1:5]
        gate_ref[...] = rows[5:6]
        heads = jnp.concatenate(
            [
                jnp.sum(rows[0:8, h * HEAD_DIM : (h + 1) * HEAD_DIM], axis=1, keepdims=True)
                for h in range(HEADS_DEV)
            ],
            axis=1,
        )
        skip_ref[...] = heads[6:7]
        rate_ref[...] = rows[7:8, 0:HEADS_DEV]
        bias_ref[...] = rows[8:9, 0:HEADS_DEV]
        conv_bc_ref[...] = rows[9:13, 0:256]

    @pl.when(step == 7)
    def _():
        bc_ref[...] = bc_all[...].T
        finish(moves(step - 1, 1 - slot))
        finish(moves(step, slot))


def widen(total, rest):
    total = total.reshape(2, 16, SUB, INNER_DEV)
    fixed = ((WIDTH, 256), (HEADS_DEV, WIDTH), (1, WIDTH)) + ((1, HEADS_DEV),) * 3
    fixed += ((4, INNER_DEV), (4, 256), (1, INNER_DEV))
    shapes = ((WIDTH, 2, INNER_DEV), (INNER_DEV, WIDTH)) + fixed
    return pl.pallas_call(
        widen_kernel,
        grid=(8,),
        out_shape=[jax.ShapeDtypeStruct(shape, F32) for shape in shapes],
        in_specs=[
            pl.BlockSpec((2, 2, SUB, INNER_DEV), lambda i: (0, i, 0, 0)),
            pl.BlockSpec((2, REST, INNER_DEV), lambda i: (0, 0, 0)),
        ],
        out_specs=[
            ANY,
            pl.BlockSpec((2 * PART, WIDTH), lambda i: (i, 0)),
        ]
        + [pl.BlockSpec(shape, lambda i: (0, 0)) for shape in fixed],
        scratch_shapes=[
            pltpu.VMEM((256, WIDTH), F32),
            pltpu.VMEM((2, 2, 2, 2 * PART, INNER_DEV), F32),
            pltpu.SemaphoreType.DMA((2, 2, 2)),
        ],
        compiler_params=pltpu.CompilerParams(vmem_limit_bytes=VMEM_CAP),
        name="widen",
    )(total, rest)


def on_device(
    x_in,
    norm_gain,
    w_zx,
    w_bc,
    w_dt,
    dt_bias,
    a_log,
    d_skip,
    conv_x,
    conv_bc,
    gate_gain,
    w_out,
    cotangent,
):
    zx_m = w_zx[0].reshape(WIDTH, WIDTH)
    bc_m, out_m, dt_m = w_bc[0], w_out[0], w_dt[0].T
    small_args = (norm_gain, gate_gain, conv_x[0], conv_bc[0], dt_bias, a_log, d_skip)
    kept, (zx_t, bc_t, out_t, smalls, dt_all, part) = forward(x_in, zx_m, bc_m, out_m, dt_m, small_args, 0)
    held = (zx_m, bc_m, out_m, zx_t, bc_t, out_t)
    total, rest, section_out, grads_in = backward(
        cotangent, x_in, part, held, smalls, dt_all, kept, 1
    )
    g_zx, g_out, g_bc, g_dt, g_norm, g_bias, g_rate, g_skip, g_conv_x, g_conv_bc, g_gate = widen(total, rest)
    return (
        section_out[None],
        grads_in[None],
        g_norm,
        g_zx[None],
        g_bc[None],
        g_dt.T[None],
        g_bias,
        g_rate,
        g_skip,
        g_conv_x[None],
        g_conv_bc[None],
        g_gate,
        g_out[None],
    )


def solution(mesh):
    in_specs = (
        P(None, "seq", None),
        P("section", None),
        P("section", None, None, "head"),
        P("section", None, None),
        P("section", None, "head"),
        P("section", "head"),
        P("section", "head"),
        P("section", "head"),
        P("section", None, "head"),
        P("section", None, None),
        P("section", "head"),
        P("section", "head", None),
        P(None, "seq", None),
    )
    out_specs = (
        P("section", None, "seq", None),
        P("section", None, "seq", None),
        P("section", None),
        P("section", None, None, "head"),
        P("section", None, None),
        P("section", None, "head"),
        P("section", "head"),
        P("section", "head"),
        P("section", "head"),
        P("section", None, "head"),
        P("section", None, None),
        P("section", "head"),
        P("section", "head", None),
    )
    return jax.shard_map(
        on_device, mesh=mesh, in_specs=in_specs, out_specs=out_specs, check_vma=False
    )
```

```python
import functools

import jax
import jax.numpy as jnp
from jax import lax
from jax.experimental import pallas as pl
from jax.experimental.pallas import tpu as pltpu
from jax.sharding import PartitionSpec as P

MESH = pl.DeviceIdType.MESH
F32 = jnp.float32
BF = jnp.bfloat16
EPS = 1e-05
INNER = 3072
ROWS = 256
WIDTH = 1536
INNER_DEV = 768
HEADS_DEV = 12
HEAD_DIM = 64
STATE = 128
RIM = 16
VMEM_CAP = 60 << 20
FIRST = (((0,), (0,)), ((), ()))
LAST = (((1,), (1,)), ((), ()))


def dot(a, b):
    return jnp.dot(a, b, preferred_element_type=F32)


def dot_first(a, b):
    return lax.dot_general(a, b, FIRST, preferred_element_type=F32)


def dot_last(a, b):
    return lax.dot_general(a, b, LAST, preferred_element_type=F32)


def two_part(a):
    high = a.astype(BF)
    return high, (a - high.astype(F32)).astype(BF)


def silu(a):
    return a * jax.nn.sigmoid(a)


def silu_slope(a):
    sigma = jax.nn.sigmoid(a)
    return sigma * (1.0 + a * (1.0 - sigma))


def spread(a):
    rows = a.shape[0]
    low_half = lax.broadcasted_iota(jnp.int32, (rows, 128), 1) < HEAD_DIM
    return jnp.concatenate(
        [
            jnp.where(low_half, a[:, 2 * j : 2 * j + 1], a[:, 2 * j + 1 : 2 * j + 2])
            for j in range(HEADS_DEV // 2)
        ],
        axis=1,
    )


def triangle(keep_after):
    t = lax.broadcasted_iota(jnp.int32, (ROWS, ROWS), 0)
    s = lax.broadcasted_iota(jnp.int32, (ROWS, ROWS), 1)
    return jnp.where((s >= t) if keep_after else (t >= s), 1.0, 0.0).astype(BF)


def running(a, keep_after):
    weights = triangle(keep_after)
    high, low = two_part(a)
    return dot(weights, high) + dot(weights, low)


S_NORM, S_GATE, S_CONV, S_BIAS, S_RATE, S_SKIP = 0, 1, 2, 6, 7, 9
STEP = 64
BLOCKS = ROWS // STEP


def softplus(a):
    return jnp.maximum(a, 0.0) + jnp.log1p(jnp.exp(-jnp.abs(a)))


def rows_at(i, more=0):
    return pl.ds(pl.multiple_of(i * STEP, STEP), STEP + more)


def tile_at(i, width=256, base=0):
    return pl.ds(pl.multiple_of(base + i * width, width), width)


def conv_rows(pre, taps):
    total = taps[0:1] * pre[RIM - 3 : RIM - 3 + STEP]
    for k in range(1, 4):
        total = total + taps[k : k + 1] * pre[RIM - 3 + k : RIM - 3 + k + STEP]
    return total


def shifted(place, distance, count):
    return lax.rem(place + distance + count, count)


def meet(targets):
    barrier = pltpu.get_barrier_semaphore()
    for target in targets:
        pl.semaphore_signal(barrier, inc=1, device_id=target, device_id_type=MESH)
    pl.semaphore_wait(barrier, len(targets))


def send(src, dst, send_sem, recv_sem, target):
    copy = pltpu.make_async_remote_copy(
        src_ref=src,
        dst_ref=dst,
        send_sem=send_sem,
        recv_sem=recv_sem,
        device_id=target,
        device_id_type=MESH,
    )
    copy.start()
    return copy


def comm_params(number):
    return pltpu.CompilerParams(
        collective_id=number, has_side_effects=True, vmem_limit_bytes=VMEM_CAP
    )


ANY = pl.BlockSpec(memory_space=pl.ANY)
VM = pl.BlockSpec(memory_space=pltpu.VMEM)


def quarter(place):
    return pl.ds(pl.multiple_of(place * 384, 384), 384)


KEPT = (
    ("normed", (ROWS + RIM, WIDTH), BF),
    ("z", (ROWS, INNER_DEV), F32),
    ("x_pre", (ROWS + RIM, INNER_DEV), F32),
    ("bc_pre", (ROWS + RIM, 256), F32),
    ("dt_pre", (ROWS, 128), F32),
    ("la", (ROWS, 128), F32),
    ("la_t", (128, ROWS), F32),
    ("xd", (ROWS, INNER_DEV), BF),
    ("bc_act", (ROWS, 256), BF),
    ("x_act", (ROWS, INNER_DEV), F32),
    ("y", (ROWS, INNER_DEV), F32),
    ("decay", (8, INNER_DEV), F32),
    ("state", (STATE, INNER_DEV), BF),
    ("scale", (ROWS, 128), F32),
    ("out", (ROWS, WIDTH), BF),
    ("following", (ROWS, WIDTH), BF),
)


def chain_load(own, decay, out_buf):
    for j in range(16):
        rows = own[8 * j : 8 * j + 8]
        out_buf[j, :, 0:384] = jnp.concatenate([rows[:, :384], rows[:, 384:]], axis=0).astype(BF)
    six = jnp.concatenate([decay[0:1, 128 * k : 128 * k + 128] for k in range(6)] * 3, axis=0)
    six = six[0:16].astype(BF)
    for j in range(16):
        out_buf[j, :, 384:512] = six


def chain_scan(forward, in_buf, back_buf):
    state = jnp.zeros((16, 384), F32)
    for step in range(16):
        i = step if forward else 15 - step
        back_buf[i] = state.astype(BF)
        part = in_buf[i].astype(F32)
        decay = jnp.concatenate(
            [
                jnp.concatenate(
                    [
                        jnp.broadcast_to(part[3 * half + k : 3 * half + k + 1, 384:512], (8, 128))
                        for k in range(3)
                    ],
                    axis=1,
                )
                for half in range(2)
            ],
            axis=0,
        )
        state = decay * state + part[:, 0:384]


def chain_unload(got_buf, state_ref):
    for j in range(8):
        first, second = got_buf[2 * j].astype(F32), got_buf[2 * j + 1].astype(F32)
        for half in range(2):
            rows = jnp.concatenate(
                [first[8 * half : 8 * half + 8], second[8 * half : 8 * half + 8]], axis=0
            )
            state_ref[16 * j : 16 * j + 16, 384 * half : 384 * half + 384] = rows.astype(BF)


def spread_send(src, dst, me, send_sem, recv_sem):
    copies = []
    for d in range(1, 16):
        to = shifted(me, d, 16)
        copies.append(send(src.at[to], dst.at[me], send_sem.at[d], recv_sem.at[d], {"seq": to}))
    dst[me] = src[me]
    return copies


def finish(copies):
    for copy in copies:
        copy.wait()


def norm_rows(v, gain):
    v = v.astype(F32)
    scale = lax.rsqrt(jnp.mean(v * v, axis=-1, keepdims=True) + EPS)
    return (v * scale * gain).astype(BF)


def forward_kernel(*refs):
    x_ref, zx_m, bc_m, out_m, dt_m = refs[:5]
    norm_gain, gate_gain, conv_x, conv_bc, dt_bias, a_log, d_skip = refs[5:12]
    stored = [{name: refs[12 + 16 * s + i] for i, (name, _, _) in enumerate(KEPT)} for s in range(2)]
    zx_t, bc_t, out_t, small_w, dt_w, part_ref = refs[44:50]
    v_buf, rim_buf, zx_w, bc_w, out_w = refs[50:55]
    tail_x, scores, dt_buf, tail, low, sq, part = refs[55:62]
    chain_out, chain_in, chain_back, chain_got = refs[62:66]
    sum_in, square_out, square_in, sum_own, next_own = refs[66:71]
    w_send, w_recv, w_own, rim_send, rim_recv = refs[71:76]
    c_sems, s_sems, t_sem, v_sem, k_sem = refs[76:80], refs[80:84], refs[84], refs[85], refs[86]
    kept = [{name: refs[87 + 16 * s + i] for i, (name, _, _) in enumerate(KEPT)} for s in range(2)]

    core, me, place = lax.axis_index("section"), lax.axis_index("seq"), lax.axis_index("head")
    other = {"section": 1 - core}
    later = shifted(me, 1, 16)
    barrier = pltpu.get_barrier_semaphore()
    targets = [other]
    targets += [{"seq": shifted(me, d, 16)} for d in range(1, 16)]
    heads = [{"head": shifted(place, d, 4)} for d in range(1, 4)]
    targets += heads
    targets += [{"head": shifted(place, d, 4), "seq": shifted(me, -1, 16)} for d in range(1, 4)]
    for target in targets:
        pl.semaphore_signal(barrier, inc=1, device_id=target, device_id_type=MESH)

    moves = [
        (bc_m, bc_w.at[core]),
        (zx_m.at[:, INNER_DEV:], zx_w.at[core, :, INNER_DEV:]),
        (zx_m.at[:, :INNER_DEV], zx_w.at[core, :, :INNER_DEV]),
        (out_m, out_w.at[core]),
    ]
    own_moves = [pltpu.make_async_copy(src, dst, w_own.at[i]) for i, (src, dst) in enumerate(moves)]
    for move in own_moves:
        move.start()
    load_v = pltpu.make_async_copy(x_ref.at[core], v_buf, v_sem)
    load_v.start()
    small_w[core] = jnp.zeros((16, WIDTH), F32)
    small_w[core, S_NORM : S_NORM + 1] = norm_gain[...]
    small_w[core, S_GATE : S_GATE + 1, :INNER_DEV] = gate_gain[...]
    small_w[core, S_CONV : S_CONV + 4, :INNER_DEV] = conv_x[...].astype(F32)
    small_w[core, S_CONV : S_CONV + 4, INNER_DEV : INNER_DEV + 256] = conv_bc[...].astype(F32)
    small_w[core, S_BIAS : S_BIAS + 1, 0:HEADS_DEV] = dt_bias[...]
    small_w[core, S_RATE : S_RATE + 1, 0:HEADS_DEV] = -jnp.exp(a_log[...])
    small_w[core, 8:9, 0:HEADS_DEV] = d_skip[...]
    skip_wide = spread(small_w[core, 8:16, 0:128])
    small_w[core, S_SKIP : S_SKIP + 1, :INNER_DEV] = skip_wide[0:1]
    dt_rows = jnp.concatenate([dt_m[...].astype(F32), jnp.zeros((4, WIDTH), F32)], axis=0)
    dt_w[core, 0:16] = dt_rows.astype(BF)
    for s in range(2):
        dt_w[s, 16:] = jnp.zeros((112, WIDTH), BF)
    pl.semaphore_wait(barrier, len(targets))
    rim_copy = send(x_ref.at[core, ROWS - RIM :], rim_buf.at[0], rim_send.at[0], rim_recv.at[0], {"seq": later})
    across = [
        send(small_w.at[core], small_w.at[core], w_send.at[4], w_recv.at[4], other),
        send(dt_w.at[core, 0:16], dt_w.at[core, 0:16], w_send.at[5], w_recv.at[5], other),
    ]
    for i, (src, dst) in enumerate(moves):
        across.append(
            pltpu.make_async_remote_copy(
                src_ref=src,
                dst_ref=dst,
                send_sem=w_send.at[i],
                recv_sem=w_recv.at[i],
                device_id=other,
                device_id_type=MESH,
            )
        )
    across[2].start()
    across[3].start()

    def arrive(section, i):
        @pl.when(core == section)
        def _():
            own_moves[i].wait()

        @pl.when(core != section)
        def _():
            across[i + 2].wait_recv()

    load_v.wait()
    rim_copy.wait()

    @pl.when(me == 0)
    def _():
        rim_buf[0] = jnp.zeros((RIM, WIDTH), BF)

    across[0].wait_recv()
    across[1].wait_recv()
    def store(s, names):
        moves = []
        for i, (name, _, _) in enumerate(KEPT):
            if name in names:
                moves.append(pltpu.make_async_copy(kept[s][name], stored[s][name], k_sem.at[s, i]))
        return moves

    first_names = ("normed", "x_pre", "bc_pre", "dt_pre", "la", "la_t", "xd", "bc_act", "x_act", "decay")
    next_names = ("z", "y", "state")
    last_names = ("scale", "out", "following")
    for s in range(2):
        k = kept[s]
        small = small_w.at[s]
        normed, z_ref, x_pre, bc_pre, la_ref, la_t_ref = (
            k["normed"], k["z"], k["x_pre"], k["bc_pre"], k["la"], k["la_t"]
        )
        xd_ref, bc_act, x_act, y_ref = k["xd"], k["bc_act"], k["x_act"], k["y"]
        gain = small[S_NORM : S_NORM + 1]
        if s:
            finish(rim_in)

            @pl.when(me == 0)
            def _():
                rim_buf[1] = jnp.zeros((RIM, WIDTH), BF)

        normed[0:RIM] = norm_rows(rim_buf[s], gain)
        if s == 0:

            @pl.loop(0, ROWS // 16)
            def _(i):
                at = pl.ds(pl.multiple_of(i * 16, 16), 16)
                normed[pl.ds(pl.multiple_of(i * 16 + RIM, 16), 16)] = norm_rows(v_buf[at], gain)

        arrive(s, 0)
        bc_pre[...] = dot(normed[...], bc_w[s])
        dt_raw = dot_last(normed[RIM:], dt_w[s])
        k["dt_pre"][...] = dt_raw
        arrive(s, 1)

        @pl.loop(0, 3)
        def _(j):
            x_pre[:, tile_at(j)] = dot(normed[...], zx_w[s, :, tile_at(j, 256, INNER_DEV)])

        if s == 0:
            across[3].wait_send()
            across[4].start()
        dt = softplus(dt_raw + small[S_BIAS : S_BIAS + 1, :128])
        dt_buf[...] = dt
        la = running(dt * small[S_RATE : S_RATE + 1, :128], False)
        la_ref[...] = la
        la_t_ref[...] = la.T
        tail[...] = jnp.exp(la[ROWS - 1 : ROWS] - la)
        decay = jnp.broadcast_to(spread(jnp.exp(la[ROWS - 8 : ROWS]))[7:8], (8, INNER_DEV))
        k["decay"][...] = decay

        @pl.loop(0, BLOCKS)
        def _(i):
            taps = small[S_CONV : S_CONV + 4]
            act = silu(conv_rows(x_pre[rows_at(i, RIM)], taps[:, :INNER_DEV]))
            x_act[rows_at(i)] = act
            xd = (act * spread(dt_buf[rows_at(i)])).astype(BF)
            xd_ref[rows_at(i)] = xd
            tail_x[rows_at(i)] = (xd.astype(F32) * spread(tail[rows_at(i)])).astype(BF)
            bc = conv_rows(bc_pre[rows_at(i, RIM)], taps[:, INNER_DEV : INNER_DEV + 256])
            bc_act[rows_at(i)] = silu(bc).astype(BF)

        b_rows, c_rows = bc_act[:, :STATE], bc_act[:, STATE:]
        if s == 0:
            across[5].start()
        for move in store(s, first_names):
            move.start()
        chain_load(dot_first(b_rows, tail_x[...]), decay, chain_out.at[s])
        copies = spread_send(chain_out.at[s], chain_in.at[s], me, c_sems[0].at[s], c_sems[1].at[s])
        arrive(s, 2)

        @pl.loop(0, 3)
        def _(j):
            z_ref[:, tile_at(j)] = dot(normed[RIM:], zx_w[s, :, tile_at(j)])

        scores[...] = dot_last(c_rows, b_rows)

        def heads_of(half):
            span = (half + 1) * 128
            rows = slice(half * 128, span)
            t = lax.broadcasted_iota(jnp.int32, (128, span), 0) + half * 128
            causal = t >= lax.broadcasted_iota(jnp.int32, (128, span), 1)
            for pair in range(HEADS_DEV // 2):
                parts = []
                for h in (2 * pair, 2 * pair + 1):
                    gap = la_ref[rows, h : h + 1] - la_t_ref[h : h + 1, :span]
                    mixing = scores[rows, :span] * jnp.exp(jnp.where(causal, gap, -1e30))
                    cols = slice(h * HEAD_DIM, (h + 1) * HEAD_DIM)
                    parts.append(dot(mixing.astype(BF), xd_ref[:span, cols]))
                y_ref[rows, pair * 128 : pair * 128 + 128] = jnp.concatenate(parts, axis=1)

        heads_of(0)
        finish(copies)
        chain_scan(True, chain_in.at[s], chain_back.at[s])
        copies = spread_send(chain_back.at[s], chain_got.at[s], me, c_sems[2].at[s], c_sems[3].at[s])
        heads_of(1)
        finish(copies)
        chain_unload(chain_got.at[s], k["state"])

        copies = []
        for half in range(2):
            rows = slice(half * 128, half * 128 + 128)

            @pl.loop(half * BLOCKS // 2, (half + 1) * BLOCKS // 2)
            def _(i):
                at = rows_at(i)
                y = y_ref[at] + spread(jnp.exp(la_ref[at])) * dot(bc_act[at, STATE:], k["state"][...])
                y_ref[at] = y
                ssd = y + small[S_SKIP : S_SKIP + 1, :INNER_DEV] * x_act[at]
                gated = ssd * silu(z_ref[at])
                if s == 0:
                    sq[at] = jnp.broadcast_to(jnp.sum(gated * gated, axis=-1, keepdims=True), (STEP, 128))
                low[at] = (gated * small[S_GATE : S_GATE + 1, :INNER_DEV]).astype(BF)

            if s == 0:
                square_out[half] = sq[rows].T[0:8]
            if half == 0:
                arrive(s, 3)
                if s:
                    for move in store_theirs(core, (bc_w, zx_w, out_w), (bc_t, zx_t, out_t), t_sem):
                        move.start()

            @pl.loop(0, 6)
            def _(j):
                part[rows, tile_at(j)] = dot(low[rows], out_w[s, :, tile_at(j)]).astype(BF)

            if s:
                continue
            batch = []
            for d in range(3):
                src = part.at[rows, quarter(shifted(place, d + 1, 4))]
                sems = s_sems[0].at[half, d], s_sems[1].at[half, d]
                batch.append(send(src, sum_in.at[d, rows], *sems, heads[d]))
                sems = s_sems[0].at[half, d + 3], s_sems[1].at[half, d + 3]
                batch.append(send(square_out.at[half], square_in.at[half, d], *sems, heads[d]))
            copies.append(batch)

        for move in store(s, next_names):
            move.start()
        if s:
            break
        for half in range(2):
            rows = slice(half * 128, half * 128 + 128)
            finish(copies[half])
            square = square_out[half]
            for d in range(3):
                square = square + square_in[half, d]
            column = lax.rsqrt(square * (1.0 / INNER) + EPS).T[:, 0:1]
            k["scale"][rows] = jnp.broadcast_to(column, (128, 128))

            @pl.loop(half * BLOCKS // 2, (half + 1) * BLOCKS // 2)
            def _(i):
                at = rows_at(i)
                total = part[at, quarter(place)].astype(F32)
                for d in range(3):
                    total = total + sum_in[d, at].astype(F32)
                total = (total * k["scale"][at][:, 0:1]).astype(BF)
                sum_own[at] = total
                k["out"][at, quarter(place)] = total

            copies[half] = []
            for d in range(3):
                sems = s_sems[2].at[half, d], s_sems[3].at[half, d]
                dst = k["out"].at[rows, quarter(place)]
                copies[half].append(send(sum_own.at[rows], dst, *sems, heads[d]))
        edge = slice(ROWS - RIM, ROWS)
        next_own[...] = (v_buf[edge, quarter(place)].astype(F32) + sum_own[edge].astype(F32)).astype(BF)
        rim_in = []
        for d in range(4):
            dst = rim_buf.at[1, :, quarter(place)]
            target = {"head": shifted(place, d, 4), "seq": later}
            rim_in.append(send(next_own, dst, rim_send.at[1 + d], rim_recv.at[1 + d], target))
        for half in range(2):
            finish(copies[half])

            @pl.loop(half * 8, half * 8 + 8)
            def _(i):
                at = pl.ds(pl.multiple_of(i * 16, 16), 16)
                following = (v_buf[at].astype(F32) + k["out"][at].astype(F32)).astype(BF)
                k["following"][at] = following
                at = pl.ds(pl.multiple_of(i * 16 + RIM, 16), 16)
                kept[1]["normed"][at] = norm_rows(following, small_w[1, S_NORM : S_NORM + 1])

        for move in store(s, last_names):
            move.start()

    store_part = pltpu.make_async_copy(part, part_ref, v_sem)
    store_part.start()
    finish(store(0, first_names + next_names + last_names))
    finish(store(1, first_names + next_names))
    store_part.wait()
    for i in (0, 1, 2, 4, 5):
        across[i].wait_send()
    for move in store_theirs(core, (bc_w, zx_w, out_w), (bc_t, zx_t, out_t), t_sem):
        move.wait()


def store_theirs(core, held, dst, sem):
    return [
        pltpu.make_async_copy(held[i].at[1 - core], dst[i], sem.at[i]) for i in range(3)
    ]


def forward(x_in, zx_m, bc_m, out_m, dt_m, smalls, number):
    dma = pltpu.SemaphoreType.DMA
    sds = jax.ShapeDtypeStruct
    vm = pltpu.VMEM
    got = pl.pallas_call(
        forward_kernel,
        out_shape=[sds(shape, kind) for _, shape, kind in KEPT * 2]
        + [sds(zx_m.shape, BF), sds(bc_m.shape, BF), sds(out_m.shape, BF)]
        + [sds((2, 16, WIDTH), F32), sds((2, 128, WIDTH), BF), sds((ROWS, WIDTH), BF)],
        in_specs=[ANY] * 4 + [VM] * 8,
        out_specs=[ANY] * 35 + [VM] * 2 + [ANY],
        scratch_shapes=[
            vm((ROWS, WIDTH), BF),
            vm((2, RIM, WIDTH), BF),
            vm((2, WIDTH, WIDTH), BF),
            vm((2, WIDTH, 256), BF),
            vm((2, INNER_DEV, WIDTH), BF),
            vm((ROWS, INNER_DEV), BF),
            vm((ROWS, ROWS), F32),
            vm((ROWS, 128), F32),
            vm((ROWS, 128), F32),
            vm((ROWS, INNER_DEV), BF),
            vm((ROWS, 128), F32),
            vm((ROWS, WIDTH), BF),
            vm((2, 16, 16, 512), BF),
            vm((2, 16, 16, 512), BF),
            vm((2, 16, 16, 384), BF),
            vm((2, 16, 16, 384), BF),
            vm((3, ROWS, 384), BF),
            vm((2, 8, 128), F32),
            vm((2, 3, 8, 128), F32),
            vm((ROWS, 384), BF),
            vm((RIM, 384), BF),
            dma((6,)),
            dma((6,)),
            dma((4,)),
            dma((5,)),
            dma((5,)),
            dma((2, 16)),
            dma((2, 16)),
            dma((2, 16)),
            dma((2, 16)),
            dma((2, 6)),
            dma((2, 6)),
            dma((2, 3)),
            dma((2, 3)),
            dma((3,)),
            dma,
            dma((2, len(KEPT))),
        ]
        + [vm(shape, kind) for _, shape, kind in KEPT * 2],
        compiler_params=comm_params(number),
        name="forward_layers",
    )(x_in, zx_m, bc_m, out_m, dt_m, *smalls)
    kept = [{name: got[16 * s + i] for i, (name, _, _) in enumerate(KEPT)} for s in range(2)]
    return kept, got[32:38]


PART = 48
EARLY, WIDE = 2 * PART, 3 * PART
SUB = WIDE + 16
GROUPS = (((0, PART), (PART, EARLY)), ((EARLY, EARLY + 32), (EARLY + 32, SUB)))
REST = 32
SLOT = ("z", "x_pre", "bc_pre", "dt_pre", "la", "la_t", "xd", "bc_act", "x_act", "y", "decay", "state", "scale", "out")
SHAPES = {name: (shape, kind) for name, shape, kind in KEPT}


def add_rows(total, more):
    return total.astype(F32) + more.astype(F32)


def backward_kernel(*refs):
    cot_ref, x_ref, part_ref = refs[:3]
    held = (refs[3:6], refs[6:9])
    small_all, dt_all = refs[9:11]
    saved = [{name: refs[11 + 16 * s + i] for i, (name, _, _) in enumerate(KEPT)} for s in range(2)]
    grads_ref, rest_ref, section_ref, leaving_ref = refs[43:47]
    rest = list(refs[47:])

    def take(count):
        got = rest[:count]
        del rest[:count]
        return got

    k = dict(zip(SLOT, take(len(SLOT))))
    normed_all, v_all, d_v, g_o_buf = take(4)
    zx_w, bc_w, out_w = take(3)
    own, spare, theirs, first, mid, second, ring = take(7)
    d_y_ref, d_z_ref, d_xd, d_y_low, wide_x, wide_y = take(6)
    scores_t, d_scores_t, d_bc, terms, direct, tail_ref, dt_ref = take(7)
    ext, d_zx, d_bd, part, sum_in, d_normed_ref, sum_own = take(7)
    chain_out, chain_in, chain_back, chain_got, state_grad = take(5)
    rim_buf, taps_ref, bc_out, bc_in, norm_ref, sums_ref, small_rows = take(7)
    rest_out, rest_cross, rest_near, rest_far, rest_low = take(5)
    k_sem, n_sem, w_sem, move_sem = take(4)
    c_sems, s_sems, rim_sems, swap_sems = take(4), take(4), take(2), take(2)
    cross_sems, one_sems, two_sems, back_sems, last_sems = take(2), take(2), take(2), take(2), take(2)
    bc_sems, rest_sems = take(2), take(2)
    row_out, row_in, final_in, final_own = take(4)
    row_sems, final_sems = take(2), take(4)
    theirs_free, first_free = take(2)

    core, me, place = lax.axis_index("section"), lax.axis_index("seq"), lax.axis_index("head")
    x, z = lax.div(me, 4), lax.rem(me, 4)
    along_z = [x * 4 + shifted(z, d, 4) for d in range(1, 4)]
    along_x = [shifted(x, d, 4) * 4 + z for d in range(1, 4)]
    ways = ((x, z, along_z, along_x), (z, x, along_x, along_z))
    other = {"section": 1 - core}
    heads = [{"head": shifted(place, d, 4)} for d in range(1, 4)]
    targets = [other] + [{"seq": shifted(me, d, 16)} for d in range(1, 16)] + heads
    targets += [{"section": 1 - core, "seq": seq} for seq in along_z + along_x]
    targets += [{"section": 1 - core, "head": shifted(place, d, 4)} for d in range(1, 4)]
    barrier = pltpu.get_barrier_semaphore()
    for target in targets:
        pl.semaphore_signal(barrier, inc=1, device_id=target, device_id_type=MESH)

    def load_kept(s):
        return [
            pltpu.make_async_copy(saved[s][name], k[name], k_sem.at[i])
            for i, name in enumerate(SLOT)
            if s == 0 or name not in ("scale", "out")
        ]

    def load_rows(s):
        source = x_ref.at[core] if s == 0 else saved[0]["following"]
        return [
            pltpu.make_async_copy(saved[s]["normed"], normed_all.at[s], n_sem.at[s, 0]),
            pltpu.make_async_copy(source, v_all.at[s], n_sem.at[s, 1]),
        ]

    weight_slots = (zx_w, bc_w, out_w)

    def load_weight(s, i):
        @pl.when(core == s)
        def _():
            pltpu.make_async_copy(held[0][i], weight_slots[i], w_sem.at[i]).start()

        @pl.when(core != s)
        def _():
            pltpu.make_async_copy(held[1][i], weight_slots[i], w_sem.at[i]).start()

    def wait_weight(i):
        pltpu.make_async_copy(held[0][i], weight_slots[i], w_sem.at[i]).wait()

    load_g_o = pltpu.make_async_copy(cot_ref.at[core], g_o_buf, n_sem.at[0, 2])
    load_g_o.start()
    load_weight(1, 2)
    for move in load_kept(1):
        move.start()
    load_weight(1, 0)
    load_weight(1, 1)
    for s in (1, 0):
        for move in load_rows(s):
            move.start()

    small_rows[...] = jnp.zeros_like(small_rows)
    def swapped(i, src, dst):
        return pltpu.make_async_remote_copy(
            src_ref=src,
            dst_ref=dst.at[core],
            send_sem=swap_sems[0].at[i],
            recv_sem=swap_sems[1].at[i],
            device_id=other,
            device_id_type=MESH,
        )

    def final(d, micro):
        return pltpu.make_async_remote_copy(
            src_ref=final_own,
            dst_ref=section_ref.at[micro, :, quarter(place)],
            send_sem=final_sems[2].at[d],
            recv_sem=final_sems[3].at[micro, d],
            device_id={"section": 1, "head": shifted(place, d + 1, 4)},
            device_id_type=MESH,
        )

    def final_stay():
        return pltpu.make_async_copy(final_own, section_ref.at[1, :, quarter(place)], move_sem.at[0])

    def cross(s, piece):
        lo, hi = GROUPS[piece][0][0], GROUPS[piece][1][1]
        return pltpu.make_async_remote_copy(
            src_ref=spare.at[:, :, lo:hi],
            dst_ref=theirs.at[:, :, lo:hi],
            send_sem=cross_sems[0].at[s, piece],
            recv_sem=cross_sems[1].at[s, piece],
            device_id=other,
            device_id_type=MESH,
        )

    def reduction(s, group):
        parts = [(n, lo, hi) + ways[n] for n, (lo, hi) in enumerate(GROUPS[group])]
        low, high = parts[0][1], parts[1][2]
        cross(s, group).wait_recv()

        @pl.loop(0, 4)
        def _(i):
            @pl.loop(0, 4)
            def _(j):
                own[s, i, j, low:high] = own[s, i, j, low:high] + theirs[i, j, low:high]

        if s == 0:
            pl.semaphore_wait(first_free.at[group], 6)
        copies = []
        for d in range(3):
            for n, lo, hi, a, b, near, far in parts:
                src = own.at[s, :, shifted(b, d + 1, 4), lo:hi]
                dst = first.at[d, :, lo:hi]
                sems = one_sems[0].at[s, group, n, d], one_sems[1].at[s, group, n, d]
                copies.append(send(src, dst, *sems, {"seq": near[d]}))
        yield
        finish(copies)

        @pl.loop(0, 4)
        def _(i):
            for n, lo, hi, a, b, near, far in parts:
                total = own[s, i, b, lo:hi].astype(F32)
                for d in range(3):
                    total = total + first[d, i, lo:hi].astype(F32)
                mid[i, lo:hi] = total.astype(BF)

        copies = []
        for d in range(3):
            for n, lo, hi, a, b, near, far in parts:
                src = mid.at[shifted(a, d + 1, 4), lo:hi]
                dst = second.at[s, d, lo:hi]
                sems = two_sems[0].at[s, group, n, d], two_sems[1].at[s, group, n, d]
                copies.append(send(src, dst, *sems, {"seq": far[d]}))
        yield
        finish(copies)
        copies = []
        for n, lo, hi, a, b, near, far in parts:
            total = mid[a, lo:hi].astype(F32)
            for d in range(3):
                total = total + second[s, d, lo:hi].astype(F32)
            ring[s, a, lo:hi] = total.astype(BF)
            for d in range(3):
                block = ring.at[s, a, lo:hi]
                sems = back_sems[0].at[s, group, n, d], back_sems[1].at[s, group, n, d]
                copies.append(send(block, block, *sems, {"seq": far[d]}))
        yield
        finish(copies)

        def last(part, d, half):
            n, lo, hi, a, b, near, far = part
            return pltpu.make_async_remote_copy(
                src_ref=ring.at[s, :, lo:hi],
                dst_ref=grads_ref.at[half, :, b, lo:hi],
                send_sem=last_sems[0].at[s, group, n, d],
                recv_sem=last_sems[1].at[s, group, n, half, d],
                device_id={"section": s, "seq": near[d] if d < 3 else me},
                device_id_type=MESH,
            )

        def stay(part):
            n, lo, hi, a, b, near, far = part
            sem = last_sems[0].at[s, group, n, 3]
            return pltpu.make_async_copy(ring.at[s, :, lo:hi], grads_ref.at[core, :, b, lo:hi], sem)

        for d in range(3):
            for part in parts:
                last(part, d, core).start()

        @pl.when(core == s)
        def _():
            for part in parts:
                stay(part).start()

        @pl.when(core != s)
        def _():
            for part in parts:
                last(part, 3, core).start()

        yield
        for part in parts:
            for d in range(3):
                last(part, d, core).wait_send()

        @pl.when(core == s)
        def _():
            for part in parts:
                stay(part).wait()
                for d in range(3):
                    last(part, d, s).wait_recv()
                for d in range(4):
                    last(part, d, 1 - s).wait_recv()

        @pl.when(core != s)
        def _():
            for part in parts:
                last(part, 3, core).wait_send()

        yield

    def reduction_rest(s):
        def move(src, dst, i, target):
            return send(src, dst, rest_sems[0].at[s, i], rest_sems[1].at[s, i], target)

        def gather(bufs, first_sem, peers):
            return [move(rest_low.at[s], bufs.at[s, d], first_sem + d, {"seq": peers[d]}) for d in range(3)]

        copy = move(rest_out.at[1 - core], rest_cross.at[s], 0, other)
        yield
        copy.wait()
        total = add_rows(rest_out[core], rest_cross[s])
        rest_low[s] = total.astype(BF)
        copies = gather(rest_near, 1, along_z)
        yield
        finish(copies)
        for d in range(3):
            total = total + rest_near[s, d].astype(F32)
        rest_low[s] = total.astype(BF)
        copies = gather(rest_far, 4, along_x)
        yield
        finish(copies)
        for d in range(3):
            total = total + rest_far[s, d].astype(F32)
        rest_low[s] = total.astype(BF)

        def deliver():
            return pltpu.make_async_remote_copy(
                src_ref=rest_low.at[s],
                dst_ref=rest_ref.at[core],
                send_sem=rest_sems[0].at[s, 7],
                recv_sem=rest_sems[1].at[s, 7],
                device_id=other,
                device_id_type=MESH,
            )

        @pl.when(core != s)
        def _():
            deliver().start()

        @pl.when(core == s)
        def _():
            rest_ref[core] = rest_low[s]

        yield

        @pl.when(core != s)
        def _():
            deliver().wait_send()

        @pl.when(core == s)
        def _():
            deliver().wait_recv()

        yield

    member_rows = lax.broadcasted_iota(jnp.int32, (INNER_DEV, 128), 0)
    member_lanes = lax.broadcasted_iota(jnp.int32, (INNER_DEV, 128), 1) * HEAD_DIM
    inside = (member_rows >= member_lanes) & (member_rows < member_lanes + HEAD_DIM)
    member = jnp.where(inside, 1.0, 0.0).astype(BF)

    def sums_of(value):
        high, low = two_part(value)
        return dot(high, member) + dot(low, member)

    half_rows = [
        [pl.ds(pl.multiple_of(h * INNER_DEV + 384 * j, 384), 384) for j in range(2)] for h in (core, 1 - core)
    ]
    half_cols = [pl.ds(pl.multiple_of(h * INNER_DEV, INNER_DEV), INNER_DEV) for h in (core, 1 - core)]
    early, late, loose = None, None, None
    old_early, old_late = None, None
    load_g_o.wait()
    for s in (1, 0):
        small = small_all.at[s]
        normed, v_ref = normed_all.at[s], v_all.at[s]
        g_o_ref = g_o_buf if s else d_v.at[1]
        y_ref, z_ref, la_ref, la_t_ref = k["y"], k["z"], k["la"], k["la_t"]
        xd_ref, bc_act, x_act = k["xd"], k["bc_act"], k["x_act"]
        x_pre, bc_pre = k["x_pre"], k["bc_pre"]
        stages = (own.at[s], spare)

        sums_ref[...] = jnp.zeros_like(sums_ref)
        wait_weight(2)

        @pl.loop(0, 3)
        def _(j):
            d_xd[:, tile_at(j)] = dot_last(g_o_ref[...], out_w[tile_at(j), :])

        if s:
            load_weight(0, 2)
        finish(load_kept(s))
        if s:
            finish(load_rows(1))

            @pl.loop(0, BLOCKS)
            def _(i):
                at = rows_at(i)
                gain = small[S_GATE : S_GATE + 1, :INNER_DEV]
                ssd = y_ref[at] + small[S_SKIP : S_SKIP + 1, :INNER_DEV] * x_act[at]
                gated = ssd * silu(z_ref[at])
                square = jnp.sum(gated * gated, axis=-1, keepdims=True)
                mean = jnp.sum(gated * gain * d_xd[at], axis=-1, keepdims=True)
                lane = lax.broadcasted_iota(jnp.int32, (STEP, 128), 1)
                tail_ref[at] = jnp.where(lane == 0, square, mean)

            row_out[...] = tail_ref[...].T[0:8]
            pl.semaphore_wait(barrier, len(targets))
            copies = [
                send(row_out, row_in.at[d], row_sems[0].at[d], row_sems[1].at[d], heads[d]) for d in range(3)
            ]
            final_copies = []
            for d in range(3):
                src = part_ref.at[:, quarter(shifted(place, d + 1, 4))]
                sems = final_sems[0].at[d], final_sems[1].at[d]
                final_copies.append(send(src, final_in.at[d], *sems, heads[d]))
            load_final = pltpu.make_async_copy(part_ref.at[:, quarter(place)], final_own, move_sem.at[0])
            load_final.start()
            finish(copies)
            total = row_out[...]
            for d in range(3):
                total = total + row_in[d]
            total = jnp.concatenate([total] * 16, axis=0).T
            scale = lax.rsqrt(total[:, 0:1] * (1.0 / INNER) + EPS)
            mean = total[:, 1:2] * scale * scale * scale * (1.0 / INNER)
            lane = lax.broadcasted_iota(jnp.int32, (ROWS, 128), 1)
            k["scale"][...] = jnp.where(lane == 0, scale, mean)

        @pl.loop(0, BLOCKS)
        def _(i):
            at = rows_at(i)
            gain = small[S_GATE : S_GATE + 1, :INNER_DEV]
            scale = k["scale"][at][:, 0:1]
            act, gate, dm = x_act[at], z_ref[at], d_xd[at]
            ssd = y_ref[at] + small[S_SKIP : S_SKIP + 1, :INNER_DEV] * act
            sigma = jax.nn.sigmoid(gate)
            gate_silu = gate * sigma
            gated = ssd * gate_silu
            scaled = gated * scale
            if s:
                mean = k["scale"][at][:, 1:2]
            else:
                mean = jnp.sum(g_o_ref[at].astype(F32) * k["out"][at].astype(F32), axis=-1, keepdims=True)
                mean = mean * scale * scale * (1.0 / INNER)
            wide_x[at] = (scaled * gain).astype(BF)
            d_gated = scale * gain * dm - gated * mean
            d_y = d_gated * gate_silu
            d_y_ref[at] = d_y
            d_y_low[at] = d_y.astype(BF)
            d_z_ref[at] = (d_gated * ssd * sigma * (1.0 + gate * (1.0 - sigma))).astype(BF)
            wide_y[at] = (spread(jnp.exp(la_ref[at])) * d_y).astype(BF)
            sums_ref[0:1] += jnp.sum(scaled * dm, axis=0, keepdims=True)
            sums_ref[1:2] += jnp.sum(d_y * act, axis=0, keepdims=True)

        b_rows, c_rows = bc_act[:, :STATE], bc_act[:, STATE:]
        chain_load(dot_first(c_rows, wide_y[...]), k["decay"], chain_out)
        copies = spread_send(chain_out, chain_in, me, c_sems[0].at[s], c_sems[1].at[s])
        if s:

            @pl.when(core == 1)
            def _():
                swapped(0, saved[0]["following"], section_ref).start()

        if s == 0:
            for piece in range(2):
                cross(1, piece).wait_send()
        for stage, cols, rows in zip(stages, half_cols, half_rows):
            for j in range(2):
                got = dot_first(wide_x[:, 384 * j : 384 * j + 384], g_o_ref[:, cols]).astype(BF)
                for i in range(8):
                    sub = 8 * j + i
                    stage[sub // 4, sub % 4, 0:PART] = got[PART * i : PART * i + PART]
            for j in range(2):
                got = dot_first(normed[RIM:, rows[j]], d_z_ref[...]).astype(BF)
                for i in range(8):
                    sub = 8 * j + i
                    stage[sub // 4, sub % 4, PART:EARLY] = got[PART * i : PART * i + PART]
        if s == 0:
            pl.semaphore_wait(theirs_free, 1)
        cross(s, 0).start()
        if s == 0:
            next(late)
            for seq in along_z + along_x:
                pl.semaphore_signal(first_free.at[1], inc=1, device_id={"seq": seq}, device_id_type=MESH)
            next(loose)

        la = la_ref[...]
        tail_ref[...] = jnp.exp(la[ROWS - 1 : ROWS] - la)
        dt_in = k["dt_pre"][...] + small[S_BIAS : S_BIAS + 1, :128]
        dt_ref[...] = softplus(dt_in)
        scores_t[...] = dot_last(b_rows, c_rows)

        def heads_of(half):
            base = half * 128
            rows = slice(base, base + 128)
            t = lax.broadcasted_iota(jnp.int32, (128, ROWS - base), 1)
            later = t >= lax.broadcasted_iota(jnp.int32, (128, ROWS - base), 0)
            total = jnp.zeros((128, ROWS - base), F32)
            for pair in range(HEADS_DEV // 2):
                parts = []
                for h in (2 * pair, 2 * pair + 1):
                    cols = slice(h * HEAD_DIM, (h + 1) * HEAD_DIM)
                    gap = la_t_ref[h : h + 1, base:] - la_ref[rows, h : h + 1]
                    decay = jnp.exp(jnp.where(later, gap, -1e30))
                    total = total + decay * dot_last(xd_ref[rows, cols], d_y_low[base:, cols])
                    mixing = (scores_t[rows, base:] * decay).astype(BF)
                    parts.append(dot(mixing, d_y_low[base:, cols]))
                d_xd[rows, pair * 128 : pair * 128 + 128] = jnp.concatenate(parts, axis=1)
            if half:
                d_scores_t[rows, 0:128] = jnp.zeros((128, 128), BF)
            d_scores_t[rows, base:] = total.astype(BF)

        heads_of(0)
        finish(copies)
        chain_scan(False, chain_in, chain_back)
        copies = spread_send(chain_back, chain_got, me, c_sems[2].at[s], c_sems[3].at[s])
        heads_of(1)
        finish(copies)
        old_early, early = early, reduction(s, 0)
        next(early)
        if s == 0:
            next(late)
            next(loose)
        if s:
            load_final.wait()
            finish(final_copies)

            @pl.loop(0, BLOCKS)
            def _(i):
                at = rows_at(i)
                total = final_own[at].astype(F32)
                for d in range(3):
                    total = total + final_in[d, at].astype(F32)
                total = (total * k["scale"][at][:, 0:1]).astype(BF).astype(F32)
                final_own[at] = (v_ref[at, quarter(place)].astype(F32) + total).astype(BF)

            for d in range(3):
                final(d, core).start()

            @pl.when(core == 1)
            def _():
                final_stay().start()

            @pl.when(core == 0)
            def _():
                final(3, core).start()
                pltpu.make_async_copy(v_all.at[1], section_ref.at[0], move_sem.at[0]).start()

        chain_unload(chain_got, state_grad)
        norm_ref[...] = jnp.zeros_like(norm_ref)
        taps_ref[...] = jnp.zeros_like(taps_ref)

        @pl.loop(0, BLOCKS)
        def _(i):
            at = rows_at(i)
            tail = spread(tail_ref[at])
            xd = xd_ref[at].astype(F32)
            wide_x[at] = (tail * xd).astype(BF)
            state_part = tail * dot(bc_act[at, :STATE], state_grad[...])
            got = d_xd[at] + state_part
            d_xd[at] = got
            norm_ref[1:2, :INNER_DEV] += jnp.sum(xd * state_part, axis=0, keepdims=True)
            terms[at] = sums_of(d_y_low[at].astype(F32) * y_ref[at] - xd * got)
            direct[at] = sums_of(x_act[at] * got)

        d_bc[:, :STATE] = dot(d_scores_t[...], c_rows) + dot_last(wide_x[...], state_grad[...])
        d_bc[:, STATE:] = dot_first(d_scores_t[...], b_rows) + dot_last(wide_y[...], k["state"][...])
        end_wide = spread(jnp.exp(la[ROWS - 8 : ROWS]))[7:8]
        both = state_grad[...].astype(F32) * k["state"][...].astype(F32)
        tail_sum = norm_ref[1:2, :INNER_DEV] + end_wide * jnp.sum(both, axis=0, keepdims=True)
        tail_sum = sums_of(jnp.broadcast_to(tail_sum, (16, INNER_DEV)))[0:1]

        @pl.loop(0, BLOCKS)
        def _(i):
            at = rows_at(i)
            taps = small[S_CONV : S_CONV + 4, INNER_DEV : INNER_DEV + 256]
            d_bcc = d_bc[at] * silu_slope(conv_rows(bc_pre[rows_at(i, RIM)], taps))
            d_bc[at] = d_bcc
            bc_out[at] = d_bcc.astype(BF)

        copies = [
            send(bc_out, bc_in.at[d], bc_sems[0].at[s, d], bc_sems[1].at[s, d], heads[d]) for d in range(3)
        ]
        d_log = running(terms[...], True) + tail_sum
        rate = small[S_RATE : S_RATE + 1, :128]
        d_dt = direct[...] + rate * d_log
        d_dt_pre = d_dt * jax.nn.sigmoid(dt_in)
        d_bd[:, 256:] = d_dt_pre.astype(BF)
        sums_ref[2:3, :128] = jnp.sum(dt_ref[...] * d_log, axis=0, keepdims=True) * rate
        sums_ref[3:4, :128] = jnp.sum(d_dt_pre, axis=0, keepdims=True)

        @pl.loop(0, BLOCKS)
        def _(i):
            at = rows_at(i)
            taps = small[S_CONV : S_CONV + 4]
            pre = x_pre[rows_at(i, RIM)]
            d_x = spread(dt_ref[at]) * d_xd[at] + small[S_SKIP : S_SKIP + 1, :INNER_DEV] * d_y_ref[at]
            d_xc = d_x * silu_slope(conv_rows(pre, taps[:, :INNER_DEV]))
            ext[at, :INNER_DEV] = d_xc
            for t in range(4):
                moved = pre[RIM - 3 + t : RIM - 3 + t + STEP]
                taps_ref[t : t + 1, :INNER_DEV] += jnp.sum(moved * d_xc, axis=0, keepdims=True)

        finish(copies)

        @pl.loop(0, BLOCKS)
        def _(i):
            at = rows_at(i)
            d_bcc = d_bc[at]
            for d in range(3):
                d_bcc = d_bcc + bc_in[d, at].astype(F32)
            ext[at, INNER_DEV:] = d_bcc
            pre = bc_pre[rows_at(i, RIM)]
            for t in range(4):
                moved = pre[RIM - 3 + t : RIM - 3 + t + STEP]
                taps_ref[t : t + 1, INNER_DEV:] += jnp.sum(moved * d_bcc, axis=0, keepdims=True)

        rim = send(
            ext.at[0:8], rim_buf, rim_sems[0].at[s], rim_sems[1].at[s], {"seq": shifted(me, -1, 16)}
        )
        if s:
            for move in load_kept(0):
                move.start()

        next(early)
        if s == 0:
            next(loose)
            next(late)
        else:
            for seq in along_z + along_x:
                pl.semaphore_signal(first_free.at[0], inc=1, device_id={"seq": seq}, device_id_type=MESH)
        rim.wait()

        @pl.when(me == 15)
        def _():
            rim_buf[...] = jnp.zeros_like(rim_buf)

        ext[ROWS : ROWS + 8] = rim_buf[...]

        @pl.loop(0, BLOCKS)
        def _(i):
            at = rows_at(i)
            taps = small[S_CONV : S_CONV + 4]
            block = ext[rows_at(i, 8)]
            d_pre = taps[0:1, : INNER_DEV + 256] * block[3 : 3 + STEP]
            for t in range(1, 4):
                d_pre = d_pre + taps[t : t + 1, : INNER_DEV + 256] * block[3 - t : 3 - t + STEP]
            d_zx[at, :INNER_DEV] = d_z_ref[at]
            d_zx[at, INNER_DEV:] = d_pre[:, :INNER_DEV].astype(BF)
            d_bd[at, :256] = d_pre[:, INNER_DEV:].astype(BF)

        wait_weight(0)
        wait_weight(1)

        @pl.loop(0, 6)
        def _(j):
            got = dot_last(d_zx[...], zx_w[tile_at(j), :])
            got = got + dot_last(d_bd[:, :256], bc_w[tile_at(j), :]) * 0.25
            got = got + dot(d_bd[:, 256:], dt_all[s, :, tile_at(j)])
            part[:, tile_at(j)] = got.astype(BF)

        if s:
            load_weight(0, 0)
            load_weight(0, 1)
        copies = []
        for d in range(1, 4):
            src = part.at[:, quarter(shifted(place, d, 4))]
            copies.append(send(src, sum_in.at[d - 1], s_sems[0].at[s, d], s_sems[1].at[s, d], heads[d - 1]))
        for stage, rows in zip(stages, half_rows):
            for j in range(2):
                got = dot_first(normed[RIM:, rows[j]], d_zx[:, INNER_DEV:]).astype(BF)
                for i in range(8):
                    sub = 8 * j + i
                    stage[sub // 4, sub % 4, EARLY:WIDE] = got[PART * i : PART * i + PART]

        for n, (stage, cols) in enumerate(zip(stages, half_cols)):
            got = dot_first(d_bd[...], normed[RIM:, cols])
            for i in range(16):
                stage[i // 4, i % 4, WIDE:SUB] = got[16 * i : 16 * i + 16].astype(BF)
            rest_out[core if n == 0 else 1 - core, 0:16] = got[256:272].astype(BF)
        cross(s, 1).start()
        next(early)
        finish(copies)

        @pl.loop(0, BLOCKS)
        def _(i):
            at = rows_at(i)
            total = part[at, quarter(place)].astype(F32)
            for d in range(3):
                total = total + sum_in[d, at].astype(F32)
            total = total.astype(BF)
            sum_own[at] = total
            d_normed_ref[at, quarter(place)] = total

        copies = []
        for d in range(1, 4):
            dst = d_normed_ref.at[:, quarter(place)]
            copies.append(send(sum_own, dst, s_sems[2].at[s, d], s_sems[3].at[s, d], heads[d - 1]))
        old_late, late = late, reduction(s, 1)
        next(early)
        if s == 0:
            next(late)
        finish(copies)
        norm_ref[...] = jnp.zeros_like(norm_ref)

        @pl.loop(0, BLOCKS)
        def _(i):
            at = rows_at(i)
            v = v_ref[at].astype(F32)
            scale = lax.rsqrt(jnp.mean(v * v, axis=-1, keepdims=True) + EPS)
            d_normed = d_normed_ref[at].astype(F32)
            scaled = v * scale
            norm_ref[0:1] += jnp.sum(scaled * d_normed, axis=0, keepdims=True)
            weighted = d_normed * small[S_NORM : S_NORM + 1]
            mean = jnp.mean(v * weighted, axis=-1, keepdims=True) * scale * scale
            d_v[s, at] = (scale * weighted - scaled * mean + g_o_ref[at].astype(F32)).astype(BF)

        for h in range(2):
            small_rows[h, 0:1] = norm_ref[0:1, h * INNER_DEV : (h + 1) * INNER_DEV]
            small_rows[h, 1:5] = taps_ref[0:4, :INNER_DEV]
            small_rows[h, 5:9] = sums_ref[0:4]
            small_rows[h, 9:13, 0:256] = taps_ref[0:4, INNER_DEV:]
            rest_out[h, 16:] = small_rows[h].astype(BF)
        old_loose, loose = loose, reduction_rest(s)
        next(loose)
        if s:
            next(late)
            pl.semaphore_signal(theirs_free, inc=1, device_id=other, device_id_type=MESH)

        @pl.when(core == 1 - s)
        def _():
            swapped(1, d_v.at[s], leaving_ref).start()

        @pl.when(core == s)
        def _():
            pltpu.make_async_copy(d_v.at[s], leaving_ref.at[s], move_sem.at[1]).start()

        if s:
            finish(load_rows(0))

    for turn in (loose, late, loose, late, loose, late, loose, early, late, old_early, old_late, old_loose):
        next(turn)
    for piece in range(2):
        cross(0, piece).wait_send()
    for d in range(3):
        final(d, core).wait_send()

    @pl.when(core == 0)
    def _():
        swapped(0, d_v.at[0], section_ref).wait_recv()
        pltpu.make_async_copy(v_all.at[1], section_ref.at[0], move_sem.at[0]).wait()
        final(3, core).wait_send()

    @pl.when(core == 1)
    def _():
        swapped(0, saved[0]["following"], section_ref).wait_send()
        final_stay().wait()
        for d in range(3):
            final(d, 1).wait_recv()
        for d in range(4):
            final(d, 0).wait_recv()

    swapped(1, d_v.at[0], leaving_ref).wait()
    pltpu.make_async_copy(d_v.at[0], leaving_ref.at[0], move_sem.at[1]).wait()


def backward(cotangent, x_in, part, held, smalls, dt_all, kept, number):
    dma = pltpu.SemaphoreType.DMA
    regular = pltpu.SemaphoreType.REGULAR
    sds = jax.ShapeDtypeStruct
    vm = pltpu.VMEM
    halves = (4, 4, SUB, INNER_DEV)
    rows_low = vm((ROWS, INNER_DEV), BF)
    rows_wide = vm((ROWS, INNER_DEV), F32)
    steps = vm((ROWS, 128), F32)
    scratch = [vm(*SHAPES[name]) for name in SLOT]
    scratch += [
        vm((2, ROWS + RIM, WIDTH), BF),
        vm((2, ROWS, WIDTH), BF),
        vm((2, ROWS, WIDTH), BF),
        vm((ROWS, WIDTH), BF),
        vm((WIDTH, WIDTH), BF),
        vm((WIDTH, 256), BF),
        vm((INNER_DEV, WIDTH), BF),
        vm((2,) + halves, BF),
        vm(halves, BF),
        vm(halves, BF),
        vm((3, 4, SUB, INNER_DEV), BF),
        vm((4, SUB, INNER_DEV), BF),
        vm((2, 3, SUB, INNER_DEV), BF),
        vm((2, 4, SUB, INNER_DEV), BF),
        rows_wide, rows_low, rows_wide, rows_low, rows_low, rows_low,
        vm((ROWS, ROWS), F32),
        vm((ROWS, ROWS), BF),
        vm((ROWS, 256), F32),
        steps, steps, steps, steps,
        vm((ROWS + 8, INNER_DEV + 256), F32),
        vm((ROWS, WIDTH), BF),
        vm((ROWS, 384), BF),
        vm((ROWS, WIDTH), BF),
        vm((3, ROWS, 384), BF),
        vm((ROWS, WIDTH), BF),
        vm((ROWS, 384), BF),
        vm((16, 16, 512), BF),
        vm((16, 16, 512), BF),
        vm((16, 16, 384), BF),
        vm((16, 16, 384), BF),
        vm((STATE, INNER_DEV), BF),
        vm((8, INNER_DEV + 256), F32),
        vm((8, INNER_DEV + 256), F32),
        vm((ROWS, 256), BF),
        vm((3, ROWS, 256), BF),
        vm((8, WIDTH), F32),
        vm((8, INNER_DEV), F32),
        vm((2, 16, INNER_DEV), F32),
        vm((2, REST, INNER_DEV), BF),
        vm((2, REST, INNER_DEV), BF),
        vm((2, 3, REST, INNER_DEV), BF),
        vm((2, 3, REST, INNER_DEV), BF),
        vm((2, REST, INNER_DEV), BF),
        dma((len(SLOT),)),
        dma((2, 3)),
        dma((3,)),
        dma((2,)),
    ]
    scratch += [dma((2, 16))] * 4 + [dma((2, 8))] * 2 + [dma((2, 4))] * 2
    scratch += [dma((2,))] * 4 + [dma((2, 2))] * 2
    scratch += [dma((2, 2, 2, 4))] * 7 + [dma((2, 2, 2, 2, 4))]
    scratch += [dma((2, 3))] * 2 + [dma((2, 8))] * 2
    scratch += [vm((8, ROWS), F32), vm((3, 8, ROWS), F32), vm((3, ROWS, 384), BF), vm((ROWS, 384), BF)]
    scratch += [dma((3,))] * 4 + [dma((4,)), dma((2, 4)), regular, regular((2,))]
    flat = [kept[s][name] for s in range(2) for name, _, _ in KEPT]
    return pl.pallas_call(
        backward_kernel,
        out_shape=[
            sds((2,) + halves, BF),
            sds((2, REST, INNER_DEV), BF),
            sds((2, ROWS, WIDTH), BF),
            sds((2, ROWS, WIDTH), BF),
        ],
        in_specs=[ANY] * 9 + [VM] * 2 + [ANY] * 32,
        out_specs=[ANY, VM, ANY, ANY],
        scratch_shapes=scratch,
        compiler_params=comm_params(number),
        name="backward_layers",
    )(cotangent, x_in, part, *held, smalls, dt_all, *flat)


def widen_kernel(
    a_ref, rest_ref, zx_ref, out_ref, bc_ref, dt_ref, norm_ref, bias_ref, rate_ref, skip_ref, conv_ref, conv_bc_ref,
    gate_ref, bc_all, wide, sem,
):
    step = pl.program_id(0)
    slot = lax.rem(step, 2)

    def moves(step, slot):
        return [
            pltpu.make_async_copy(
                wide.at[slot, h, kind],
                zx_ref.at[pl.ds(h * INNER_DEV + step * 2 * PART, 2 * PART), kind, :],
                sem.at[slot, h, kind],
            )
            for h in range(2)
            for kind in range(2)
        ]

    @pl.when(step >= 2)
    def _():
        finish(moves(step - 2, slot))

    for h in range(2):
        cols = slice(h * INNER_DEV, (h + 1) * INNER_DEV)
        for n in range(2):
            rows = slice(n * PART, n * PART + PART)
            wide[slot, h, 0, rows] = a_ref[h, n, PART:EARLY].astype(F32)
            wide[slot, h, 1, rows] = a_ref[h, n, EARLY:WIDE].astype(F32)
            out_ref[rows, cols] = a_ref[h, n, 0:PART].astype(F32)
            at = pl.ds(pl.multiple_of(step * 32 + n * 16, 16), 16)
            bc_all[at, cols] = a_ref[h, n, WIDE:SUB].astype(F32)
    for move in moves(step, slot):
        move.start()

    @pl.when(step == 0)
    def _():
        rows = rest_ref[0].astype(F32)
        more = rest_ref[1].astype(F32)
        dt_ref[:, :INNER_DEV] = rows[0:HEADS_DEV]
        dt_ref[:, INNER_DEV:] = more[0:HEADS_DEV]
        rows = rows[16:]
        norm_ref[:, :INNER_DEV] = rows[0:1]
        norm_ref[:, INNER_DEV:] = more[16:17]
        conv_ref[...] = rows[1:5]
        gate_ref[...] = rows[5:6]
        heads = jnp.concatenate(
            [
                jnp.sum(rows[0:8, h * HEAD_DIM : (h + 1) * HEAD_DIM], axis=1, keepdims=True)
                for h in range(HEADS_DEV)
            ],
            axis=1,
        )
        skip_ref[...] = heads[6:7]
        rate_ref[...] = rows[7:8, 0:HEADS_DEV]
        bias_ref[...] = rows[8:9, 0:HEADS_DEV]
        conv_bc_ref[...] = rows[9:13, 0:256]

    @pl.when(step == 7)
    def _():
        bc_ref[...] = bc_all[...].T
        finish(moves(step - 1, 1 - slot))
        finish(moves(step, slot))


def widen(total, rest):
    total = total.reshape(2, 16, SUB, INNER_DEV)
    fixed = ((WIDTH, 256), (HEADS_DEV, WIDTH), (1, WIDTH)) + ((1, HEADS_DEV),) * 3
    fixed += ((4, INNER_DEV), (4, 256), (1, INNER_DEV))
    shapes = ((WIDTH, 2, INNER_DEV), (INNER_DEV, WIDTH)) + fixed
    return pl.pallas_call(
        widen_kernel,
        grid=(8,),
        out_shape=[jax.ShapeDtypeStruct(shape, F32) for shape in shapes],
        in_specs=[
            pl.BlockSpec((2, 2, SUB, INNER_DEV), lambda i: (0, i, 0, 0)),
            pl.BlockSpec((2, REST, INNER_DEV), lambda i: (0, 0, 0)),
        ],
        out_specs=[
            ANY,
            pl.BlockSpec((2 * PART, WIDTH), lambda i: (i, 0)),
        ]
        + [pl.BlockSpec(shape, lambda i: (0, 0)) for shape in fixed],
        scratch_shapes=[
            pltpu.VMEM((256, WIDTH), F32),
            pltpu.VMEM((2, 2, 2, 2 * PART, INNER_DEV), F32),
            pltpu.SemaphoreType.DMA((2, 2, 2)),
        ],
        compiler_params=pltpu.CompilerParams(vmem_limit_bytes=VMEM_CAP),
        name="widen",
    )(total, rest)


def on_device(
    x_in,
    norm_gain,
    w_zx,
    w_bc,
    w_dt,
    dt_bias,
    a_log,
    d_skip,
    conv_x,
    conv_bc,
    gate_gain,
    w_out,
    cotangent,
):
    zx_m = w_zx[0].reshape(WIDTH, WIDTH)
    bc_m, out_m, dt_m = w_bc[0], w_out[0], w_dt[0].T
    small_args = (norm_gain, gate_gain, conv_x[0], conv_bc[0], dt_bias, a_log, d_skip)
    kept, (zx_t, bc_t, out_t, smalls, dt_all, part) = forward(x_in, zx_m, bc_m, out_m, dt_m, small_args, 0)
    held = (zx_m, bc_m, out_m, zx_t, bc_t, out_t)
    total, rest, section_out, grads_in = backward(
        cotangent, x_in, part, held, smalls, dt_all, kept, 1
    )
    g_zx, g_out, g_bc, g_dt, g_norm, g_bias, g_rate, g_skip, g_conv_x, g_conv_bc, g_gate = widen(total, rest)
    return (
        section_out[None],
        grads_in[None],
        g_norm,
        g_zx[None],
        g_bc[None],
        g_dt.T[None],
        g_bias,
        g_rate,
        g_skip,
        g_conv_x[None],
        g_conv_bc[None],
        g_gate,
        g_out[None],
    )


def solution(mesh):
    in_specs = (
        P(None, "seq", None),
        P("section", None),
        P("section", None, None, "head"),
        P("section", None, None),
        P("section", None, "head"),
        P("section", "head"),
        P("section", "head"),
        P("section", "head"),
        P("section", None, "head"),
        P("section", None, None),
        P("section", "head"),
        P("section", "head", None),
        P(None, "seq", None),
    )
    out_specs = (
        P("section", None, "seq", None),
        P("section", None, "seq", None),
        P("section", None),
        P("section", None, None, "head"),
        P("section", None, None),
        P("section", None, "head"),
        P("section", "head"),
        P("section", "head"),
        P("section", "head"),
        P("section", None, "head"),
        P("section", None, None),
        P("section", "head"),
        P("section", "head", None),
    )
    return jax.shard_map(
        on_device, mesh=mesh, in_specs=in_specs, out_specs=out_specs, check_vma=False
    )
```

```python
import functools

import jax
import jax.numpy as jnp
from jax import lax
from jax.experimental import pallas as pl
from jax.experimental.pallas import tpu as pltpu
from jax.sharding import PartitionSpec as P

MESH = pl.DeviceIdType.MESH
F32 = jnp.float32
BF = jnp.bfloat16
EPS = 1e-05
INNER = 3072
ROWS = 256
WIDTH = 1536
INNER_DEV = 768
HEADS_DEV = 12
HEAD_DIM = 64
STATE = 128
RIM = 16
VMEM_CAP = 60 << 20
FIRST = (((0,), (0,)), ((), ()))
LAST = (((1,), (1,)), ((), ()))


def dot(a, b):
    return jnp.dot(a, b, preferred_element_type=F32)


def dot_first(a, b):
    return lax.dot_general(a, b, FIRST, preferred_element_type=F32)


def dot_last(a, b):
    return lax.dot_general(a, b, LAST, preferred_element_type=F32)


def two_part(a):
    high = a.astype(BF)
    return high, (a - high.astype(F32)).astype(BF)


def silu(a):
    return a * jax.nn.sigmoid(a)


def silu_slope(a):
    sigma = jax.nn.sigmoid(a)
    return sigma * (1.0 + a * (1.0 - sigma))


def spread(a):
    rows = a.shape[0]
    low_half = lax.broadcasted_iota(jnp.int32, (rows, 128), 1) < HEAD_DIM
    return jnp.concatenate(
        [
            jnp.where(low_half, a[:, 2 * j : 2 * j + 1], a[:, 2 * j + 1 : 2 * j + 2])
            for j in range(HEADS_DEV // 2)
        ],
        axis=1,
    )


def triangle(keep_after):
    t = lax.broadcasted_iota(jnp.int32, (ROWS, ROWS), 0)
    s = lax.broadcasted_iota(jnp.int32, (ROWS, ROWS), 1)
    return jnp.where((s >= t) if keep_after else (t >= s), 1.0, 0.0).astype(BF)


def running(a, keep_after):
    weights = triangle(keep_after)
    high, low = two_part(a)
    return dot(weights, high) + dot(weights, low)


S_NORM, S_GATE, S_CONV, S_BIAS, S_RATE, S_SKIP = 0, 1, 2, 6, 7, 9
STEP = 64
BLOCKS = ROWS // STEP


def softplus(a):
    return jnp.maximum(a, 0.0) + jnp.log1p(jnp.exp(-jnp.abs(a)))


def rows_at(i, more=0):
    return pl.ds(pl.multiple_of(i * STEP, STEP), STEP + more)


def tile_at(i, width=256, base=0):
    return pl.ds(pl.multiple_of(base + i * width, width), width)


def conv_rows(pre, taps):
    total = taps[0:1] * pre[RIM - 3 : RIM - 3 + STEP]
    for k in range(1, 4):
        total = total + taps[k : k + 1] * pre[RIM - 3 + k : RIM - 3 + k + STEP]
    return total


def shifted(place, distance, count):
    return lax.rem(place + distance + count, count)


def meet(targets):
    barrier = pltpu.get_barrier_semaphore()
    for target in targets:
        pl.semaphore_signal(barrier, inc=1, device_id=target, device_id_type=MESH)
    pl.semaphore_wait(barrier, len(targets))


def send(src, dst, send_sem, recv_sem, target):
    copy = pltpu.make_async_remote_copy(
        src_ref=src,
        dst_ref=dst,
        send_sem=send_sem,
        recv_sem=recv_sem,
        device_id=target,
        device_id_type=MESH,
    )
    copy.start()
    return copy


def comm_params(number):
    return pltpu.CompilerParams(
        collective_id=number, has_side_effects=True, vmem_limit_bytes=VMEM_CAP
    )


ANY = pl.BlockSpec(memory_space=pl.ANY)
VM = pl.BlockSpec(memory_space=pltpu.VMEM)


def quarter(place):
    return pl.ds(pl.multiple_of(place * 384, 384), 384)


KEPT = (
    ("normed", (ROWS + RIM, WIDTH), BF),
    ("z", (ROWS, INNER_DEV), F32),
    ("x_pre", (ROWS + RIM, INNER_DEV), F32),
    ("bc_pre", (ROWS + RIM, 256), F32),
    ("dt_pre", (ROWS, 128), F32),
    ("la", (ROWS, 128), F32),
    ("la_t", (128, ROWS), F32),
    ("xd", (ROWS, INNER_DEV), BF),
    ("bc_act", (ROWS, 256), BF),
    ("x_act", (ROWS, INNER_DEV), F32),
    ("y", (ROWS, INNER_DEV), F32),
    ("decay", (8, INNER_DEV), F32),
    ("state", (STATE, INNER_DEV), BF),
    ("scale", (ROWS, 128), F32),
    ("out", (ROWS, WIDTH), BF),
    ("following", (ROWS, WIDTH), BF),
)


def chain_load(own, decay, out_buf):
    for j in range(16):
        rows = own[8 * j : 8 * j + 8]
        out_buf[j, :, 0:384] = jnp.concatenate([rows[:, :384], rows[:, 384:]], axis=0).astype(BF)
    six = jnp.concatenate([decay[0:1, 128 * k : 128 * k + 128] for k in range(6)] * 3, axis=0)
    six = six[0:16].astype(BF)
    for j in range(16):
        out_buf[j, :, 384:512] = six


def chain_scan(forward, in_buf, back_buf):
    state = jnp.zeros((16, 384), F32)
    for step in range(16):
        i = step if forward else 15 - step
        back_buf[i] = state.astype(BF)
        part = in_buf[i].astype(F32)
        decay = jnp.concatenate(
            [
                jnp.concatenate(
                    [
                        jnp.broadcast_to(part[3 * half + k : 3 * half + k + 1, 384:512], (8, 128))
                        for k in range(3)
                    ],
                    axis=1,
                )
                for half in range(2)
            ],
            axis=0,
        )
        state = decay * state + part[:, 0:384]


def chain_unload(got_buf, state_ref):
    for j in range(8):
        first, second = got_buf[2 * j].astype(F32), got_buf[2 * j + 1].astype(F32)
        for half in range(2):
            rows = jnp.concatenate(
                [first[8 * half : 8 * half + 8], second[8 * half : 8 * half + 8]], axis=0
            )
            state_ref[16 * j : 16 * j + 16, 384 * half : 384 * half + 384] = rows.astype(BF)


def spread_send(src, dst, me, send_sem, recv_sem):
    copies = []
    for d in range(1, 16):
        to = shifted(me, d, 16)
        copies.append(send(src.at[to], dst.at[me], send_sem.at[d], recv_sem.at[d], {"seq": to}))
    dst[me] = src[me]
    return copies


def finish(copies):
    for copy in copies:
        copy.wait()


def norm_rows(v, gain):
    v = v.astype(F32)
    scale = lax.rsqrt(jnp.mean(v * v, axis=-1, keepdims=True) + EPS)
    return (v * scale * gain).astype(BF)


def forward_kernel(*refs):
    x_ref, zx_m, bc_m, out_m, dt_m = refs[:5]
    norm_gain, gate_gain, conv_x, conv_bc, dt_bias, a_log, d_skip = refs[5:12]
    stored = [{name: refs[12 + 16 * s + i] for i, (name, _, _) in enumerate(KEPT)} for s in range(2)]
    zx_t, bc_t, out_t, small_w, dt_w, part_ref = refs[44:50]
    v_buf, rim_buf, zx_w, bc_w, out_w = refs[50:55]
    tail_x, scores, dt_buf, tail, low, sq, part = refs[55:62]
    chain_out, chain_in, chain_back, chain_got = refs[62:66]
    sum_in, square_out, square_in, sum_own, next_own = refs[66:71]
    w_send, w_recv, w_own, rim_send, rim_recv = refs[71:76]
    c_sems, s_sems, t_sem, v_sem, k_sem = refs[76:80], refs[80:84], refs[84], refs[85], refs[86]
    kept = [{name: refs[87 + 16 * s + i] for i, (name, _, _) in enumerate(KEPT)} for s in range(2)]

    core, me, place = lax.axis_index("section"), lax.axis_index("seq"), lax.axis_index("head")
    other = {"section": 1 - core}
    later = shifted(me, 1, 16)
    barrier = pltpu.get_barrier_semaphore()
    targets = [other]
    targets += [{"seq": shifted(me, d, 16)} for d in range(1, 16)]
    heads = [{"head": shifted(place, d, 4)} for d in range(1, 4)]
    targets += heads
    targets += [{"head": shifted(place, d, 4), "seq": shifted(me, -1, 16)} for d in range(1, 4)]
    for target in targets:
        pl.semaphore_signal(barrier, inc=1, device_id=target, device_id_type=MESH)

    moves = [
        (bc_m, bc_w.at[core]),
        (zx_m.at[:, INNER_DEV:], zx_w.at[core, :, INNER_DEV:]),
        (zx_m.at[:, :INNER_DEV], zx_w.at[core, :, :INNER_DEV]),
        (out_m, out_w.at[core]),
    ]
    own_moves = [pltpu.make_async_copy(src, dst, w_own.at[i]) for i, (src, dst) in enumerate(moves)]
    for move in own_moves:
        move.start()
    load_v = pltpu.make_async_copy(x_ref.at[core], v_buf, v_sem)
    load_v.start()
    small_w[core] = jnp.zeros((16, WIDTH), F32)
    small_w[core, S_NORM : S_NORM + 1] = norm_gain[...]
    small_w[core, S_GATE : S_GATE + 1, :INNER_DEV] = gate_gain[...]
    small_w[core, S_CONV : S_CONV + 4, :INNER_DEV] = conv_x[...].astype(F32)
    small_w[core, S_CONV : S_CONV + 4, INNER_DEV : INNER_DEV + 256] = conv_bc[...].astype(F32)
    small_w[core, S_BIAS : S_BIAS + 1, 0:HEADS_DEV] = dt_bias[...]
    small_w[core, S_RATE : S_RATE + 1, 0:HEADS_DEV] = -jnp.exp(a_log[...])
    small_w[core, 8:9, 0:HEADS_DEV] = d_skip[...]
    skip_wide = spread(small_w[core, 8:16, 0:128])
    small_w[core, S_SKIP : S_SKIP + 1, :INNER_DEV] = skip_wide[0:1]
    dt_rows = jnp.concatenate([dt_m[...].astype(F32), jnp.zeros((4, WIDTH), F32)], axis=0)
    dt_w[core, 0:16] = dt_rows.astype(BF)
    for s in range(2):
        dt_w[s, 16:] = jnp.zeros((112, WIDTH), BF)
    pl.semaphore_wait(barrier, len(targets))
    rim_copy = send(x_ref.at[core, ROWS - RIM :], rim_buf.at[0], rim_send.at[0], rim_recv.at[0], {"seq": later})
    across = [
        send(small_w.at[core], small_w.at[core], w_send.at[4], w_recv.at[4], other),
        send(dt_w.at[core, 0:16], dt_w.at[core, 0:16], w_send.at[5], w_recv.at[5], other),
    ]
    for i, (src, dst) in enumerate(moves):
        across.append(
            pltpu.make_async_remote_copy(
                src_ref=src,
                dst_ref=dst,
                send_sem=w_send.at[i],
                recv_sem=w_recv.at[i],
                device_id=other,
                device_id_type=MESH,
            )
        )
    across[2].start()
    across[3].start()

    def arrive(section, i):
        @pl.when(core == section)
        def _():
            own_moves[i].wait()

        @pl.when(core != section)
        def _():
            across[i + 2].wait_recv()

    load_v.wait()
    rim_copy.wait()

    @pl.when(me == 0)
    def _():
        rim_buf[0] = jnp.zeros((RIM, WIDTH), BF)

    across[0].wait_recv()
    across[1].wait_recv()
    def store(s, names):
        moves = []
        for i, (name, _, _) in enumerate(KEPT):
            if name in names:
                moves.append(pltpu.make_async_copy(kept[s][name], stored[s][name], k_sem.at[s, i]))
        return moves

    first_names = ("normed", "x_pre", "bc_pre", "dt_pre", "la", "la_t", "xd", "bc_act", "x_act", "decay")
    next_names = ("z", "y", "state")
    last_names = ("scale", "out", "following")
    for s in range(2):
        k = kept[s]
        small = small_w.at[s]
        normed, z_ref, x_pre, bc_pre, la_ref, la_t_ref = (
            k["normed"], k["z"], k["x_pre"], k["bc_pre"], k["la"], k["la_t"]
        )
        xd_ref, bc_act, x_act, y_ref = k["xd"], k["bc_act"], k["x_act"], k["y"]
        gain = small[S_NORM : S_NORM + 1]
        if s:
            finish(rim_in)

            @pl.when(me == 0)
            def _():
                rim_buf[1] = jnp.zeros((RIM, WIDTH), BF)

        normed[0:RIM] = norm_rows(rim_buf[s], gain)
        if s == 0:

            @pl.loop(0, ROWS // 16)
            def _(i):
                at = pl.ds(pl.multiple_of(i * 16, 16), 16)
                normed[pl.ds(pl.multiple_of(i * 16 + RIM, 16), 16)] = norm_rows(v_buf[at], gain)

        arrive(s, 0)
        bc_pre[...] = dot(normed[...], bc_w[s])
        dt_raw = dot_last(normed[RIM:], dt_w[s])
        k["dt_pre"][...] = dt_raw
        arrive(s, 1)

        @pl.loop(0, 3)
        def _(j):
            x_pre[:, tile_at(j)] = dot(normed[...], zx_w[s, :, tile_at(j, 256, INNER_DEV)])

        if s == 0:
            across[3].wait_send()
            across[4].start()
        dt = softplus(dt_raw + small[S_BIAS : S_BIAS + 1, :128])
        dt_buf[...] = dt
        la = running(dt * small[S_RATE : S_RATE + 1, :128], False)
        la_ref[...] = la
        la_t_ref[...] = la.T
        tail[...] = jnp.exp(la[ROWS - 1 : ROWS] - la)
        decay = jnp.broadcast_to(spread(jnp.exp(la[ROWS - 8 : ROWS]))[7:8], (8, INNER_DEV))
        k["decay"][...] = decay

        @pl.loop(0, BLOCKS)
        def _(i):
            taps = small[S_CONV : S_CONV + 4]
            act = silu(conv_rows(x_pre[rows_at(i, RIM)], taps[:, :INNER_DEV]))
            x_act[rows_at(i)] = act
            xd = (act * spread(dt_buf[rows_at(i)])).astype(BF)
            xd_ref[rows_at(i)] = xd
            tail_x[rows_at(i)] = (xd.astype(F32) * spread(tail[rows_at(i)])).astype(BF)
            bc = conv_rows(bc_pre[rows_at(i, RIM)], taps[:, INNER_DEV : INNER_DEV + 256])
            bc_act[rows_at(i)] = silu(bc).astype(BF)

        b_rows, c_rows = bc_act[:, :STATE], bc_act[:, STATE:]
        if s == 0:
            across[5].start()
        for move in store(s, first_names):
            move.start()
        chain_load(dot_first(b_rows, tail_x[...]), decay, chain_out.at[s])
        copies = spread_send(chain_out.at[s], chain_in.at[s], me, c_sems[0].at[s], c_sems[1].at[s])
        arrive(s, 2)

        @pl.loop(0, 3)
        def _(j):
            z_ref[:, tile_at(j)] = dot(normed[RIM:], zx_w[s, :, tile_at(j)])

        scores[...] = dot_last(c_rows, b_rows)

        def heads_of(half):
            span = (half + 1) * 128
            rows = slice(half * 128, span)
            t = lax.broadcasted_iota(jnp.int32, (128, span), 0) + half * 128
            causal = t >= lax.broadcasted_iota(jnp.int32, (128, span), 1)
            for pair in range(HEADS_DEV // 2):
                parts = []
                for h in (2 * pair, 2 * pair + 1):
                    gap = la_ref[rows, h : h + 1] - la_t_ref[h : h + 1, :span]
                    mixing = scores[rows, :span] * jnp.exp(jnp.where(causal, gap, -1e30))
                    cols = slice(h * HEAD_DIM, (h + 1) * HEAD_DIM)
                    parts.append(dot(mixing.astype(BF), xd_ref[:span, cols]))
                y_ref[rows, pair * 128 : pair * 128 + 128] = jnp.concatenate(parts, axis=1)

        heads_of(0)
        finish(copies)
        chain_scan(True, chain_in.at[s], chain_back.at[s])
        copies = spread_send(chain_back.at[s], chain_got.at[s], me, c_sems[2].at[s], c_sems[3].at[s])
        heads_of(1)
        finish(copies)
        chain_unload(chain_got.at[s], k["state"])

        copies = []
        for half in range(2):
            rows = slice(half * 128, half * 128 + 128)

            @pl.loop(half * BLOCKS // 2, (half + 1) * BLOCKS // 2)
            def _(i):
                at = rows_at(i)
                y = y_ref[at] + spread(jnp.exp(la_ref[at])) * dot(bc_act[at, STATE:], k["state"][...])
                y_ref[at] = y
                ssd = y + small[S_SKIP : S_SKIP + 1, :INNER_DEV] * x_act[at]
                gated = ssd * silu(z_ref[at])
                if s == 0:
                    sq[at] = jnp.broadcast_to(jnp.sum(gated * gated, axis=-1, keepdims=True), (STEP, 128))
                low[at] = (gated * small[S_GATE : S_GATE + 1, :INNER_DEV]).astype(BF)

            if s == 0:
                square_out[half] = sq[rows].T[0:8]
            if half == 0:
                arrive(s, 3)
                if s:
                    for move in store_theirs(core, (bc_w, zx_w, out_w), (bc_t, zx_t, out_t), t_sem):
                        move.start()

            @pl.loop(0, 6)
            def _(j):
                part[rows, tile_at(j)] = dot(low[rows], out_w[s, :, tile_at(j)]).astype(BF)

            if s:
                continue
            batch = []
            for d in range(3):
                src = part.at[rows, quarter(shifted(place, d + 1, 4))]
                sems = s_sems[0].at[half, d], s_sems[1].at[half, d]
                batch.append(send(src, sum_in.at[d, rows], *sems, heads[d]))
                sems = s_sems[0].at[half, d + 3], s_sems[1].at[half, d + 3]
                batch.append(send(square_out.at[half], square_in.at[half, d], *sems, heads[d]))
            copies.append(batch)

        for move in store(s, next_names):
            move.start()
        if s:
            break
        for half in range(2):
            rows = slice(half * 128, half * 128 + 128)
            finish(copies[half])
            square = square_out[half]
            for d in range(3):
                square = square + square_in[half, d]
            column = lax.rsqrt(square * (1.0 / INNER) + EPS).T[:, 0:1]
            k["scale"][rows] = jnp.broadcast_to(column, (128, 128))

            @pl.loop(half * BLOCKS // 2, (half + 1) * BLOCKS // 2)
            def _(i):
                at = rows_at(i)
                total = part[at, quarter(place)].astype(F32)
                for d in range(3):
                    total = total + sum_in[d, at].astype(F32)
                total = (total * k["scale"][at][:, 0:1]).astype(BF)
                sum_own[at] = total
                k["out"][at, quarter(place)] = total

            copies[half] = []
            for d in range(3):
                sems = s_sems[2].at[half, d], s_sems[3].at[half, d]
                dst = k["out"].at[rows, quarter(place)]
                copies[half].append(send(sum_own.at[rows], dst, *sems, heads[d]))
        edge = slice(ROWS - RIM, ROWS)
        next_own[...] = (v_buf[edge, quarter(place)].astype(F32) + sum_own[edge].astype(F32)).astype(BF)
        rim_in = []
        for d in range(4):
            dst = rim_buf.at[1, :, quarter(place)]
            target = {"head": shifted(place, d, 4), "seq": later}
            rim_in.append(send(next_own, dst, rim_send.at[1 + d], rim_recv.at[1 + d], target))
        for half in range(2):
            finish(copies[half])

            @pl.loop(half * 8, half * 8 + 8)
            def _(i):
                at = pl.ds(pl.multiple_of(i * 16, 16), 16)
                following = (v_buf[at].astype(F32) + k["out"][at].astype(F32)).astype(BF)
                k["following"][at] = following
                at = pl.ds(pl.multiple_of(i * 16 + RIM, 16), 16)
                kept[1]["normed"][at] = norm_rows(following, small_w[1, S_NORM : S_NORM + 1])

        for move in store(s, last_names):
            move.start()

    store_part = pltpu.make_async_copy(part, part_ref, v_sem)
    store_part.start()
    finish(store(0, first_names + next_names + last_names))
    finish(store(1, first_names + next_names))
    store_part.wait()
    for i in (0, 1, 2, 4, 5):
        across[i].wait_send()
    for move in store_theirs(core, (bc_w, zx_w, out_w), (bc_t, zx_t, out_t), t_sem):
        move.wait()


def store_theirs(core, held, dst, sem):
    return [
        pltpu.make_async_copy(held[i].at[1 - core], dst[i], sem.at[i]) for i in range(3)
    ]


def forward(x_in, zx_m, bc_m, out_m, dt_m, smalls, number):
    dma = pltpu.SemaphoreType.DMA
    sds = jax.ShapeDtypeStruct
    vm = pltpu.VMEM
    got = pl.pallas_call(
        forward_kernel,
        out_shape=[sds(shape, kind) for _, shape, kind in KEPT * 2]
        + [sds(zx_m.shape, BF), sds(bc_m.shape, BF), sds(out_m.shape, BF)]
        + [sds((2, 16, WIDTH), F32), sds((2, 128, WIDTH), BF), sds((ROWS, WIDTH), BF)],
        in_specs=[ANY] * 4 + [VM] * 8,
        out_specs=[ANY] * 35 + [VM] * 2 + [ANY],
        scratch_shapes=[
            vm((ROWS, WIDTH), BF),
            vm((2, RIM, WIDTH), BF),
            vm((2, WIDTH, WIDTH), BF),
            vm((2, WIDTH, 256), BF),
            vm((2, INNER_DEV, WIDTH), BF),
            vm((ROWS, INNER_DEV), BF),
            vm((ROWS, ROWS), F32),
            vm((ROWS, 128), F32),
            vm((ROWS, 128), F32),
            vm((ROWS, INNER_DEV), BF),
            vm((ROWS, 128), F32),
            vm((ROWS, WIDTH), BF),
            vm((2, 16, 16, 512), BF),
            vm((2, 16, 16, 512), BF),
            vm((2, 16, 16, 384), BF),
            vm((2, 16, 16, 384), BF),
            vm((3, ROWS, 384), BF),
            vm((2, 8, 128), F32),
            vm((2, 3, 8, 128), F32),
            vm((ROWS, 384), BF),
            vm((RIM, 384), BF),
            dma((6,)),
            dma((6,)),
            dma((4,)),
            dma((5,)),
            dma((5,)),
            dma((2, 16)),
            dma((2, 16)),
            dma((2, 16)),
            dma((2, 16)),
            dma((2, 6)),
            dma((2, 6)),
            dma((2, 3)),
            dma((2, 3)),
            dma((3,)),
            dma,
            dma((2, len(KEPT))),
        ]
        + [vm(shape, kind) for _, shape, kind in KEPT * 2],
        compiler_params=comm_params(number),
        name="forward_layers",
    )(x_in, zx_m, bc_m, out_m, dt_m, *smalls)
    kept = [{name: got[16 * s + i] for i, (name, _, _) in enumerate(KEPT)} for s in range(2)]
    return kept, got[32:38]


PART = 48
EARLY, WIDE = 2 * PART, 3 * PART
SUB = WIDE + 16
GROUPS = (((0, PART), (PART, EARLY)), ((EARLY, EARLY + 32), (EARLY + 32, SUB)))
REST = 32
SLOT = ("z", "x_pre", "bc_pre", "dt_pre", "la", "la_t", "xd", "bc_act", "x_act", "y", "decay", "state", "scale", "out")
SHAPES = {name: (shape, kind) for name, shape, kind in KEPT}


def add_rows(total, more):
    return total.astype(F32) + more.astype(F32)


def backward_kernel(*refs):
    cot_ref, x_ref, part_ref = refs[:3]
    held = (refs[3:6], refs[6:9])
    small_all, dt_all = refs[9:11]
    saved = [{name: refs[11 + 16 * s + i] for i, (name, _, _) in enumerate(KEPT)} for s in range(2)]
    grads_ref, rest_ref, section_ref, leaving_ref = refs[43:47]
    rest = list(refs[47:])

    def take(count):
        got = rest[:count]
        del rest[:count]
        return got

    k = dict(zip(SLOT, take(len(SLOT))))
    normed_all, v_all, d_v, g_o_buf = take(4)
    zx_w, bc_w, out_w = take(3)
    own, spare, theirs, first, mid, second, ring = take(7)
    d_y_ref, d_z_ref, d_xd, d_y_low, wide_x, wide_y = take(6)
    scores_t, d_scores_t, d_bc, terms, direct, tail_ref, dt_ref = take(7)
    ext, d_zx, d_bd, part, sum_in, d_normed_ref, sum_own = take(7)
    chain_out, chain_in, chain_back, chain_got, state_grad = take(5)
    rim_buf, taps_ref, bc_out, bc_in, norm_ref, sums_ref, small_rows = take(7)
    rest_out, rest_cross, rest_near, rest_far, rest_low = take(5)
    k_sem, n_sem, w_sem, move_sem = take(4)
    c_sems, s_sems, rim_sems, swap_sems = take(4), take(4), take(2), take(2)
    cross_sems, one_sems, two_sems, back_sems, last_sems = take(2), take(2), take(2), take(2), take(2)
    bc_sems, rest_sems = take(2), take(2)
    row_out, row_in, final_in, final_own = take(4)
    row_sems, final_sems = take(2), take(4)
    theirs_free, first_free = take(2)

    core, me, place = lax.axis_index("section"), lax.axis_index("seq"), lax.axis_index("head")
    x, z = lax.div(me, 4), lax.rem(me, 4)
    along_z = [x * 4 + shifted(z, d, 4) for d in range(1, 4)]
    along_x = [shifted(x, d, 4) * 4 + z for d in range(1, 4)]
    ways = ((x, z, along_z, along_x), (z, x, along_x, along_z))
    other = {"section": 1 - core}
    heads = [{"head": shifted(place, d, 4)} for d in range(1, 4)]
    targets = [other] + [{"seq": shifted(me, d, 16)} for d in range(1, 16)] + heads
    targets += [{"section": 1 - core, "seq": seq} for seq in along_z + along_x]
    targets += [{"section": 1 - core, "head": shifted(place, d, 4)} for d in range(1, 4)]
    barrier = pltpu.get_barrier_semaphore()
    for target in targets:
        pl.semaphore_signal(barrier, inc=1, device_id=target, device_id_type=MESH)

    def load_kept(s):
        return [
            pltpu.make_async_copy(saved[s][name], k[name], k_sem.at[i])
            for i, name in enumerate(SLOT)
            if s == 0 or name not in ("scale", "out")
        ]

    def load_rows(s):
        source = x_ref.at[core] if s == 0 else saved[0]["following"]
        return [
            pltpu.make_async_copy(saved[s]["normed"], normed_all.at[s], n_sem.at[s, 0]),
            pltpu.make_async_copy(source, v_all.at[s], n_sem.at[s, 1]),
        ]

    weight_slots = (zx_w, bc_w, out_w)

    def load_weight(s, i):
        @pl.when(core == s)
        def _():
            pltpu.make_async_copy(held[0][i], weight_slots[i], w_sem.at[i]).start()

        @pl.when(core != s)
        def _():
            pltpu.make_async_copy(held[1][i], weight_slots[i], w_sem.at[i]).start()

    def wait_weight(i):
        pltpu.make_async_copy(held[0][i], weight_slots[i], w_sem.at[i]).wait()

    load_g_o = pltpu.make_async_copy(cot_ref.at[core], g_o_buf, n_sem.at[0, 2])
    load_g_o.start()
    load_weight(1, 2)
    for move in load_kept(1):
        move.start()
    load_weight(1, 0)
    load_weight(1, 1)
    for s in (1, 0):
        for move in load_rows(s):
            move.start()

    small_rows[...] = jnp.zeros_like(small_rows)
    def swapped(i, src, dst):
        return pltpu.make_async_remote_copy(
            src_ref=src,
            dst_ref=dst.at[core],
            send_sem=swap_sems[0].at[i],
            recv_sem=swap_sems[1].at[i],
            device_id=other,
            device_id_type=MESH,
        )

    def final(d, micro):
        return pltpu.make_async_remote_copy(
            src_ref=final_own,
            dst_ref=section_ref.at[micro, :, quarter(place)],
            send_sem=final_sems[2].at[d],
            recv_sem=final_sems[3].at[micro, d],
            device_id={"section": 1, "head": shifted(place, d + 1, 4)},
            device_id_type=MESH,
        )

    def final_stay():
        return pltpu.make_async_copy(final_own, section_ref.at[1, :, quarter(place)], move_sem.at[0])

    def cross(s, piece):
        lo, hi = GROUPS[piece][0][0], GROUPS[piece][1][1]
        return pltpu.make_async_remote_copy(
            src_ref=spare.at[:, :, lo:hi],
            dst_ref=theirs.at[:, :, lo:hi],
            send_sem=cross_sems[0].at[s, piece],
            recv_sem=cross_sems[1].at[s, piece],
            device_id=other,
            device_id_type=MESH,
        )

    def reduction(s, group):
        parts = [(n, lo, hi) + ways[n] for n, (lo, hi) in enumerate(GROUPS[group])]
        low, high = parts[0][1], parts[1][2]
        cross(s, group).wait_recv()

        @pl.loop(0, 4)
        def _(i):
            @pl.loop(0, 4)
            def _(j):
                own[s, i, j, low:high] = own[s, i, j, low:high] + theirs[i, j, low:high]

        if s == 0:
            pl.semaphore_wait(first_free.at[group], 6)
        copies = []
        for d in range(3):
            for n, lo, hi, a, b, near, far in parts:
                src = own.at[s, :, shifted(b, d + 1, 4), lo:hi]
                dst = first.at[d, :, lo:hi]
                sems = one_sems[0].at[s, group, n, d], one_sems[1].at[s, group, n, d]
                copies.append(send(src, dst, *sems, {"seq": near[d]}))
        yield
        finish(copies)

        @pl.loop(0, 4)
        def _(i):
            for n, lo, hi, a, b, near, far in parts:
                total = own[s, i, b, lo:hi].astype(F32)
                for d in range(3):
                    total = total + first[d, i, lo:hi].astype(F32)
                mid[i, lo:hi] = total.astype(BF)

        copies = []
        for d in range(3):
            for n, lo, hi, a, b, near, far in parts:
                src = mid.at[shifted(a, d + 1, 4), lo:hi]
                dst = second.at[s, d, lo:hi]
                sems = two_sems[0].at[s, group, n, d], two_sems[1].at[s, group, n, d]
                copies.append(send(src, dst, *sems, {"seq": far[d]}))
        yield
        finish(copies)
        copies = []
        for n, lo, hi, a, b, near, far in parts:
            total = mid[a, lo:hi].astype(F32)
            for d in range(3):
                total = total + second[s, d, lo:hi].astype(F32)
            ring[s, a, lo:hi] = total.astype(BF)
            for d in range(3):
                block = ring.at[s, a, lo:hi]
                sems = back_sems[0].at[s, group, n, d], back_sems[1].at[s, group, n, d]
                copies.append(send(block, block, *sems, {"seq": far[d]}))
        yield
        finish(copies)

        def last(part, d, half):
            n, lo, hi, a, b, near, far = part
            return pltpu.make_async_remote_copy(
                src_ref=ring.at[s, :, lo:hi],
                dst_ref=grads_ref.at[half, :, b, lo:hi],
                send_sem=last_sems[0].at[s, group, n, d],
                recv_sem=last_sems[1].at[s, group, n, half, d],
                device_id={"section": s, "seq": near[d] if d < 3 else me},
                device_id_type=MESH,
            )

        def stay(part):
            n, lo, hi, a, b, near, far = part
            sem = last_sems[0].at[s, group, n, 3]
            return pltpu.make_async_copy(ring.at[s, :, lo:hi], grads_ref.at[core, :, b, lo:hi], sem)

        for d in range(3):
            for part in parts:
                last(part, d, core).start()

        @pl.when(core == s)
        def _():
            for part in parts:
                stay(part).start()

        @pl.when(core != s)
        def _():
            for part in parts:
                last(part, 3, core).start()

        yield
        for part in parts:
            for d in range(3):
                last(part, d, core).wait_send()

        @pl.when(core == s)
        def _():
            for part in parts:
                stay(part).wait()
                for d in range(3):
                    last(part, d, s).wait_recv()
                for d in range(4):
                    last(part, d, 1 - s).wait_recv()

        @pl.when(core != s)
        def _():
            for part in parts:
                last(part, 3, core).wait_send()

        yield

    def reduction_rest(s):
        def move(src, dst, i, target):
            return send(src, dst, rest_sems[0].at[s, i], rest_sems[1].at[s, i], target)

        def gather(bufs, first_sem, peers):
            return [move(rest_low.at[s], bufs.at[s, d], first_sem + d, {"seq": peers[d]}) for d in range(3)]

        copy = move(rest_out.at[1 - core], rest_cross.at[s], 0, other)
        yield
        copy.wait()
        total = add_rows(rest_out[core], rest_cross[s])
        rest_low[s] = total.astype(BF)
        copies = gather(rest_near, 1, along_z)
        yield
        finish(copies)
        for d in range(3):
            total = total + rest_near[s, d].astype(F32)
        rest_low[s] = total.astype(BF)
        copies = gather(rest_far, 4, along_x)
        yield
        finish(copies)
        for d in range(3):
            total = total + rest_far[s, d].astype(F32)
        rest_low[s] = total.astype(BF)

        def deliver():
            return pltpu.make_async_remote_copy(
                src_ref=rest_low.at[s],
                dst_ref=rest_ref.at[core],
                send_sem=rest_sems[0].at[s, 7],
                recv_sem=rest_sems[1].at[s, 7],
                device_id=other,
                device_id_type=MESH,
            )

        @pl.when(core != s)
        def _():
            deliver().start()

        @pl.when(core == s)
        def _():
            rest_ref[core] = rest_low[s]

        yield

        @pl.when(core != s)
        def _():
            deliver().wait_send()

        @pl.when(core == s)
        def _():
            deliver().wait_recv()

        yield

    member_rows = lax.broadcasted_iota(jnp.int32, (INNER_DEV, 128), 0)
    member_lanes = lax.broadcasted_iota(jnp.int32, (INNER_DEV, 128), 1) * HEAD_DIM
    inside = (member_rows >= member_lanes) & (member_rows < member_lanes + HEAD_DIM)
    member = jnp.where(inside, 1.0, 0.0).astype(BF)

    def sums_of(value):
        high, low = two_part(value)
        return dot(high, member) + dot(low, member)

    half_rows = [
        [pl.ds(pl.multiple_of(h * INNER_DEV + 384 * j, 384), 384) for j in range(2)] for h in (core, 1 - core)
    ]
    half_cols = [pl.ds(pl.multiple_of(h * INNER_DEV, INNER_DEV), INNER_DEV) for h in (core, 1 - core)]
    early, late, loose = None, None, None
    old_early, old_late = None, None
    load_g_o.wait()
    for s in (1, 0):
        small = small_all.at[s]
        normed, v_ref = normed_all.at[s], v_all.at[s]
        g_o_ref = g_o_buf if s else d_v.at[1]
        y_ref, z_ref, la_ref, la_t_ref = k["y"], k["z"], k["la"], k["la_t"]
        xd_ref, bc_act, x_act = k["xd"], k["bc_act"], k["x_act"]
        x_pre, bc_pre = k["x_pre"], k["bc_pre"]
        stages = (own.at[s], spare)

        sums_ref[...] = jnp.zeros_like(sums_ref)
        wait_weight(2)

        @pl.loop(0, 3)
        def _(j):
            d_xd[:, tile_at(j)] = dot_last(g_o_ref[...], out_w[tile_at(j), :])

        if s:
            load_weight(0, 2)
        finish(load_kept(s))
        if s:
            finish(load_rows(1))

            @pl.loop(0, BLOCKS)
            def _(i):
                at = rows_at(i)
                gain = small[S_GATE : S_GATE + 1, :INNER_DEV]
                ssd = y_ref[at] + small[S_SKIP : S_SKIP + 1, :INNER_DEV] * x_act[at]
                gated = ssd * silu(z_ref[at])
                square = jnp.sum(gated * gated, axis=-1, keepdims=True)
                mean = jnp.sum(gated * gain * d_xd[at], axis=-1, keepdims=True)
                lane = lax.broadcasted_iota(jnp.int32, (STEP, 128), 1)
                tail_ref[at] = jnp.where(lane == 0, square, mean)

            row_out[...] = tail_ref[...].T[0:8]
            pl.semaphore_wait(barrier, len(targets))
            copies = [
                send(row_out, row_in.at[d], row_sems[0].at[d], row_sems[1].at[d], heads[d]) for d in range(3)
            ]
            final_copies = []
            for d in range(3):
                src = part_ref.at[:, quarter(shifted(place, d + 1, 4))]
                sems = final_sems[0].at[d], final_sems[1].at[d]
                final_copies.append(send(src, final_in.at[d], *sems, heads[d]))
            load_final = pltpu.make_async_copy(part_ref.at[:, quarter(place)], final_own, move_sem.at[0])
            load_final.start()
            finish(copies)
            total = row_out[...]
            for d in range(3):
                total = total + row_in[d]
            total = jnp.concatenate([total] * 16, axis=0).T
            scale = lax.rsqrt(total[:, 0:1] * (1.0 / INNER) + EPS)
            mean = total[:, 1:2] * scale * scale * scale * (1.0 / INNER)
            lane = lax.broadcasted_iota(jnp.int32, (ROWS, 128), 1)
            k["scale"][...] = jnp.where(lane == 0, scale, mean)

        @pl.loop(0, BLOCKS)
        def _(i):
            at = rows_at(i)
            gain = small[S_GATE : S_GATE + 1, :INNER_DEV]
            scale = k["scale"][at][:, 0:1]
            act, gate, dm = x_act[at], z_ref[at], d_xd[at]
            ssd = y_ref[at] + small[S_SKIP : S_SKIP + 1, :INNER_DEV] * act
            sigma = jax.nn.sigmoid(gate)
            gate_silu = gate * sigma
            gated = ssd * gate_silu
            scaled = gated * scale
            if s:
                mean = k["scale"][at][:, 1:2]
            else:
                mean = jnp.sum(g_o_ref[at].astype(F32) * k["out"][at].astype(F32), axis=-1, keepdims=True)
                mean = mean * scale * scale * (1.0 / INNER)
            wide_x[at] = (scaled * gain).astype(BF)
            d_gated = scale * gain * dm - gated * mean
            d_y = d_gated * gate_silu
            d_y_ref[at] = d_y
            d_y_low[at] = d_y.astype(BF)
            d_z_ref[at] = (d_gated * ssd * sigma * (1.0 + gate * (1.0 - sigma))).astype(BF)
            wide_y[at] = (spread(jnp.exp(la_ref[at])) * d_y).astype(BF)
            sums_ref[0:1] += jnp.sum(scaled * dm, axis=0, keepdims=True)
            sums_ref[1:2] += jnp.sum(d_y * act, axis=0, keepdims=True)

        b_rows, c_rows = bc_act[:, :STATE], bc_act[:, STATE:]
        chain_load(dot_first(c_rows, wide_y[...]), k["decay"], chain_out)
        copies = spread_send(chain_out, chain_in, me, c_sems[0].at[s], c_sems[1].at[s])
        if s:

            @pl.when(core == 1)
            def _():
                swapped(0, saved[0]["following"], section_ref).start()

        if s == 0:
            for piece in range(2):
                cross(1, piece).wait_send()
        for stage, cols, rows in zip(stages, half_cols, half_rows):
            for j in range(2):
                got = dot_first(wide_x[:, 384 * j : 384 * j + 384], g_o_ref[:, cols]).astype(BF)
                for i in range(8):
                    sub = 8 * j + i
                    stage[sub // 4, sub % 4, 0:PART] = got[PART * i : PART * i + PART]
            for j in range(2):
                got = dot_first(normed[RIM:, rows[j]], d_z_ref[...]).astype(BF)
                for i in range(8):
                    sub = 8 * j + i
                    stage[sub // 4, sub % 4, PART:EARLY] = got[PART * i : PART * i + PART]
        if s == 0:
            pl.semaphore_wait(theirs_free, 1)
        cross(s, 0).start()
        if s == 0:
            next(late)
            for seq in along_z + along_x:
                pl.semaphore_signal(first_free.at[1], inc=1, device_id={"seq": seq}, device_id_type=MESH)
            next(loose)

        la = la_ref[...]
        tail_ref[...] = jnp.exp(la[ROWS - 1 : ROWS] - la)
        dt_in = k["dt_pre"][...] + small[S_BIAS : S_BIAS + 1, :128]
        dt_ref[...] = softplus(dt_in)
        scores_t[...] = dot_last(b_rows, c_rows)

        def heads_of(half):
            base = half * 128
            rows = slice(base, base + 128)
            t = lax.broadcasted_iota(jnp.int32, (128, ROWS - base), 1)
            later = t >= lax.broadcasted_iota(jnp.int32, (128, ROWS - base), 0)
            total = jnp.zeros((128, ROWS - base), F32)
            for pair in range(HEADS_DEV // 2):
                parts = []
                for h in (2 * pair, 2 * pair + 1):
                    cols = slice(h * HEAD_DIM, (h + 1) * HEAD_DIM)
                    gap = la_t_ref[h : h + 1, base:] - la_ref[rows, h : h + 1]
                    decay = jnp.exp(jnp.where(later, gap, -1e30))
                    total = total + decay * dot_last(xd_ref[rows, cols], d_y_low[base:, cols])
                    mixing = (scores_t[rows, base:] * decay).astype(BF)
                    parts.append(dot(mixing, d_y_low[base:, cols]))
                d_xd[rows, pair * 128 : pair * 128 + 128] = jnp.concatenate(parts, axis=1)
            if half:
                d_scores_t[rows, 0:128] = jnp.zeros((128, 128), BF)
            d_scores_t[rows, base:] = total.astype(BF)

        heads_of(0)
        finish(copies)
        chain_scan(False, chain_in, chain_back)
        copies = spread_send(chain_back, chain_got, me, c_sems[2].at[s], c_sems[3].at[s])
        heads_of(1)
        finish(copies)
        old_early, early = early, reduction(s, 0)
        next(early)
        if s == 0:
            next(late)
            next(loose)
        if s:
            load_final.wait()
            finish(final_copies)

            @pl.loop(0, BLOCKS)
            def _(i):
                at = rows_at(i)
                total = final_own[at].astype(F32)
                for d in range(3):
                    total = total + final_in[d, at].astype(F32)
                total = (total * k["scale"][at][:, 0:1]).astype(BF).astype(F32)
                final_own[at] = (v_ref[at, quarter(place)].astype(F32) + total).astype(BF)

            for d in range(3):
                final(d, core).start()

            @pl.when(core == 1)
            def _():
                final_stay().start()

            @pl.when(core == 0)
            def _():
                final(3, core).start()
                pltpu.make_async_copy(v_all.at[1], section_ref.at[0], move_sem.at[0]).start()

        chain_unload(chain_got, state_grad)
        norm_ref[...] = jnp.zeros_like(norm_ref)
        taps_ref[...] = jnp.zeros_like(taps_ref)

        @pl.loop(0, BLOCKS)
        def _(i):
            at = rows_at(i)
            tail = spread(tail_ref[at])
            xd = xd_ref[at].astype(F32)
            wide_x[at] = (tail * xd).astype(BF)
            state_part = tail * dot(bc_act[at, :STATE], state_grad[...])
            got = d_xd[at] + state_part
            d_xd[at] = got
            norm_ref[1:2, :INNER_DEV] += jnp.sum(xd * state_part, axis=0, keepdims=True)
            terms[at] = sums_of(d_y_low[at].astype(F32) * y_ref[at] - xd * got)
            direct[at] = sums_of(x_act[at] * got)

        d_bc[:, :STATE] = dot(d_scores_t[...], c_rows) + dot_last(wide_x[...], state_grad[...])
        d_bc[:, STATE:] = dot_first(d_scores_t[...], b_rows) + dot_last(wide_y[...], k["state"][...])
        end_wide = spread(jnp.exp(la[ROWS - 8 : ROWS]))[7:8]
        both = state_grad[...].astype(F32) * k["state"][...].astype(F32)
        tail_sum = norm_ref[1:2, :INNER_DEV] + end_wide * jnp.sum(both, axis=0, keepdims=True)
        tail_sum = sums_of(jnp.broadcast_to(tail_sum, (16, INNER_DEV)))[0:1]

        @pl.loop(0, BLOCKS)
        def _(i):
            at = rows_at(i)
            taps = small[S_CONV : S_CONV + 4, INNER_DEV : INNER_DEV + 256]
            d_bcc = d_bc[at] * silu_slope(conv_rows(bc_pre[rows_at(i, RIM)], taps))
            d_bc[at] = d_bcc
            bc_out[at] = d_bcc.astype(BF)

        copies = [
            send(bc_out, bc_in.at[d], bc_sems[0].at[s, d], bc_sems[1].at[s, d], heads[d]) for d in range(3)
        ]
        d_log = running(terms[...], True) + tail_sum
        rate = small[S_RATE : S_RATE + 1, :128]
        d_dt = direct[...] + rate * d_log
        d_dt_pre = d_dt * jax.nn.sigmoid(dt_in)
        d_bd[:, 256:] = d_dt_pre.astype(BF)
        sums_ref[2:3, :128] = jnp.sum(dt_ref[...] * d_log, axis=0, keepdims=True) * rate
        sums_ref[3:4, :128] = jnp.sum(d_dt_pre, axis=0, keepdims=True)

        @pl.loop(0, BLOCKS)
        def _(i):
            at = rows_at(i)
            taps = small[S_CONV : S_CONV + 4]
            pre = x_pre[rows_at(i, RIM)]
            d_x = spread(dt_ref[at]) * d_xd[at] + small[S_SKIP : S_SKIP + 1, :INNER_DEV] * d_y_ref[at]
            d_xc = d_x * silu_slope(conv_rows(pre, taps[:, :INNER_DEV]))
            ext[at, :INNER_DEV] = d_xc
            for t in range(4):
                moved = pre[RIM - 3 + t : RIM - 3 + t + STEP]
                taps_ref[t : t + 1, :INNER_DEV] += jnp.sum(moved * d_xc, axis=0, keepdims=True)

        finish(copies)

        @pl.loop(0, BLOCKS)
        def _(i):
            at = rows_at(i)
            d_bcc = d_bc[at]
            for d in range(3):
                d_bcc = d_bcc + bc_in[d, at].astype(F32)
            ext[at, INNER_DEV:] = d_bcc
            pre = bc_pre[rows_at(i, RIM)]
            for t in range(4):
                moved = pre[RIM - 3 + t : RIM - 3 + t + STEP]
                taps_ref[t : t + 1, INNER_DEV:] += jnp.sum(moved * d_bcc, axis=0, keepdims=True)

        rim = send(
            ext.at[0:8], rim_buf, rim_sems[0].at[s], rim_sems[1].at[s], {"seq": shifted(me, -1, 16)}
        )
        if s:
            for move in load_kept(0):
                move.start()

        next(early)
        if s == 0:
            next(loose)
            next(late)
        else:
            for seq in along_z + along_x:
                pl.semaphore_signal(first_free.at[0], inc=1, device_id={"seq": seq}, device_id_type=MESH)
        rim.wait()

        @pl.when(me == 15)
        def _():
            rim_buf[...] = jnp.zeros_like(rim_buf)

        ext[ROWS : ROWS + 8] = rim_buf[...]

        @pl.loop(0, BLOCKS)
        def _(i):
            at = rows_at(i)
            taps = small[S_CONV : S_CONV + 4]
            block = ext[rows_at(i, 8)]
            d_pre = taps[0:1, : INNER_DEV + 256] * block[3 : 3 + STEP]
            for t in range(1, 4):
                d_pre = d_pre + taps[t : t + 1, : INNER_DEV + 256] * block[3 - t : 3 - t + STEP]
            d_zx[at, :INNER_DEV] = d_z_ref[at]
            d_zx[at, INNER_DEV:] = d_pre[:, :INNER_DEV].astype(BF)
            d_bd[at, :256] = d_pre[:, INNER_DEV:].astype(BF)

        wait_weight(0)
        wait_weight(1)

        @pl.loop(0, 6)
        def _(j):
            got = dot_last(d_zx[...], zx_w[tile_at(j), :])
            got = got + dot_last(d_bd[:, :256], bc_w[tile_at(j), :]) * 0.25
            got = got + dot(d_bd[:, 256:], dt_all[s, :, tile_at(j)])
            part[:, tile_at(j)] = got.astype(BF)

        if s:
            load_weight(0, 0)
            load_weight(0, 1)
        copies = []
        for d in range(1, 4):
            src = part.at[:, quarter(shifted(place, d, 4))]
            copies.append(send(src, sum_in.at[d - 1], s_sems[0].at[s, d], s_sems[1].at[s, d], heads[d - 1]))
        for stage, rows in zip(stages, half_rows):
            for j in range(2):
                got = dot_first(normed[RIM:, rows[j]], d_zx[:, INNER_DEV:]).astype(BF)
                for i in range(8):
                    sub = 8 * j + i
                    stage[sub // 4, sub % 4, EARLY:WIDE] = got[PART * i : PART * i + PART]

        for n, (stage, cols) in enumerate(zip(stages, half_cols)):
            got = dot_first(d_bd[...], normed[RIM:, cols])
            for i in range(16):
                stage[i // 4, i % 4, WIDE:SUB] = got[16 * i : 16 * i + 16].astype(BF)
            rest_out[core if n == 0 else 1 - core, 0:16] = got[256:272].astype(BF)
        cross(s, 1).start()
        next(early)
        finish(copies)

        @pl.loop(0, BLOCKS)
        def _(i):
            at = rows_at(i)
            total = part[at, quarter(place)].astype(F32)
            for d in range(3):
                total = total + sum_in[d, at].astype(F32)
            total = total.astype(BF)
            sum_own[at] = total
            d_normed_ref[at, quarter(place)] = total

        copies = []
        for d in range(1, 4):
            dst = d_normed_ref.at[:, quarter(place)]
            copies.append(send(sum_own, dst, s_sems[2].at[s, d], s_sems[3].at[s, d], heads[d - 1]))
        old_late, late = late, reduction(s, 1)
        next(early)
        if s == 0:
            next(late)
        finish(copies)
        norm_ref[...] = jnp.zeros_like(norm_ref)

        @pl.loop(0, BLOCKS)
        def _(i):
            at = rows_at(i)
            v = v_ref[at].astype(F32)
            scale = lax.rsqrt(jnp.mean(v * v, axis=-1, keepdims=True) + EPS)
            d_normed = d_normed_ref[at].astype(F32)
            scaled = v * scale
            norm_ref[0:1] += jnp.sum(scaled * d_normed, axis=0, keepdims=True)
            weighted = d_normed * small[S_NORM : S_NORM + 1]
            mean = jnp.mean(v * weighted, axis=-1, keepdims=True) * scale * scale
            d_v[s, at] = (scale * weighted - scaled * mean + g_o_ref[at].astype(F32)).astype(BF)

        for h in range(2):
            small_rows[h, 0:1] = norm_ref[0:1, h * INNER_DEV : (h + 1) * INNER_DEV]
            small_rows[h, 1:5] = taps_ref[0:4, :INNER_DEV]
            small_rows[h, 5:9] = sums_ref[0:4]
            small_rows[h, 9:13, 0:256] = taps_ref[0:4, INNER_DEV:]
            rest_out[h, 16:] = small_rows[h].astype(BF)
        old_loose, loose = loose, reduction_rest(s)
        next(loose)
        if s:
            next(late)
            pl.semaphore_signal(theirs_free, inc=1, device_id=other, device_id_type=MESH)

        @pl.when(core == 1 - s)
        def _():
            swapped(1, d_v.at[s], leaving_ref).start()

        @pl.when(core == s)
        def _():
            pltpu.make_async_copy(d_v.at[s], leaving_ref.at[s], move_sem.at[1]).start()

        if s:
            finish(load_rows(0))

    for turn in (loose, late, loose, late, loose, late, loose, early, late, old_early, old_late, old_loose):
        next(turn)
    for piece in range(2):
        cross(0, piece).wait_send()
    for d in range(3):
        final(d, core).wait_send()

    @pl.when(core == 0)
    def _():
        swapped(0, d_v.at[0], section_ref).wait_recv()
        pltpu.make_async_copy(v_all.at[1], section_ref.at[0], move_sem.at[0]).wait()
        final(3, core).wait_send()

    @pl.when(core == 1)
    def _():
        swapped(0, saved[0]["following"], section_ref).wait_send()
        final_stay().wait()
        for d in range(3):
            final(d, 1).wait_recv()
        for d in range(4):
            final(d, 0).wait_recv()

    swapped(1, d_v.at[0], leaving_ref).wait()
    pltpu.make_async_copy(d_v.at[0], leaving_ref.at[0], move_sem.at[1]).wait()


def backward(cotangent, x_in, part, held, smalls, dt_all, kept, number):
    dma = pltpu.SemaphoreType.DMA
    regular = pltpu.SemaphoreType.REGULAR
    sds = jax.ShapeDtypeStruct
    vm = pltpu.VMEM
    halves = (4, 4, SUB, INNER_DEV)
    rows_low = vm((ROWS, INNER_DEV), BF)
    rows_wide = vm((ROWS, INNER_DEV), F32)
    steps = vm((ROWS, 128), F32)
    scratch = [vm(*SHAPES[name]) for name in SLOT]
    scratch += [
        vm((2, ROWS + RIM, WIDTH), BF),
        vm((2, ROWS, WIDTH), BF),
        vm((2, ROWS, WIDTH), BF),
        vm((ROWS, WIDTH), BF),
        vm((WIDTH, WIDTH), BF),
        vm((WIDTH, 256), BF),
        vm((INNER_DEV, WIDTH), BF),
        vm((2,) + halves, BF),
        vm(halves, BF),
        vm(halves, BF),
        vm((3, 4, SUB, INNER_DEV), BF),
        vm((4, SUB, INNER_DEV), BF),
        vm((2, 3, SUB, INNER_DEV), BF),
        vm((2, 4, SUB, INNER_DEV), BF),
        rows_wide, rows_low, rows_wide, rows_low, rows_low, rows_low,
        vm((ROWS, ROWS), F32),
        vm((ROWS, ROWS), BF),
        vm((ROWS, 256), F32),
        steps, steps, steps, steps,
        vm((ROWS + 8, INNER_DEV + 256), F32),
        vm((ROWS, WIDTH), BF),
        vm((ROWS, 384), BF),
        vm((ROWS, WIDTH), BF),
        vm((3, ROWS, 384), BF),
        vm((ROWS, WIDTH), BF),
        vm((ROWS, 384), BF),
        vm((16, 16, 512), BF),
        vm((16, 16, 512), BF),
        vm((16, 16, 384), BF),
        vm((16, 16, 384), BF),
        vm((STATE, INNER_DEV), BF),
        vm((8, INNER_DEV + 256), F32),
        vm((8, INNER_DEV + 256), F32),
        vm((ROWS, 256), BF),
        vm((3, ROWS, 256), BF),
        vm((8, WIDTH), F32),
        vm((8, INNER_DEV), F32),
        vm((2, 16, INNER_DEV), F32),
        vm((2, REST, INNER_DEV), BF),
        vm((2, REST, INNER_DEV), BF),
        vm((2, 3, REST, INNER_DEV), BF),
        vm((2, 3, REST, INNER_DEV), BF),
        vm((2, REST, INNER_DEV), BF),
        dma((len(SLOT),)),
        dma((2, 3)),
        dma((3,)),
        dma((2,)),
    ]
    scratch += [dma((2, 16))] * 4 + [dma((2, 8))] * 2 + [dma((2, 4))] * 2
    scratch += [dma((2,))] * 4 + [dma((2, 2))] * 2
    scratch += [dma((2, 2, 2, 4))] * 7 + [dma((2, 2, 2, 2, 4))]
    scratch += [dma((2, 3))] * 2 + [dma((2, 8))] * 2
    scratch += [vm((8, ROWS), F32), vm((3, 8, ROWS), F32), vm((3, ROWS, 384), BF), vm((ROWS, 384), BF)]
    scratch += [dma((3,))] * 4 + [dma((4,)), dma((2, 4)), regular, regular((2,))]
    flat = [kept[s][name] for s in range(2) for name, _, _ in KEPT]
    return pl.pallas_call(
        backward_kernel,
        out_shape=[
            sds((2,) + halves, BF),
            sds((2, REST, INNER_DEV), BF),
            sds((2, ROWS, WIDTH), BF),
            sds((2, ROWS, WIDTH), BF),
        ],
        in_specs=[ANY] * 9 + [VM] * 2 + [ANY] * 32,
        out_specs=[ANY, VM, ANY, ANY],
        scratch_shapes=scratch,
        compiler_params=comm_params(number),
        name="backward_layers",
    )(cotangent, x_in, part, *held, smalls, dt_all, *flat)


def widen_kernel(
    a_ref, rest_ref, zx_ref, out_ref, bc_ref, dt_ref, norm_ref, bias_ref, rate_ref, skip_ref, conv_ref, conv_bc_ref,
    gate_ref, bc_all, wide, sem,
):
    step = pl.program_id(0)
    slot = lax.rem(step, 2)

    def moves(step, slot):
        return [
            pltpu.make_async_copy(
                wide.at[slot, h, kind],
                zx_ref.at[pl.ds(h * INNER_DEV + step * 2 * PART, 2 * PART), kind, :],
                sem.at[slot, h, kind],
            )
            for h in range(2)
            for kind in range(2)
        ]

    @pl.when(step >= 2)
    def _():
        finish(moves(step - 2, slot))

    for h in range(2):
        cols = slice(h * INNER_DEV, (h + 1) * INNER_DEV)
        for n in range(2):
            rows = slice(n * PART, n * PART + PART)
            wide[slot, h, 0, rows] = a_ref[h, n, PART:EARLY].astype(F32)
            wide[slot, h, 1, rows] = a_ref[h, n, EARLY:WIDE].astype(F32)
            out_ref[rows, cols] = a_ref[h, n, 0:PART].astype(F32)
            at = pl.ds(pl.multiple_of(step * 32 + n * 16, 16), 16)
            bc_all[at, cols] = a_ref[h, n, WIDE:SUB].astype(F32)
    for move in moves(step, slot):
        move.start()

    @pl.when(step == 0)
    def _():
        rows = rest_ref[0].astype(F32)
        more = rest_ref[1].astype(F32)
        for h in range(HEADS_DEV):
            dt_ref[h, :, :INNER_DEV] = rows[h : h + 1]
            dt_ref[h, :, INNER_DEV:] = more[h : h + 1]
        rows = rows[16:]
        norm_ref[:, :INNER_DEV] = rows[0:1]
        norm_ref[:, INNER_DEV:] = more[16:17]
        conv_ref[...] = rows[1:5]
        gate_ref[...] = rows[5:6]
        heads = jnp.concatenate(
            [
                jnp.sum(rows[0:8, h * HEAD_DIM : (h + 1) * HEAD_DIM], axis=1, keepdims=True)
                for h in range(HEADS_DEV)
            ],
            axis=1,
        )
        skip_ref[...] = heads[6:7]
        rate_ref[...] = rows[7:8, 0:HEADS_DEV]
        bias_ref[...] = rows[8:9, 0:HEADS_DEV]
        conv_bc_ref[...] = rows[9:13, 0:256]

    @pl.when(step == 7)
    def _():
        bc_ref[...] = bc_all[...].T
        finish(moves(step - 1, 1 - slot))
        finish(moves(step, slot))


def widen(total, rest):
    total = total.reshape(2, 16, SUB, INNER_DEV)
    fixed = ((WIDTH, 256), (HEADS_DEV, 1, WIDTH), (1, WIDTH)) + ((1, HEADS_DEV),) * 3
    fixed += ((4, INNER_DEV), (4, 256), (1, INNER_DEV))
    shapes = ((WIDTH, 2, INNER_DEV), (INNER_DEV, WIDTH)) + fixed
    return pl.pallas_call(
        widen_kernel,
        grid=(8,),
        out_shape=[jax.ShapeDtypeStruct(shape, F32) for shape in shapes],
        in_specs=[
            pl.BlockSpec((2, 2, SUB, INNER_DEV), lambda i: (0, i, 0, 0)),
            pl.BlockSpec((2, REST, INNER_DEV), lambda i: (0, 0, 0)),
        ],
        out_specs=[
            ANY,
            pl.BlockSpec((2 * PART, WIDTH), lambda i: (i, 0)),
        ]
        + [pl.BlockSpec(shape, lambda i, n=len(shape): (0,) * n) for shape in fixed],
        scratch_shapes=[
            pltpu.VMEM((256, WIDTH), F32),
            pltpu.VMEM((2, 2, 2, 2 * PART, INNER_DEV), F32),
            pltpu.SemaphoreType.DMA((2, 2, 2)),
        ],
        compiler_params=pltpu.CompilerParams(vmem_limit_bytes=VMEM_CAP),
        name="widen",
    )(total, rest)


def on_device(
    x_in,
    norm_gain,
    w_zx,
    w_bc,
    w_dt,
    dt_bias,
    a_log,
    d_skip,
    conv_x,
    conv_bc,
    gate_gain,
    w_out,
    cotangent,
):
    zx_m = w_zx[0].reshape(WIDTH, WIDTH)
    bc_m, out_m, dt_m = w_bc[0], w_out[0], w_dt[0].T
    small_args = (norm_gain, gate_gain, conv_x[0], conv_bc[0], dt_bias, a_log, d_skip)
    kept, (zx_t, bc_t, out_t, smalls, dt_all, part) = forward(x_in, zx_m, bc_m, out_m, dt_m, small_args, 0)
    held = (zx_m, bc_m, out_m, zx_t, bc_t, out_t)
    total, rest, section_out, grads_in = backward(
        cotangent, x_in, part, held, smalls, dt_all, kept, 1
    )
    g_zx, g_out, g_bc, g_dt, g_norm, g_bias, g_rate, g_skip, g_conv_x, g_conv_bc, g_gate = widen(total, rest)
    return (
        section_out[None],
        grads_in[None],
        g_norm,
        g_zx[None],
        g_bc[None],
        g_dt.transpose(1, 2, 0),
        g_bias,
        g_rate,
        g_skip,
        g_conv_x[None],
        g_conv_bc[None],
        g_gate,
        g_out[None],
    )


def solution(mesh):
    in_specs = (
        P(None, "seq", None),
        P("section", None),
        P("section", None, None, "head"),
        P("section", None, None),
        P("section", None, "head"),
        P("section", "head"),
        P("section", "head"),
        P("section", "head"),
        P("section", None, "head"),
        P("section", None, None),
        P("section", "head"),
        P("section", "head", None),
        P(None, "seq", None),
    )
    out_specs = (
        P("section", None, "seq", None),
        P("section", None, "seq", None),
        P("section", None),
        P("section", None, None, "head"),
        P("section", None, None),
        P("section", None, "head"),
        P("section", "head"),
        P("section", "head"),
        P("section", "head"),
        P("section", None, "head"),
        P("section", None, None),
        P("section", "head"),
        P("section", "head", None),
    )
    return jax.shard_map(
        on_device, mesh=mesh, in_specs=in_specs, out_specs=out_specs, check_vma=False
    )
```
